128 devices in a mesh: dp: 2 (over x_lo), context: 16 (over z, y), tensor: 4 (over x_hi, core).
Axes of the slice: x: 4 (x_hi: 2, x_lo: 2; x = x_hi * 2 + x_lo), y: 4, z: 4, core: 2. Of those that a mesh axis runs over, the one named last changes fastest.
Arguments:
- latents: bfloat16 [4, 1024, 1024], P('dp', 'context'), may hold values from -6 to 6
- cond: bfloat16 [4, 1024], P('dp'), may hold values from -6 to 6
- ada_weight: bfloat16 [1, 1024, 6144], P(None, 'tensor', ('dp', 'context')), may hold values from -0.1875 to 0.1875
- ada_bias: bfloat16 [1, 6144], replicated, may hold values from -3 to 3
- query_key_value_weight: bfloat16 [1, 1024, 3, 1024], P(None, ('dp', 'context'), None, 'tensor'), may hold values from -0.1875 to 0.1875
- qv_bias: bfloat16 [1, 2, 1024], P(None, None, 'tensor'), may hold values from -3 to 3
- attention_output_weight: bfloat16 [1, 1024, 1024], P(None, 'tensor', ('dp', 'context')), may hold values from -3 to 3
- attention_output_bias: bfloat16 [1, 1024], replicated, may hold values from -3 to 3
- first_dense_weight: bfloat16 [1, 1024, 4096], P(None, ('dp', 'context'), 'tensor'), may hold values from -0.1875 to 0.1875
- first_dense_bias: bfloat16 [1, 4096], P(None, 'tensor'), may hold values from -3 to 3
- second_dense_weight: bfloat16 [1, 4096, 1024], P(None, 'tensor', ('dp', 'context')), may hold values from -0.09375 to 0.09375
- second_dense_bias: bfloat16 [1, 1024], replicated, may hold values from -3 to 3
- cotangent: bfloat16 [4, 1024, 1024], P('dp', 'context'), may hold values from -6 to 6
Outputs:
- block_out: bfloat16 [4, 1024, 1024], P('dp', 'context')
- latents_grad: float32 [4, 1024, 1024], P('dp', 'context')
- cond_grad: float32 [4, 1024], P('dp', 'tensor')
- ada_weight_grad: float32 [1, 1024, 6144], P(None, 'tensor', ('dp', 'context'))
- ada_bias_grad: float32 [1, 6144], replicated
- qkv_weight_grad: float32 [1, 1024, 3, 1024], P(None, ('dp', 'context'), None, 'tensor')
- qv_bias_grad: float32 [1, 2, 1024], P(None, None, 'tensor')
- out_weight_grad: float32 [1, 1024, 1024], P(None, 'tensor', ('dp', 'context'))
- out_bias_grad: float32 [1, 1024], replicated
- fc1_weight_grad: float32 [1, 1024, 4096], P(None, ('dp', 'context'), 'tensor')
- fc1_bias_grad: float32 [1, 4096], P(None, 'tensor')
- fc2_weight_grad: float32 [1, 4096, 1024], P(None, 'tensor', ('dp', 'context'))
- fc2_bias_grad: float32 [1, 1024], replicated
The draws below stay inside these ranges and needn't reach their ends.
All inputs are finite; a program needn't handle non-finite values.
Results may differ from the reference program's by a relative error of at most 0.009.
The reference program's roundings to bfloat16 on the way count: a program that leaves them out, or rounds other values in their place, can miss the bound.
Values may be sent and summed in bfloat16 or wider, within the bound.
A program may use at most 128 MiB of HBM per device.

```python
import math
import jax
import jax.numpy as jnp
from jax import lax

HEADS = 16
HEAD_DIM = 64
FF = 4096
LAYERS = 1
SEQ_LEN = 1024
D = 1024
SEQS = 4


def shard_levels(stream_key, shape, cuts, low, largest):
    def one(axis_at, blocks):
        draws = jax.random.uniform(jax.random.fold_in(jax.random.fold_in(stream_key, 6), axis_at), (blocks,), jnp.float32, low / len(cuts), largest / len(cuts))
        return jnp.repeat(jnp.exp(draws), shape[axis_at] // blocks).reshape((-1,) + (1,) * (len(shape) - axis_at - 1))

    gain = one(*cuts[0])
    for cut in cuts[1:]:
        gain = gain * one(*cut)
    return gain


def centred(key, shape, scale, reach, split=(), held_as=jnp.bfloat16):
    drawn = jax.random.normal(key, shape, jnp.float32) * scale
    if len(split) > 0:
        drawn = shard_levels(key, shape, split, -0.22, 0.18) * drawn
    return jnp.clip(drawn, min=-reach, max=reach).astype(held_as)


def setup_inputs(seed: int = 0) -> dict:
    seeds = jax.random.split(jax.random.key(seed), 14)
    return {
        "latents": centred(seeds[0], (SEQS, SEQ_LEN, D), 1.0, 6.0, ((0, 2), (1, 16))),
        "cond": centred(seeds[1], (SEQS, D), 1.0, 6.0, ((0, 2),)),
        "ada_weight": centred(seeds[2], (LAYERS, D, 6 * D), D ** -0.5, 0.1875, ((1, 4), (2, 32))),
        "ada_bias": centred(seeds[3], (LAYERS, 6 * D), 0.5, 3.0),
        "query_key_value_weight": centred(seeds[4], (LAYERS, D, 3, D), D ** -0.5, 0.1875, ((1, 32), (3, 4))),
        "qv_bias": centred(seeds[5], (LAYERS, 2, D), 0.5, 3.0, ((2, 4),)),
        "attention_output_weight": centred(seeds[6], (LAYERS, D, D), 4 ** -0.5, 3.0, ((1, 4), (2, 32))),
        "attention_output_bias": centred(seeds[7], (LAYERS, D), 0.5, 3.0),
        "first_dense_weight": centred(seeds[8], (LAYERS, D, FF), D ** -0.5, 0.1875, ((1, 32), (2, 4))),
        "first_dense_bias": centred(seeds[9], (LAYERS, FF), 0.5, 3.0, ((1, 4),)),
        "second_dense_weight": centred(seeds[10], (LAYERS, FF, D), FF ** -0.5, 0.09375, ((1, 4), (2, 32))),
        "second_dense_bias": centred(seeds[11], (LAYERS, D), 0.5, 3.0),
        "cotangent": centred(seeds[12], (SEQS, SEQ_LEN, D), 1.0, 6.0, ((0, 2), (1, 16))),
    }


@jax.custom_vjp
def low(v):
    return lax.optimization_barrier(v.astype(jnp.bfloat16)).astype(jnp.float32)

@jax.custom_vjp
def reduced_backward(v):
    return v

def low_keep(v):
    return (low(v), None)

def low_pass(kept, grad):
    return (grad,)

def back_keep(v):
    return (v, None)

def back_low(kept, grad):
    return (low(grad),)
low.defvjp(low_keep, low_pass)
reduced_backward.defvjp(back_keep, back_low)

def round_both(values):
    return reduced_backward(low(values))

def exact_precision(form, left, right):
    return jnp.einsum(form, left, right, precision=lax.Precision.HIGHEST)

def normalize(values):
    center = values - lax.optimization_barrier(jnp.mean(values, axis=-1, keepdims=True))
    return center * lax.rsqrt(lax.optimization_barrier(jnp.mean(center * center, axis=-1, keepdims=True)) + 1e-06)

def attend(block):
    query, keys, values = block
    length = query.shape[0]
    query_heads = query.reshape(length, HEADS, HEAD_DIM)
    key_heads = keys.reshape(length, HEADS, HEAD_DIM)
    value_heads = values.reshape(length, HEADS, HEAD_DIM)
    scores = exact_precision('qhd,khd->hqk', query_heads, key_heads) * (1.0 / math.sqrt(HEAD_DIM))
    scores = reduced_backward(scores)
    top = lax.optimization_barrier(jnp.max(scores, axis=-1, keepdims=True))
    expo = jnp.exp(scores - top)
    prob = low(expo / lax.optimization_barrier(jnp.sum(expo, axis=-1, keepdims=True)))
    mixed_tokens = exact_precision('hqk,khd->qhd', prob, value_heads)
    return mixed_tokens.reshape(length, HEADS * HEAD_DIM)

def forward(latents, cond, ada_weight, ada_bias, query_key_value_weight, qv_bias, attention_output_weight, attention_output_bias, first_dense_weight, first_dense_bias, second_dense_weight, second_dense_bias):
    seqs, length, width = latents.shape
    cond_act = low(jax.nn.silu(cond))
    stream = latents
    for layer_index in range(LAYERS):
        modulation = exact_precision('sd,df->sf', cond_act, ada_weight[layer_index]) + ada_bias[layer_index]
        modulation = modulation.reshape(seqs, 6, 1, width)
        hidden_state = low(normalize(stream) * (1.0 + modulation[:, 1]) + modulation[:, 0])
        mixed_tokens = exact_precision('nvi,itw->nvtw', hidden_state, query_key_value_weight[layer_index])
        query = round_both(mixed_tokens[:, :, 0] + qv_bias[layer_index, 0])
        keys = round_both(mixed_tokens[:, :, 1])
        values = round_both(mixed_tokens[:, :, 2] + qv_bias[layer_index, 1])
        attended_tokens = lax.map(jax.checkpoint(attend), (query, keys, values))
        attended_tokens = round_both(attended_tokens)
        branch_output = reduced_backward(exact_precision('pub,bo->puo', attended_tokens, attention_output_weight[layer_index]) + attention_output_bias[layer_index])
        middle = stream + modulation[:, 2] * branch_output
        second_hidden_state = low(normalize(middle) * (1.0 + modulation[:, 4]) + modulation[:, 3])
        before_block = reduced_backward(exact_precision('pxo,og->pxg', second_hidden_state, first_dense_weight[layer_index]) + first_dense_bias[layer_index])
        activated_hidden = low(jax.nn.gelu(before_block, approximate=True))
        feed_forward = reduced_backward(exact_precision('pub,bo->puo', activated_hidden, second_dense_weight[layer_index]) + second_dense_bias[layer_index])
        stream = middle + modulation[:, 5] * feed_forward
    return stream

def reference(latents, cond, ada_weight, ada_bias, query_key_value_weight, qv_bias, attention_output_weight, attention_output_bias, first_dense_weight, first_dense_bias, second_dense_weight, second_dense_bias, cotangent):
    arrays = (latents, cond, ada_weight, ada_bias, query_key_value_weight, qv_bias, attention_output_weight, attention_output_bias, first_dense_weight, first_dense_bias, second_dense_weight, second_dense_bias)
    arrays = tuple((item.astype(jnp.float32) for item in arrays))
    output, pull = jax.vjp(forward, *arrays)
    grads = pull(cotangent.astype(jnp.float32))
    return (output.astype(jnp.bfloat16), grads[0], grads[1], grads[2], grads[3], grads[4], grads[5], grads[6], grads[7], grads[8], grads[9], grads[10], grads[11])
```

```python
import functools
import math

import jax
import jax.numpy as jnp
from jax import lax
from jax.experimental import pallas as pl
from jax.experimental.pallas import tpu as pltpu
from jax.sharding import PartitionSpec as P

EPSILON = 1e-06
F32 = jnp.float32
BF16 = jnp.bfloat16
MESH = pl.DeviceIdType.MESH
VMEM = pl.BlockSpec(memory_space=pltpu.VMEM)
DMA = pltpu.SemaphoreType.DMA


def place():
    dp = lax.axis_index("dp")
    ctx = lax.axis_index("context")
    t = lax.axis_index("tensor")
    return dp, ctx, t, (t // 2) * 2 + dp, ctx % 4, ctx // 4, t % 2


def device(x, y, z, core):
    return (x % 2, z * 4 + y, (x // 2) * 2 + core)


def remote(src, dst, send, recv, target):
    return pltpu.make_async_remote_copy(
        src_ref=src, dst_ref=dst, send_sem=send, recv_sem=recv,
        device_id=target, device_id_type=MESH,
    )


def greet(targets):
    barrier = pltpu.get_barrier_semaphore()
    count = 0
    for first, last, target in targets:
        def one(k, carry, target=target):
            pl.semaphore_signal(barrier, inc=1, device_id=target(k), device_id_type=MESH)
            return carry
        lax.fori_loop(first, last, one, 0)
        count += last - first
    pl.semaphore_wait(barrier, count)


def z_peer(k):
    dp, ctx, t, x, y, z, core = place()
    return (dp, ((z + k) % 4) * 4 + y, t)


def y_peer(k):
    dp, ctx, t, x, y, z, core = place()
    return (dp, z * 4 + (y + k) % 4, t)


def ring_index():
    dp, ctx, t, x, y, z, core = place()
    return x * 2 + core


def ring_peer(k):
    dp, ctx, t, x, y, z, core = place()
    r = (x * 2 + core + k) % 8
    return device(r // 2, y, z, r % 2)


def plane_peer(k):
    dp, ctx, t, x, y, z, core = place()
    f = (y * 8 + x * 2 + core + k) % 32
    return device((f // 2) % 4, f // 8, z, f % 2)


def shard_peer(k):
    dp, ctx, t, x, y, z, core = place()
    f = (dp * 16 + ctx + k) % 32
    return (f // 16, f % 16, t)


def any_peer(k):
    dp, ctx, t, x, y, z, core = place()
    f = ((dp * 16 + ctx) * 4 + t + k) % 128
    return (f // 64, (f // 4) % 16, f % 4)


def gather_start(own, slots, mine, n, peer, send, recv):
    def one(k, carry):
        remote(own, slots.at[mine], send.at[k], recv.at[mine], peer(k)).start()
        return carry
    lax.fori_loop(1, n, one, 0)


def gather_wait(own, slots, mine, n, peer, send, recv):
    def one(k, carry):
        other = (mine + k) % n
        copy = remote(own, slots.at[other], send.at[k], recv.at[other], peer(k))
        copy.wait_recv()
        copy.wait_send()
        return carry
    lax.fori_loop(1, n, one, 0)


def scatter_start(parts, slots, mine, n, peer, send, recv):
    def one(k, carry):
        other = (mine + k) % n
        remote(parts.at[other], slots.at[mine], send.at[k], recv.at[mine], peer(k)).start()
        return carry
    lax.fori_loop(1, n, one, 0)


def scatter_wait(parts, slots, mine, n, peer, send, recv):
    def one(k, carry):
        other = (mine + k) % n
        copy = remote(parts.at[other], slots.at[other], send.at[k], recv.at[other], peer(k))
        copy.wait_recv()
        copy.wait_send()
        return carry
    lax.fori_loop(1, n, one, 0)


def call(kernel, collective_id, outs, scratch, args, vmem=60):
    return pl.pallas_call(
        kernel,
        out_shape=outs,
        in_specs=[VMEM] * len(args),
        out_specs=[VMEM] * len(outs),
        scratch_shapes=scratch,
        compiler_params=pltpu.CompilerParams(
            collective_id=collective_id, has_side_effects=True, vmem_limit_bytes=vmem << 20
        ),
    )(*args)


def shape(dims, dtype):
    return jax.ShapeDtypeStruct(dims, dtype)


def normalize(values):
    center = values - jnp.mean(values, axis=-1, keepdims=True)
    inverse = lax.rsqrt(jnp.mean(center * center, axis=-1, keepdims=True) + EPSILON)
    return center * inverse, inverse


def norm_back(grad_hat, normed, inverse):
    first = jnp.mean(grad_hat, axis=-1, keepdims=True)
    second = jnp.mean(grad_hat * normed, axis=-1, keepdims=True)
    return inverse * (grad_hat - first - normed * second)


def dot(left, right, contract):
    return lax.dot_general(
        left, right, ((contract[0], contract[1]), ((), ())), preferred_element_type=F32
    )


NN = ((1,), (0,))
NT = ((1,), (1,))
TN = ((0,), (0,))


def pre_kernel(lat, cot, wp, cond, ada, xg, cg, wf, modg,
               cond_b, part, parts, total,
               w_send, w_recv, w2_send, w2_recv, wx_send, wx_recv, w_local,
               x_send, x_recv, c_send, c_recv, m_send, m_recv, g_send, g_recv, k_send, k_recv):
    dp, ctx, t, x, y, z, core = place()
    x_hi = t // 2
    partner = (1 - dp, ctx, t)
    greet([(1, 128, any_peer)])
    cond_copy = remote(cond, cond_b, k_send, k_recv, partner)
    cond_copy.start()
    across = remote(wp.at[1 - dp], wf.at[dp, ctx], wx_send, wx_recv, partner)
    across.start()
    local = pltpu.make_async_copy(wp.at[dp], wf.at[dp, ctx], w_local)
    local.start()

    def tokens(src, dst, send, recv, act):
        for other in range(4):
            same = jnp.logical_and(x == y, x == other)
            target = device(other, x, z, core)
            copy = remote(src.at[x_hi], dst.at[y], send.at[other], recv.at[y], target)
            if act == "start":
                @pl.when(jnp.logical_not(same))
                def _():
                    copy.start()

                @pl.when(same)
                def _():
                    pltpu.make_async_copy(src.at[x_hi], dst.at[y], recv.at[y]).start()
            else:
                @pl.when(jnp.logical_not(same))
                def _():
                    copy.wait_send()

                remote(src.at[x_hi], dst.at[other], send.at[other], recv.at[other], partner).wait_recv()

    tokens(lat, xg, x_send, x_recv, "start")

    def own_rows(k, carry):
        peer = (ctx + k) % 16
        remote(wp.at[dp], wf.at[dp, ctx], w_send.at[k], w_recv.at[ctx], (dp, peer, t)).start()
        return carry
    lax.fori_loop(1, 16, own_rows, 0)
    tokens(cot, cg, c_send, c_recv, "start")

    cond_copy.wait()
    part[dp] = dot(cond[...].astype(BF16), ada[...], NN)
    part[1 - dp] = dot(cond_b[...].astype(BF16), ada[...], NN)

    def tensor_peer(k):
        return (dp, ctx, (t + k) % 4)
    gather_start(part, parts, t, 4, tensor_peer, m_send, m_recv)
    parts[t] = part[...]

    across.wait()

    def other_rows(k, carry):
        peer = (ctx + k) % 16
        mine = wf.at[1 - dp, ctx]
        remote(mine, mine, w2_send.at[k], w2_recv.at[ctx], (dp, peer, t)).start()
        return carry
    lax.fori_loop(1, 16, other_rows, 0)

    gather_wait(part, parts, t, 4, tensor_peer, m_send, m_recv)
    total[...] = (parts[0] + parts[1]) + (parts[2] + parts[3])
    mine = dp * 16 + ctx

    def mod_start(k, carry):
        f = (mine + k) % 32
        remote(total.at[f % 2], modg.at[mine], g_send.at[k], g_recv.at[mine], shard_peer(k)).start()
        return carry
    lax.fori_loop(1, 32, mod_start, 0)
    modg[mine] = total[y % 2]

    def mod_wait(k, carry):
        f = (mine + k) % 32
        copy = remote(total.at[0], modg.at[f], g_send.at[k], g_recv.at[f], shard_peer(k))
        copy.wait()
        return carry
    lax.fori_loop(1, 32, mod_wait, 0)
    tokens(lat, xg, x_send, x_recv, "wait")
    tokens(cot, cg, c_send, c_recv, "wait")
    local.wait()

    def rows_wait(k, carry):
        peer = (ctx + k) % 16
        remote(wp.at[dp], wf.at[dp, peer], w_send.at[k], w_recv.at[peer], (dp, peer, t)).wait()
        one = wf.at[1 - dp, peer]
        remote(one, one, w2_send.at[k], w2_recv.at[peer], (dp, peer, t)).wait()
        return carry
    lax.fori_loop(1, 16, rows_wait, 0)


def keys_kernel(own, slots, send, recv):
    z = place()[5]
    greet([(1, 4, z_peer)])
    gather_start(own, slots, z, 4, z_peer, send, recv)
    slots[z] = own[...]
    gather_wait(own, slots, z, 4, z_peer, send, recv)


def middle_kernel(parts, x_ref, vec, hidden, branch_ref, middle_ref, slots, own, s1, r1, s2, r2):
    r = ring_index()
    greet([(1, 8, ring_peer)])
    scatter_start(parts, slots, r, 8, ring_peer, s1, r1)
    slots[r] = parts[r]
    scatter_wait(parts, slots, r, 8, ring_peer, s1, r1)
    branch = jnp.sum(slots[...].astype(F32), axis=0) + vec[6:7]
    middle = x_ref[...].astype(F32) + vec[2:3] * branch
    branch_ref[...] = branch
    middle_ref[...] = middle
    normed, _ = normalize(middle)
    own[...] = (normed * (1.0 + vec[4:5]) + vec[3:4]).astype(BF16)
    gather_start(own, hidden, r, 8, ring_peer, s2, r2)
    hidden[r] = own[...]
    gather_wait(own, hidden, r, 8, ring_peer, s2, r2)


def turn_kernel(feed_parts, grad_parts, cot, branch_ref, middle_ref, vec,
                d_branch, d_middle_ref, out_ref, sums, slots1, slots2, own,
                s0, r0, s1, r1, s2, r2):
    r = ring_index()
    greet([(1, 8, ring_peer)])
    scatter_start(grad_parts, slots2, r, 8, ring_peer, s1, r1)
    scatter_start(feed_parts, slots1, r, 8, ring_peer, s0, r0)
    slots2[r] = grad_parts[r]
    slots1[r] = feed_parts[r]
    scatter_wait(grad_parts, slots2, r, 8, ring_peer, s1, r1)
    grad = cot[...].astype(F32)
    middle = middle_ref[...]
    normed, inverse = normalize(middle)
    d_hidden = jnp.sum(slots2[...].astype(F32), axis=0)
    d_middle = grad + norm_back(d_hidden * (1.0 + vec[4:5]), normed, inverse)
    own[...] = (d_middle * vec[2:3]).astype(BF16)
    gather_start(own, d_branch, r, 8, ring_peer, s2, r2)
    d_branch[r] = own[...]
    d_middle_ref[...] = d_middle
    scatter_wait(feed_parts, slots1, r, 8, ring_peer, s0, r0)
    feed = jnp.sum(slots1[...].astype(F32), axis=0) + vec[7:8]
    out_ref[...] = (middle + vec[5:6] * feed).astype(BF16)
    sums[...] = jnp.zeros_like(sums)
    sums[2:3] = jnp.sum(d_middle * branch_ref[...], axis=0, keepdims=True)
    sums[3:4] = jnp.sum(d_hidden, axis=0, keepdims=True)
    sums[4:5] = jnp.sum(d_hidden * normed, axis=0, keepdims=True)
    sums[5:6] = jnp.sum(grad * feed, axis=0, keepdims=True)
    gather_wait(own, d_branch, r, 8, ring_peer, s2, r2)


def d_keys_kernel(parts, out, slots, send, recv):
    z = place()[5]
    greet([(1, 4, z_peer)])
    scatter_start(parts, slots, z, 4, z_peer, send, recv)
    slots[z] = parts[z]
    scatter_wait(parts, slots, z, 4, z_peer, send, recv)
    out[...] = jnp.sum(slots[...].astype(F32), axis=0).astype(BF16)


def last_kernel(parts, x_ref, d_middle, block, vec, sums, small,
                grad_out, block_out, small_all,
                slots, own, m_own, m_slots, z_own, z_slots, y_own,
                s1, r1, gs, gr, bs, br, ms, mr, zs, zr, ys, yr):
    dp, ctx, t, x, y, z, core = place()
    r = ring_index()
    greet([(1, 32, plane_peer), (1, 4, z_peer)])
    scatter_start(parts, slots, r, 8, ring_peer, s1, r1)

    def spread(src, dst, send, recv, act):
        for k in range(4):
            x_hi, other = k // 2, k % 2
            x_to = 2 * x_hi + y % 2
            same = jnp.logical_and(jnp.logical_and(x_to == x, x == y), core == other)
            target = device(x_to, x, z, other)
            slot = dst.at[y // 2, core]
            recv_sem = recv.at[(y // 2) * 2 + core]
            copy = remote(src, slot, send.at[k], recv_sem, target)
            if act == "start":
                @pl.when(jnp.logical_not(same))
                def _():
                    copy.start()

                @pl.when(same)
                def _():
                    pltpu.make_async_copy(src, slot, recv_sem).start()
            else:
                @pl.when(jnp.logical_not(same))
                def _():
                    copy.wait_send()

                remote(src, dst.at[k // 2, k % 2], send.at[k], recv.at[k],
                       (1 - dp, ctx, t)).wait_recv()

    spread(block, block_out, bs, br, "start")
    slots[r] = parts[r]
    scatter_wait(parts, slots, r, 8, ring_peer, s1, r1)
    normed, inverse = normalize(x_ref[...].astype(F32))
    d_hidden = jnp.sum(slots[...].astype(F32), axis=0)
    own[...] = d_middle[...] + norm_back(d_hidden * (1.0 + vec[1:2]), normed, inverse)
    spread(own, grad_out, gs, gr, "start")
    m_own[...] = sums[...]
    m_own[0:1] = jnp.sum(d_hidden, axis=0, keepdims=True)
    m_own[1:2] = jnp.sum(d_hidden * normed, axis=0, keepdims=True)
    gather_start(m_own, m_slots, r, 8, ring_peer, ms, mr)
    m_slots[r] = m_own[...]
    gather_wait(m_own, m_slots, r, 8, ring_peer, ms, mr)
    z_own[0:8] = jnp.sum(m_slots[...], axis=0)
    z_own[8:16] = small[...]
    gather_start(z_own, z_slots, z, 4, z_peer, zs, zr)
    z_slots[z] = z_own[...]
    gather_wait(z_own, z_slots, z, 4, z_peer, zs, zr)
    y_own[...] = jnp.sum(z_slots[...], axis=0)
    gather_start(y_own, small_all, y, 4, y_peer, ys, yr)
    small_all[y] = y_own[...]
    gather_wait(y_own, small_all, y, 4, y_peer, ys, yr)
    spread(block, block_out, bs, br, "wait")
    spread(own, grad_out, gs, gr, "wait")


def weights_kernel(parts, bias, cond_part, out, bias_out, cond_out, slots, rows, c_slots,
                   ws, wr, xs, xr, ks, kr, cs, cr):
    dp, ctx, t, x, y, z, core = place()
    partner = (1 - dp, ctx, t)
    mine = dp * 16 + ctx
    greet([(1, 32, shard_peer)])
    gather_start(cond_part, c_slots, mine, 32, shard_peer, cs, cr)
    bias_copy = remote(bias, bias_out.at[dp], ks, kr, partner)
    bias_copy.start()

    def start(k, carry):
        peer = (ctx + k) % 16
        remote(parts.at[:, peer], slots.at[ctx], ws.at[k], wr.at[ctx], (dp, peer, t)).start()
        return carry
    lax.fori_loop(1, 16, start, 0)
    slots[ctx] = parts[:, ctx]
    c_slots[mine] = cond_part[...]
    bias_out[dp] = bias[...]

    def wait(k, carry):
        peer = (ctx + k) % 16
        remote(parts.at[:, peer], slots.at[peer], ws.at[k], wr.at[peer], (dp, peer, t)).wait()
        return carry
    lax.fori_loop(1, 16, wait, 0)

    def add(k, carry):
        for half in range(2):
            rows[half] += slots[k, half].astype(F32)
        return carry
    rows[...] = jnp.zeros_like(rows)
    lax.fori_loop(0, 16, add, 0)
    across = remote(rows.at[1 - dp], out.at[dp], xs, xr, partner)
    across.start()
    out[dp] = rows[dp]
    gather_wait(cond_part, c_slots, mine, 32, shard_peer, cs, cr)
    cond_out[...] = jnp.sum(c_slots[...], axis=0)
    bias_back = remote(bias, bias_out.at[1 - dp], ks, kr, partner)
    bias_back.wait()
    remote(rows.at[1 - dp], out.at[1 - dp], xs, xr, partner).wait()


def on_device(
    latents, cond, ada_weight, ada_bias, qkv_weight, qv_bias, out_weight, out_bias,
    first_weight, first_bias, second_weight, second_bias, cotangent,
):
    dp, ctx, t, x, y, z, core = place()
    ring = x * 2 + core
    scale = 1.0 / math.sqrt(64)
    cond_slice = lax.dynamic_slice_in_dim(cond.astype(F32), t * 256, 256, 1)
    cond_act = jax.nn.silu(cond_slice).astype(BF16).astype(F32)
    cond_block = jnp.pad(cond_act, ((0, 6), (0, 0)))
    ada = ada_weight[0]
    ada_pad = jnp.pad(ada, ((0, 0), (0, 64)))
    qkv_half = qkv_weight[0].reshape(32, 3, 2, 128).transpose(2, 0, 1, 3).reshape(2, 32, 384)
    out_half = out_weight[0].T.reshape(32, 2, 128).transpose(1, 0, 2)
    first_half = first_weight[0].reshape(32, 2, 512).transpose(1, 0, 2)
    second_half = second_weight[0].T.reshape(32, 2, 512).transpose(1, 0, 2)
    pack = jnp.concatenate([qkv_half, out_half, first_half, second_half], axis=2)

    xg, cg, wf, modg, cond_other = call(
        pre_kernel_out, 1,
        [shape((4, 64, 1024), BF16), shape((4, 64, 1024), BF16),
         shape((2, 16, 32, 1536), BF16), shape((32, 8, 256), F32), shape((8, 256), F32)],
        [pltpu.VMEM((2, 8, 256), F32), pltpu.VMEM((4, 2, 8, 256), F32),
         pltpu.VMEM((2, 8, 256), F32),
         DMA((16,)), DMA((16,)), DMA((16,)), DMA((16,)), DMA, DMA, DMA,
         DMA((4,)), DMA((4,)), DMA((4,)), DMA((4,)), DMA((4,)), DMA((4,)),
         DMA((32,)), DMA((32,)), DMA, DMA],
        [latents, cotangent, pack, cond_block, ada_pad],
    )
    w = wf.reshape(1024, 1536)
    w_qkv, w_out, w_first, w_second = w[:, :384], w[:, 384:512], w[:, 512:1024], w[:, 1024:]
    row = lax.dynamic_slice_in_dim(modg, y // 2, 1, 1)[:, 0, :192].reshape(6144)
    modulation = (row + ada_bias[0].astype(F32)).reshape(6, 1024)
    vec = jnp.concatenate(
        [modulation, out_bias.astype(F32), second_bias.astype(F32)], axis=0
    )
    stream = xg.reshape(256, 1024)
    cot = cg.reshape(256, 1024)
    x_own = lax.dynamic_slice_in_dim(stream, ring * 32, 32, 0)
    cot_own = lax.dynamic_slice_in_dim(cot, ring * 32, 32, 0)

    normed, _ = normalize(stream.astype(F32))
    hidden = (normed * (1.0 + vec[1]) + vec[0]).astype(BF16)
    mixed = dot(hidden, w_qkv, NN)
    biases = lax.dynamic_slice_in_dim(qv_bias[0].astype(F32), dp * 128, 128, 1)
    query = (mixed[:, :128] + biases[0]).astype(BF16)
    key_value = jnp.concatenate([mixed[:, 128:256], mixed[:, 256:] + biases[1]], axis=1).astype(BF16)
    (all_kv,) = call(
        keys_kernel, 2, [shape((4, 256, 256), BF16)], [DMA((4,)), DMA((4,))], [key_value]
    )
    all_kv = all_kv.reshape(1024, 256)
    q2 = query.reshape(256, 2, 64)
    k2 = all_kv[:, :128].reshape(1024, 2, 64)
    v2 = all_kv[:, 128:].reshape(1024, 2, 64)
    scores = jnp.einsum("qhd,khd->hqk", q2, k2, preferred_element_type=F32) * scale
    top = jnp.max(scores, axis=-1, keepdims=True)
    expo = jnp.exp(scores - top)
    prob = expo / jnp.sum(expo, axis=-1, keepdims=True)
    prob_low = prob.astype(BF16)
    attended = jnp.einsum("hqk,khd->qhd", prob_low, v2, preferred_element_type=F32)
    attended = attended.astype(BF16).reshape(256, 128)
    branch_part = dot(attended, w_out, NT).astype(BF16).reshape(8, 32, 1024)
    chunk = shape((32, 1024), F32)
    tokens = shape((8, 32, 1024), BF16)
    hidden_two, branch_own, middle_own = call(
        middle_kernel, 3, [tokens, chunk, chunk],
        [pltpu.VMEM((8, 32, 1024), BF16), pltpu.VMEM((32, 1024), BF16)] + [DMA((8,))] * 4,
        [branch_part, x_own, vec],
    )
    hidden_two = hidden_two.reshape(256, 1024)
    bias_first = lax.dynamic_slice_in_dim(first_bias[0].astype(F32), dp * 512, 512, 0)
    before = dot(hidden_two, w_first, NN) + bias_first
    activated, pull = jax.vjp(lambda v: jax.nn.gelu(v, approximate=True), before)
    activated = activated.astype(BF16)
    feed_part = dot(activated, w_second, NT).astype(BF16).reshape(8, 32, 1024)
    d_feed = (cot.astype(F32) * vec[5]).astype(BF16)
    d_before = pull(dot(d_feed, w_second, NN))[0].astype(BF16)
    grad_part = dot(d_before, w_first, NT).astype(BF16).reshape(8, 32, 1024)
    d_branch, d_middle_own, block_own, sums = call(
        turn_kernel, 4, [tokens, chunk, shape((32, 1024), BF16), shape((8, 1024), F32)],
        [pltpu.VMEM((8, 32, 1024), BF16), pltpu.VMEM((8, 32, 1024), BF16),
         pltpu.VMEM((32, 1024), BF16)] + [DMA((8,))] * 6,
        [feed_part, grad_part, cot_own, branch_own, middle_own, vec],
    )
    d_branch = d_branch.reshape(256, 1024)
    d_attended = dot(d_branch, w_out, NN).astype(BF16).reshape(256, 2, 64)
    d_prob = jnp.einsum("qhd,khd->hqk", d_attended, v2, preferred_element_type=F32)
    row_sums = jnp.sum(prob * d_prob, axis=-1, keepdims=True)
    d_scores = (prob * (d_prob - row_sums)).astype(BF16)
    d_query = jnp.einsum("hqk,khd->qhd", d_scores, k2, preferred_element_type=F32) * scale
    d_query = d_query.astype(BF16).reshape(256, 128)
    d_keys = jnp.einsum("hqk,qhd->khd", d_scores, q2, preferred_element_type=F32) * scale
    d_values = jnp.einsum("hqk,qhd->khd", prob_low, d_attended, preferred_element_type=F32)
    d_kv = jnp.concatenate([d_keys.reshape(1024, 128), d_values.reshape(1024, 128)], axis=1)
    (d_kv,) = call(
        d_keys_kernel, 5, [shape((256, 256), BF16)],
        [pltpu.VMEM((4, 256, 256), BF16), DMA((4,)), DMA((4,))],
        [d_kv.astype(BF16).reshape(4, 256, 256)],
    )
    d_qkv = jnp.concatenate([d_query, d_kv], axis=1)
    d_hidden_part = dot(d_qkv, w_qkv, NT).astype(BF16).reshape(8, 32, 1024)
    bias_row = jnp.concatenate([
        jnp.sum(d_before.astype(F32), axis=0),
        jnp.sum(d_query.astype(F32), axis=0),
        jnp.sum(d_kv[:, 128:].astype(F32), axis=0),
        jnp.zeros((256,), F32),
    ])
    small = jnp.concatenate([
        jnp.sum(d_branch.astype(F32), axis=0)[None],
        jnp.sum(d_feed.astype(F32), axis=0)[None],
        bias_row[None],
        jnp.zeros((5, 1024), F32),
    ], axis=0)
    latents_grad, block_out, small_all = call(
        last_kernel, 6,
        [shape((2, 2, 32, 1024), F32), shape((2, 2, 32, 1024), BF16), shape((4, 16, 1024), F32)],
        [pltpu.VMEM((8, 32, 1024), BF16), pltpu.VMEM((32, 1024), F32),
         pltpu.VMEM((8, 1024), F32), pltpu.VMEM((8, 8, 1024), F32),
         pltpu.VMEM((16, 1024), F32), pltpu.VMEM((4, 16, 1024), F32), pltpu.VMEM((16, 1024), F32),
         DMA((8,)), DMA((8,)), DMA((4,)), DMA((4,)), DMA((4,)), DMA((4,)),
         DMA((8,)), DMA((8,)), DMA((4,)), DMA((4,)), DMA((4,)), DMA((4,))],
        [d_hidden_part, x_own, d_middle_own, block_own, vec, sums, small],
    )
    d_mod = small_all[:, :6].reshape(2, 2, 6144).transpose(1, 0, 2).reshape(4, 6144)
    biases = jnp.sum(small_all[:, 8:11], axis=0)
    d_mod_part = lax.dynamic_slice_in_dim(d_mod, (dp * 16 + ctx) * 192, 192, 1)
    cond_pair = jnp.stack([cond_act, cond_other[:2]])
    cond_four = jnp.where(dp == 0, cond_pair, cond_pair[::-1]).reshape(4, 256)
    highest = lax.Precision.HIGHEST
    ada_grad = jnp.dot(cond_four.T, d_mod_part, precision=highest)
    cond_part = jnp.dot(d_mod_part, ada.astype(F32).T, precision=highest)
    grads = jnp.concatenate([
        dot(hidden, d_qkv, TN), dot(d_branch, attended, TN),
        dot(hidden_two, d_before, TN), dot(d_feed, activated, TN),
    ], axis=1).astype(BF16).reshape(2, 16, 32, 1536)
    w_grad, bias_pair, cond_total = call(
        weights_kernel, 7,
        [shape((2, 32, 1536), F32), shape((2, 8, 1024), F32), shape((8, 256), F32)],
        [pltpu.VMEM((16, 2, 32, 1536), BF16), pltpu.VMEM((2, 32, 1536), F32),
         pltpu.VMEM((32, 8, 256), F32),
         DMA((16,)), DMA((16,)), DMA, DMA, DMA, DMA, DMA((32,)), DMA((32,))],
        [grads, jnp.pad(biases[2:3], ((0, 7), (0, 0))), jnp.pad(cond_part, ((0, 4), (0, 0)))],
    )
    sigmoid = jax.nn.sigmoid(cond_slice)
    cond_mine = lax.dynamic_slice_in_dim(cond_total, dp * 2, 2, 0)
    cond_grad = cond_mine * sigmoid * (1.0 + cond_slice * (1.0 - sigmoid))
    pair = bias_pair[:, 0]
    qkv_grad = w_grad[:, :, :384].reshape(2, 32, 3, 128).transpose(1, 2, 0, 3).reshape(1, 32, 3, 256)
    out_grad = w_grad[:, :, 384:512].transpose(0, 2, 1).reshape(1, 256, 32)
    first_grad = w_grad[:, :, 512:1024].transpose(1, 0, 2).reshape(1, 32, 1024)
    second_grad = w_grad[:, :, 1024:].transpose(0, 2, 1).reshape(1, 1024, 32)
    return (
        block_out.reshape(2, 64, 1024),
        latents_grad.reshape(2, 64, 1024),
        cond_grad,
        ada_grad[None],
        jnp.sum(d_mod, axis=0)[None],
        qkv_grad,
        pair[:, 512:768].reshape(2, 2, 128).transpose(1, 0, 2).reshape(1, 2, 256),
        out_grad,
        biases[0:1],
        first_grad,
        pair[:, :512].reshape(1, 1024),
        second_grad,
        biases[1:2],
    )


def pre_kernel_out(lat, cot, wp, cond, ada, xg, cg, wf, modg, cond_b, part, parts, total, *sems):
    pre_kernel(lat, cot, wp, cond, ada, xg, cg, wf, modg, cond_b, part, parts, total, *sems)


def solution(mesh):
    return jax.shard_map(
        on_device,
        mesh=mesh,
        in_specs=(
            P("dp", "context", None),
            P("dp", None),
            P(None, "tensor", ("dp", "context")),
            P(),
            P(None, ("dp", "context"), None, "tensor"),
            P(None, None, "tensor"),
            P(None, "tensor", ("dp", "context")),
            P(),
            P(None, ("dp", "context"), "tensor"),
            P(None, "tensor"),
            P(None, "tensor", ("dp", "context")),
            P(),
            P("dp", "context", None),
        ),
        out_specs=(
            P("dp", "context", None),
            P("dp", "context", None),
            P("dp", "tensor"),
            P(None, "tensor", ("dp", "context")),
            P(),
            P(None, ("dp", "context"), None, "tensor"),
            P(None, None, "tensor"),
            P(None, "tensor", ("dp", "context")),
            P(),
            P(None, ("dp", "context"), "tensor"),
            P(None, "tensor"),
            P(None, "tensor", ("dp", "context")),
            P(),
        ),
        check_vma=False,
    )
```

```python
import math

import jax
import jax.numpy as jnp
from jax import lax
from jax.experimental import pallas as pl
from jax.experimental.pallas import tpu as pltpu
from jax.sharding import PartitionSpec as P

EPSILON = 1e-06
F32 = jnp.float32
BF16 = jnp.bfloat16
MESH = pl.DeviceIdType.MESH
VMEM = pl.BlockSpec(memory_space=pltpu.VMEM)
DMA = pltpu.SemaphoreType.DMA


def place():
    dp = lax.axis_index("dp")
    ctx = lax.axis_index("context")
    t = lax.axis_index("tensor")
    return dp, ctx, t, (t // 2) * 2 + dp, ctx % 4, ctx // 4, t % 2


def device(x, y, z, core):
    return (x % 2, z * 4 + y, (x // 2) * 2 + core)


def remote(src, dst, send, recv, target):
    return pltpu.make_async_remote_copy(
        src_ref=src, dst_ref=dst, send_sem=send, recv_sem=recv,
        device_id=target, device_id_type=MESH,
    )


def greet(targets):
    barrier = pltpu.get_barrier_semaphore()
    count = 0
    for first, last, target in targets:
        def one(k, carry, target=target):
            pl.semaphore_signal(barrier, inc=1, device_id=target(k), device_id_type=MESH)
            return carry
        lax.fori_loop(first, last, one, 0)
        count += last - first
    pl.semaphore_wait(barrier, count)


def z_peer(k):
    dp, ctx, t, x, y, z, core = place()
    return (dp, ((z + k) % 4) * 4 + y, t)


def y_peer(k):
    dp, ctx, t, x, y, z, core = place()
    return (dp, z * 4 + (y + k) % 4, t)


def ring_index():
    dp, ctx, t, x, y, z, core = place()
    return x * 2 + core


def ring_peer(k):
    dp, ctx, t, x, y, z, core = place()
    r = (x * 2 + core + k) % 8
    return device(r // 2, y, z, r % 2)


def gather_start(own, slots, mine, n, peer, send, recv):
    def one(k, carry):
        remote(own, slots.at[mine], send.at[k], recv.at[mine], peer(k)).start()
        return carry
    lax.fori_loop(1, n, one, 0)


def gather_wait(own, slots, mine, n, peer, send, recv):
    def one(k, carry):
        other = (mine + k) % n
        copy = remote(own, slots.at[other], send.at[k], recv.at[other], peer(k))
        copy.wait_recv()
        copy.wait_send()
        return carry
    lax.fori_loop(1, n, one, 0)


def scatter_start(parts, slots, mine, n, peer, send, recv):
    def one(k, carry):
        other = (mine + k) % n
        remote(parts.at[other], slots.at[mine], send.at[k], recv.at[mine], peer(k)).start()
        return carry
    lax.fori_loop(1, n, one, 0)


def scatter_wait(parts, slots, mine, n, peer, send, recv):
    def one(k, carry):
        other = (mine + k) % n
        copy = remote(parts.at[other], slots.at[other], send.at[k], recv.at[other], peer(k))
        copy.wait_recv()
        copy.wait_send()
        return carry
    lax.fori_loop(1, n, one, 0)


def shape(dims, dtype):
    return jax.ShapeDtypeStruct(dims, dtype)


def normalize(values):
    center = values - jnp.mean(values, axis=-1, keepdims=True)
    inverse = lax.rsqrt(jnp.mean(center * center, axis=-1, keepdims=True) + EPSILON)
    return center * inverse, inverse


def norm_back(grad_hat, normed, inverse):
    first = jnp.mean(grad_hat, axis=-1, keepdims=True)
    second = jnp.mean(grad_hat * normed, axis=-1, keepdims=True)
    return inverse * (grad_hat - first - normed * second)


def dot(left, right, contract, precision=None):
    return lax.dot_general(
        left, right, (contract, ((), ())), precision=precision, preferred_element_type=F32
    )


NN = ((1,), (0,))
NT = ((1,), (1,))
TN = ((0,), (0,))
SCALE = 1.0 / math.sqrt(64)
ROOT = math.sqrt(2.0 / math.pi)
STEPS = (1, 3, 2)


def from_back(k):
    y, z = lax.axis_index("context") % 4, lax.axis_index("context") // 4
    return (y + 4 - k) % 4, (z + 4 - k) % 4


def plane_one(full, h, send, recv, start):
    dp, ctx, t, x, y, z, core = place()
    mine = full.at[h, z, y]
    for k in STEPS:
        target = (dp, ((z + h * k) % 4) * 4 + (y + (1 - h) * k) % 4, t)
        if start:
            remote(mine, mine, send.at[h, k], recv.at[h, k], target).start()
        else:
            slot = full.at[h, (z + h * (4 - k)) % 4, (y + (1 - h) * (4 - k)) % 4]
            remote(mine, slot, send.at[h, k], recv.at[h, k], target).wait()


def plane_two(full, send, recv, start):
    dp, ctx, t, x, y, z, core = place()
    for k in STEPS:
        by, bz = from_back(k)
        row, column = full.at[0, z], full.at[1, :, y]
        if start:
            remote(row, row, send.at[0, k], recv.at[0, k], z_peer(k)).start()
            remote(column, column, send.at[1, k], recv.at[1, k], y_peer(k)).start()
        else:
            remote(row, full.at[0, bz], send.at[0, k], recv.at[0, k], z_peer(k)).wait()
            remote(column, full.at[1, :, by], send.at[1, k], recv.at[1, k], y_peer(k)).wait()


def reduce_one(parts, slots, send, recv, start):
    dp, ctx, t, x, y, z, core = place()
    for k in STEPS:
        by, bz = from_back(k)
        row, column = parts.at[0, (z + k) % 4], parts.at[1, :, (y + k) % 4]
        to_row = slots.at[0, z if start else bz]
        to_column = slots.at[1, y if start else by]
        for copy in (remote(row, to_row, send.at[0, k], recv.at[0, k], z_peer(k)),
                     remote(column, to_column, send.at[1, k], recv.at[1, k], y_peer(k))):
            copy.start() if start else copy.wait()
    if start:
        slots[0, z] = parts[0, z]
        slots[1, y] = parts[1, :, y]


def reduce_two(parts, slots, send, recv, start):
    dp, ctx, t, x, y, z, core = place()
    for k in STEPS:
        by, bz = from_back(k)
        to_y = slots.at[0, y if start else by]
        to_z = slots.at[1, z if start else bz]
        for copy in (remote(parts.at[0, (y + k) % 4], to_y, send.at[0, k], recv.at[0, k], y_peer(k)),
                     remote(parts.at[1, (z + k) % 4], to_z, send.at[1, k], recv.at[1, k], z_peer(k))):
            copy.start() if start else copy.wait()
    if start:
        slots[0, y] = parts[0, y]
        slots[1, z] = parts[1, z]


def add_slots(slots, out):
    for h in range(2):
        total = slots[h, 0].astype(F32)
        for k in range(1, 4):
            total = total + slots[h, k].astype(F32)
        out[h] = total.astype(out.dtype)


def tokens(src, dst, send, recv, start):
    dp, ctx, t, x, y, z, core = place()
    for other in range(4):
        same = jnp.logical_and(x == y, x == other)
        copy = remote(src.at[t // 2], dst.at[y], send.at[other], recv.at[y],
                      device(other, x, z, core))
        if start:
            @pl.when(jnp.logical_not(same))
            def _():
                copy.start()

            @pl.when(same)
            def _():
                pltpu.make_async_copy(src.at[t // 2], dst.at[y], recv.at[y]).start()
        else:
            @pl.when(jnp.logical_not(same))
            def _():
                copy.wait_send()

            remote(src.at[t // 2], dst.at[other], send.at[other], recv.at[other],
                   (1 - dp, ctx, t)).wait_recv()


def spread(src, dst, send, recv, start):
    dp, ctx, t, x, y, z, core = place()
    for k in range(4):
        x_hi, other = k // 2, k % 2
        x_to = 2 * x_hi + y % 2
        same = jnp.logical_and(jnp.logical_and(x_to == x, x == y), core == other)
        slot = dst.at[y // 2, core]
        recv_sem = recv.at[(y // 2) * 2 + core]
        copy = remote(src, slot, send.at[k], recv_sem, device(x_to, x, z, other))
        if start:
            @pl.when(jnp.logical_not(same))
            def _():
                copy.start()

            @pl.when(same)
            def _():
                pltpu.make_async_copy(src, slot, recv_sem).start()
        else:
            @pl.when(jnp.logical_not(same))
            def _():
                copy.wait_send()

            remote(src, dst.at[k // 2, k % 2], send.at[k], recv.at[k],
                   (1 - dp, ctx, t)).wait_recv()


def tokens_target(k):
    dp, ctx, t, x, y, z, core = place()
    return device(k, x, z, core)


def tokens_source(k):
    dp, ctx, t, x, y, z, core = place()
    return device(y, k, z, core)


def spread_target(k):
    dp, ctx, t, x, y, z, core = place()
    return device(2 * (k // 2) + y % 2, x, z, k % 2)


def spread_source(k):
    dp, ctx, t, x, y, z, core = place()
    return device(y, 2 * (k // 2) + dp, z, k % 2)


def ctx_peer(k):
    dp, ctx, t, x, y, z, core = place()
    return (dp, (ctx + k) % 16, t)


INPUTS = dict(lat=0, cot=1, packa=2, packb=3, cond=4, ada=5, ada_bias=6, qv=7, b1=8, ob=9, b2=10)
OUTPUTS = dict(
    block_out=((2, 2, 32, 1024), BF16),
    grad_out=((2, 2, 32, 1024), F32),
    cond_out=((8, 256), F32),
    ada_out=((256, 256), F32),
    ada_bias_out=((1, 6144), F32),
    ga_out=((2, 32, 512), F32),
    gb_out=((2, 32, 1024), F32),
    bias_out=((2, 8, 1024), F32),
    wide_out=((8, 1024), F32),
)
BUFFERS = dict(
    xg=((4, 64, 1024), BF16), cg=((4, 64, 1024), BF16),
    wa=((2, 4, 4, 32, 512), BF16), wb=((2, 4, 4, 32, 1024), BF16),
    cond_b=((8, 256), F32), cond8=((8, 256), F32),
    part=((8, 256), F32), parts=((8, 8, 256), F32), pair=((2, 8, 256), F32),
    modg=((16, 2, 8, 256), F32), flat=((8, 6144), F32), vec=((8, 1024), F32),
    normed=((256, 1024), F32), hidden=((256, 1024), BF16),
    kv=((256, 256), BF16), kvg=((4, 256, 256), BF16), prob=((2, 256, 1024), F32),
    branch_part=((8, 32, 1024), BF16), branch_slots=((8, 32, 1024), BF16),
    h2_own=((32, 1024), BF16), h2=((8, 32, 1024), BF16),
    d_feed=((256, 1024), BF16), d_act=((256, 512), F32),
    dh2_part=((8, 32, 1024), BF16), dh2_slots=((8, 32, 1024), BF16),
    feed_part=((8, 32, 1024), BF16), feed_slots=((8, 32, 1024), BF16),
    db_own=((32, 1024), BF16), db=((8, 32, 1024), BF16),
    block_own=((32, 1024), BF16), d_middle=((32, 1024), F32),
    dkv_part=((4, 256, 256), BF16), dkv_slots=((4, 256, 256), BF16),
    dh_part=((8, 32, 1024), BF16), dh_slots=((8, 32, 1024), BF16),
    grad_own=((32, 1024), F32),
    m_own=((8, 1024), F32), m_slots=((8, 8, 1024), F32),
    z_own=((16, 1024), F32), z_slots=((4, 16, 1024), F32),
    y_own=((16, 1024), F32), y_slots=((4, 16, 1024), F32),
    dm=((8, 6144), F32), bias_own=((8, 1024), F32),
    cond_part=((8, 256), F32), cond_slots=((16, 8, 256), F32), cond_sum=((8, 256), F32),
    cond_other=((8, 256), F32),
    ga=((2, 4, 4, 32, 512), BF16), ga1=((2, 4, 4, 32, 512), BF16),
    ga2=((2, 4, 32, 512), BF16), ga3=((2, 4, 32, 512), BF16), gas=((2, 32, 512), F32),
    gb=((2, 4, 4, 32, 1024), BF16), gb1=((2, 4, 4, 32, 1024), BF16),
    gb2=((2, 4, 32, 1024), BF16), gb3=((2, 4, 32, 1024), BF16), gbs=((2, 32, 1024), F32),
)
SEMS = dict(
    s_cond=(), s_xa=(), s_xb=(), s_xg=(4,), s_cg=(4,),
    s_wa1=(2, 4), s_wa2=(2, 4), s_wb1=(2, 4), s_wb2=(2, 4),
    s_mod=(8,), s_mod2=(16,), s_kv=(4,),
    s_branch=(8,), s_h2=(8,), s_dh2=(8,), s_feed=(8,), s_db=(8,),
    s_block=(4,), s_dkv=(4,), s_dh=(8,), s_grad=(4,),
    s_m=(8,), s_z=(4,), s_y=(4,), s_bias=(), s_c=(16,), s_cx=(),
    s_ga1=(2, 4), s_ga2=(2, 4), s_gb1=(2, 4), s_gb2=(2, 4), s_gax=(), s_gbx=(),
)


class Refs:
    pass


def block_kernel(*refs):
    g = Refs()
    names = list(INPUTS) + list(OUTPUTS) + list(BUFFERS)
    for name, ref in zip(names, refs):
        setattr(g, name, ref)
    sems = refs[len(names):]
    for i, name in enumerate(SEMS):
        setattr(g, name, (sems[2 * i], sems[2 * i + 1]))
    dp, ctx, t, x, y, z, core = place()
    r = x * 2 + core
    partner = (1 - dp, ctx, t)

    greet([(1, 8, ring_peer), (1, 16, ctx_peer)] + [(0, 4, f) for f in (
        tokens_target, tokens_source, spread_target, spread_source)])

    cond_copy = remote(g.cond, g.cond_b, *g.s_cond, partner)
    cond_copy.start()
    across_a = remote(g.packa.at[1 - dp], g.wa.at[dp, z, y], *g.s_xa, partner)
    across_a.start()
    g.wa[dp, z, y] = g.packa[dp]
    plane_one(g.wa, dp, *g.s_wa1, True)
    tokens(g.lat, g.xg, *g.s_xg, True)
    cond_copy.wait()
    g.cond8[...] = g.cond[...] + g.cond_b[...]
    g.part[...] = dot(g.cond8[...].astype(BF16), g.ada[...], NN)
    gather_start(g.part, g.parts, r, 8, ring_peer, *g.s_mod)
    g.parts[r] = g.part[...]
    across_b = remote(g.packb.at[1 - dp], g.wb.at[dp, z, y], *g.s_xb, partner)
    across_b.start()
    g.wb[dp, z, y] = g.packb[dp]
    remote(g.packa.at[1 - dp], g.wa.at[1 - dp, z, y], *g.s_xa, partner).wait()
    plane_one(g.wa, 1 - dp, *g.s_wa1, True)
    gather_wait(g.part, g.parts, r, 8, ring_peer, *g.s_mod)
    for c in range(2):
        g.pair[c] = (g.parts[2 * c] + g.parts[2 * c + 1]) + (g.parts[2 * c + 4] + g.parts[2 * c + 5])
    gather_start(g.pair, g.modg, ctx, 16, ctx_peer, *g.s_mod2)
    g.modg[ctx] = g.pair[...]
    plane_one(g.wa, dp, *g.s_wa1, False)
    plane_one(g.wa, 1 - dp, *g.s_wa1, False)
    plane_two(g.wa, *g.s_wa2, True)
    plane_one(g.wb, dp, *g.s_wb1, True)
    remote(g.packb.at[1 - dp], g.wb.at[1 - dp, z, y], *g.s_xb, partner).wait()
    plane_one(g.wb, 1 - dp, *g.s_wb1, True)
    tokens(g.cot, g.cg, *g.s_cg, True)

    tokens(g.lat, g.xg, *g.s_xg, False)
    normed, _ = normalize(g.xg[...].astype(F32).reshape(256, 1024))
    g.normed[...] = normed
    gather_wait(g.pair, g.modg, ctx, 16, ctx_peer, *g.s_mod2)
    for p in range(16):
        c, first = p // 8, (2 * p) % 16
        both = jnp.concatenate([g.modg[first, c][:, :192], g.modg[first + 1, c][:, :192]], axis=1)
        g.flat[:, 384 * p:384 * p + 384] = (
            both + g.ada_bias[0:1, 384 * p:384 * p + 384].astype(F32))
    for k in range(6):
        g.vec[k:k + 1] = g.flat[pl.ds(y, 1), k * 1024:(k + 1) * 1024]
    shift1, scale1, gate1, shift2, scale2, gate2 = [g.vec[k:k + 1] for k in range(6)]
    hidden = (g.normed[...] * (1.0 + scale1) + shift1).astype(BF16)
    g.hidden[...] = hidden
    plane_two(g.wa, *g.s_wa2, False)
    mixed = dot(hidden, g.wa[:, :, :, :, :384].reshape(1024, 384), NN)
    query = (mixed[:, :128] + g.qv[0:1]).astype(BF16)
    g.kv[:, :128] = mixed[:, 128:256].astype(BF16)
    g.kv[:, 128:] = (mixed[:, 256:] + g.qv[1:2]).astype(BF16)
    gather_start(g.kv, g.kvg, z, 4, z_peer, *g.s_kv)
    g.kvg[z] = g.kv[...]
    plane_one(g.wb, dp, *g.s_wb1, False)
    plane_one(g.wb, 1 - dp, *g.s_wb1, False)
    plane_two(g.wb, *g.s_wb2, True)
    gather_wait(g.kv, g.kvg, z, 4, z_peer, *g.s_kv)

    heads = []
    for h in range(2):
        key = g.kvg[:, :, 64 * h:64 * h + 64].reshape(1024, 64)
        value = g.kvg[:, :, 128 + 64 * h:192 + 64 * h].reshape(1024, 64)
        scores = dot(query[:, 64 * h:64 * h + 64], key, NT) * SCALE
        expo = jnp.exp(scores - jnp.max(scores, axis=-1, keepdims=True))
        prob = expo / jnp.sum(expo, axis=-1, keepdims=True)
        g.prob[h] = prob
        heads.append(dot(prob.astype(BF16), value, NN))
    attended = jnp.concatenate(heads, axis=1).astype(BF16)
    w_out = g.wa[:, :, :, :, 384:].reshape(1024, 128)
    g.branch_part[...] = dot(attended, w_out, NT).astype(BF16).reshape(8, 32, 1024)
    scatter_start(g.branch_part, g.branch_slots, r, 8, ring_peer, *g.s_branch)
    g.branch_slots[r] = g.branch_part[r]
    tokens(g.cot, g.cg, *g.s_cg, False)
    d_feed = (g.cg[...].astype(F32).reshape(256, 1024) * gate2).astype(BF16)
    g.d_feed[...] = d_feed
    plane_two(g.wb, *g.s_wb2, False)
    w_second = g.wb[:, :, :, :, 512:].reshape(1024, 512)
    g.d_act[...] = dot(d_feed, w_second, NN)
    g.z_own[...] = jnp.zeros_like(g.z_own)
    g.z_own[9:10] = jnp.sum(d_feed.astype(F32), axis=0, keepdims=True)
    scatter_wait(g.branch_part, g.branch_slots, r, 8, ring_peer, *g.s_branch)

    own_rows = pl.ds(pl.multiple_of(core * 32, 32), 32)
    x_own = g.xg[x, own_rows].astype(F32)
    branch = jnp.sum(g.branch_slots[...].astype(F32), axis=0) + g.ob[...].astype(F32)
    middle = x_own + gate1 * branch
    normed_two, inverse_two = normalize(middle)
    g.h2_own[...] = (normed_two * (1.0 + scale2) + shift2).astype(BF16)
    gather_start(g.h2_own, g.h2, r, 8, ring_peer, *g.s_h2)
    g.h2[r] = g.h2_own[...]
    gather_wait(g.h2_own, g.h2, r, 8, ring_peer, *g.s_h2)

    hidden_two = g.h2[...].reshape(256, 1024)
    w_first = g.wb[:, :, :, :, :512].reshape(1024, 512)
    before = dot(hidden_two, w_first, NN) + g.b1[...]
    square = before * before
    tanh = jnp.tanh(ROOT * before * (1.0 + 0.044715 * square))
    activated = (0.5 * before * (1.0 + tanh)).astype(BF16)
    slope = 0.5 * (1.0 + tanh) + (0.5 * ROOT) * before * (1.0 - tanh * tanh) * (
        1.0 + (3.0 * 0.044715) * square)
    d_before = (g.d_act[...] * slope).astype(BF16)
    g.dh2_part[...] = dot(d_before, w_first, NT).astype(BF16).reshape(8, 32, 1024)
    scatter_start(g.dh2_part, g.dh2_slots, r, 8, ring_peer, *g.s_dh2)
    g.dh2_slots[r] = g.dh2_part[r]
    g.feed_part[...] = dot(activated, w_second, NT).astype(BF16).reshape(8, 32, 1024)
    g.gb[:, :, :, :, :512] = dot(hidden_two, d_before, TN).astype(BF16).reshape(2, 4, 4, 32, 512)
    g.gb[:, :, :, :, 512:] = dot(d_feed, activated, TN).astype(BF16).reshape(2, 4, 4, 32, 512)
    reduce_one(g.gb, g.gb1, *g.s_gb1, True)
    g.z_own[10:11, :512] = jnp.sum(d_before.astype(F32), axis=0, keepdims=True)
    scatter_wait(g.dh2_part, g.dh2_slots, r, 8, ring_peer, *g.s_dh2)

    cot_own = g.cg[x, own_rows].astype(F32)
    d_hidden = jnp.sum(g.dh2_slots[...].astype(F32), axis=0)
    d_middle = cot_own + norm_back(d_hidden * (1.0 + scale2), normed_two, inverse_two)
    g.d_middle[...] = d_middle
    g.db_own[...] = (d_middle * gate1).astype(BF16)
    gather_start(g.db_own, g.db, r, 8, ring_peer, *g.s_db)
    scatter_start(g.feed_part, g.feed_slots, r, 8, ring_peer, *g.s_feed)
    g.db[r] = g.db_own[...]
    g.feed_slots[r] = g.feed_part[r]
    g.m_own[...] = jnp.zeros_like(g.m_own)
    g.m_own[2:3] = jnp.sum(d_middle * branch, axis=0, keepdims=True)
    g.m_own[3:4] = jnp.sum(d_hidden, axis=0, keepdims=True)
    g.m_own[4:5] = jnp.sum(d_hidden * normed_two, axis=0, keepdims=True)
    gather_wait(g.db_own, g.db, r, 8, ring_peer, *g.s_db)

    d_branch = g.db[...].reshape(256, 1024)
    d_attended = dot(d_branch, w_out, NN).astype(BF16)
    d_query, d_key, d_value = [], [], []
    for h in range(2):
        key = g.kvg[:, :, 64 * h:64 * h + 64].reshape(1024, 64)
        value = g.kvg[:, :, 128 + 64 * h:192 + 64 * h].reshape(1024, 64)
        d_one = d_attended[:, 64 * h:64 * h + 64]
        prob = g.prob[h]
        d_prob = dot(d_one, value, NT)
        d_scores = (prob * (d_prob - jnp.sum(prob * d_prob, axis=-1, keepdims=True))).astype(BF16)
        d_key.append(dot(d_scores, query[:, 64 * h:64 * h + 64], TN) * SCALE)
        d_value.append(dot(prob.astype(BF16), d_one, TN))
        d_query.append(dot(d_scores, key, NN) * SCALE)
    d_kv = jnp.concatenate(d_key + d_value, axis=1).astype(BF16)
    g.dkv_part[...] = d_kv.reshape(4, 256, 256)
    scatter_start(g.dkv_part, g.dkv_slots, z, 4, z_peer, *g.s_dkv)
    g.dkv_slots[z] = g.dkv_part[z]
    d_query = jnp.concatenate(d_query, axis=1).astype(BF16)
    g.ga[:, :, :, :, 384:] = dot(d_branch, attended, TN).astype(BF16).reshape(2, 4, 4, 32, 128)
    g.z_own[8:9] = jnp.sum(d_branch.astype(F32), axis=0, keepdims=True)
    g.z_own[10:11, 512:640] = jnp.sum(d_query.astype(F32), axis=0, keepdims=True)
    scatter_wait(g.feed_part, g.feed_slots, r, 8, ring_peer, *g.s_feed)
    feed = jnp.sum(g.feed_slots[...].astype(F32), axis=0) + g.b2[...].astype(F32)
    g.block_own[...] = (middle + gate2 * feed).astype(BF16)
    spread(g.block_own, g.block_out, *g.s_block, True)
    g.m_own[5:6] = jnp.sum(cot_own * feed, axis=0, keepdims=True)
    reduce_one(g.gb, g.gb1, *g.s_gb1, False)
    add_slots(g.gb1, g.gb2)
    reduce_two(g.gb2, g.gb3, *g.s_gb2, True)
    scatter_wait(g.dkv_part, g.dkv_slots, z, 4, z_peer, *g.s_dkv)

    d_kv = jnp.sum(g.dkv_slots[...].astype(F32), axis=0).astype(BF16)
    g.z_own[10:11, 640:768] = jnp.sum(d_kv[:, 128:].astype(F32), axis=0, keepdims=True)
    d_qkv = jnp.concatenate([d_query, d_kv], axis=1)
    d_part = dot(d_qkv, g.wa[:, :, :, :, :384].reshape(1024, 384), NT)
    g.dh_part[...] = d_part.astype(BF16).reshape(8, 32, 1024)
    scatter_start(g.dh_part, g.dh_slots, r, 8, ring_peer, *g.s_dh)
    g.m_own[0:1] = jnp.sum(d_part, axis=0, keepdims=True)
    g.m_own[1:2] = jnp.sum(d_part * g.normed[...], axis=0, keepdims=True)
    gather_start(g.m_own, g.m_slots, r, 8, ring_peer, *g.s_m)
    g.dh_slots[r] = g.dh_part[r]
    g.m_slots[r] = g.m_own[...]
    g.ga[:, :, :, :, :384] = dot(g.hidden[...], d_qkv, TN).astype(BF16).reshape(2, 4, 4, 32, 384)
    reduce_one(g.ga, g.ga1, *g.s_ga1, True)
    gather_wait(g.m_own, g.m_slots, r, 8, ring_peer, *g.s_m)
    g.z_own[0:8] = jnp.sum(g.m_slots[...], axis=0)
    gather_start(g.z_own, g.z_slots, z, 4, z_peer, *g.s_z)
    g.z_slots[z] = g.z_own[...]
    scatter_wait(g.dh_part, g.dh_slots, r, 8, ring_peer, *g.s_dh)

    x_normed, x_inverse = normalize(x_own)
    d_hidden = jnp.sum(g.dh_slots[...].astype(F32), axis=0)
    g.grad_own[...] = g.d_middle[...] + norm_back(d_hidden * (1.0 + scale1), x_normed, x_inverse)
    spread(g.grad_own, g.grad_out, *g.s_grad, True)
    gather_wait(g.z_own, g.z_slots, z, 4, z_peer, *g.s_z)
    g.y_own[...] = jnp.sum(g.z_slots[...], axis=0)
    gather_start(g.y_own, g.y_slots, y, 4, y_peer, *g.s_y)
    g.y_slots[y] = g.y_own[...]
    reduce_two(g.gb2, g.gb3, *g.s_gb2, False)
    add_slots(g.gb3, g.gbs)
    remote(g.gbs.at[1 - dp], g.gb_out.at[dp], *g.s_gbx, partner).start()
    g.gb_out[dp] = g.gbs[dp]
    reduce_one(g.ga, g.ga1, *g.s_ga1, False)
    add_slots(g.ga1, g.ga2)
    reduce_two(g.ga2, g.ga3, *g.s_ga2, True)
    gather_wait(g.y_own, g.y_slots, y, 4, y_peer, *g.s_y)

    total = jnp.sum(g.y_slots[...], axis=0)
    g.wide_out[...] = total[8:16]
    g.bias_own[...] = total[8:16]
    remote(g.bias_own, g.bias_out.at[dp], *g.s_bias, partner).start()
    g.bias_out[dp] = g.bias_own[...]
    g.dm[...] = jnp.zeros_like(g.dm)
    for k in range(6):
        for i in range(4):
            g.dm[i:i + 1, k * 1024:(k + 1) * 1024] = g.y_slots[i, k:k + 1]
        g.ada_bias_out[:, k * 1024:(k + 1) * 1024] = total[k:k + 1]
    chunk = dp * 16 + ctx
    columns = g.dm[:, pl.ds(pl.multiple_of(((3 * chunk) // 2) * 128, 128), 256)]
    columns = jnp.where(chunk % 2 == 1, pltpu.roll(columns, 192, 1), columns)
    g.cond_part[...] = dot(columns, g.ada[...].astype(F32), NT, lax.Precision.HIGHEST)
    gather_start(g.cond_part, g.cond_slots, ctx, 16, ctx_peer, *g.s_c)
    g.cond_slots[ctx] = g.cond_part[...]
    g.ada_out[...] = dot(g.cond8[...], columns, TN, lax.Precision.HIGHEST)
    gather_wait(g.cond_part, g.cond_slots, ctx, 16, ctx_peer, *g.s_c)
    g.cond_sum[...] = jnp.sum(g.cond_slots[...], axis=0)
    cond_copy = remote(g.cond_sum, g.cond_other, *g.s_cx, partner)
    cond_copy.start()
    reduce_two(g.ga2, g.ga3, *g.s_ga2, False)
    add_slots(g.ga3, g.gas)
    remote(g.gas.at[1 - dp], g.ga_out.at[dp], *g.s_gax, partner).start()
    g.ga_out[dp] = g.gas[dp]
    cond_copy.wait()
    g.cond_out[...] = g.cond_sum[...] + g.cond_other[...]
    remote(g.bias_own, g.bias_out.at[1 - dp], *g.s_bias, partner).wait()
    remote(g.gbs.at[1 - dp], g.gb_out.at[1 - dp], *g.s_gbx, partner).wait()
    remote(g.gas.at[1 - dp], g.ga_out.at[1 - dp], *g.s_gax, partner).wait()
    spread(g.block_own, g.block_out, *g.s_block, False)
    spread(g.grad_own, g.grad_out, *g.s_grad, False)


def on_device(
    latents, cond, ada_weight, ada_bias, qkv_weight, qv_bias, out_weight, out_bias,
    first_weight, first_bias, second_weight, second_bias, cotangent,
):
    dp, ctx, t, x, y, z, core = place()
    cond_slice = lax.dynamic_slice_in_dim(cond.astype(F32), t * 256, 256, 1)
    cond_act = jax.nn.silu(cond_slice).astype(BF16).astype(F32)
    empty = jnp.zeros((1, 256), F32)
    even = jnp.concatenate([cond_act[0:1], empty, cond_act[1:2], empty])
    odd = jnp.concatenate([empty, cond_act[0:1], empty, cond_act[1:2]])
    cond_block = jnp.pad(jnp.where(dp == 0, even, odd), ((0, 4), (0, 0)))
    ada_pad = jnp.pad(ada_weight[0], ((0, 0), (0, 64)))
    qkv_half = qkv_weight[0].reshape(32, 3, 2, 128).transpose(2, 0, 1, 3).reshape(2, 32, 384)
    out_half = out_weight[0].T.reshape(32, 2, 128).transpose(1, 0, 2)
    first_half = first_weight[0].reshape(32, 2, 512).transpose(1, 0, 2)
    second_half = second_weight[0].T.reshape(32, 2, 512).transpose(1, 0, 2)
    args = [
        latents, cotangent,
        jnp.concatenate([qkv_half, out_half], axis=2),
        jnp.concatenate([first_half, second_half], axis=2),
        cond_block, ada_pad, ada_bias,
        lax.dynamic_slice_in_dim(qv_bias[0].astype(F32), dp * 128, 128, 1),
        lax.dynamic_slice_in_dim(first_bias.astype(F32), dp * 512, 512, 1),
        out_bias, second_bias,
    ]
    outs = pl.pallas_call(
        block_kernel,
        out_shape=[shape(*one) for one in OUTPUTS.values()],
        in_specs=[VMEM] * len(args),
        out_specs=[VMEM] * len(OUTPUTS),
        scratch_shapes=[pltpu.VMEM(*one) for one in BUFFERS.values()]
        + [DMA(one) for one in SEMS.values() for _ in range(2)],
        compiler_params=pltpu.CompilerParams(
            collective_id=1, has_side_effects=True, vmem_limit_bytes=60 << 20
        ),
        name="block",
    )(*args)
    o = Refs()
    for name, out in zip(OUTPUTS, outs):
        setattr(o, name, out)
    sigmoid = jax.nn.sigmoid(cond_slice)
    sums = o.cond_out
    cond_mine = jnp.where(dp == 0, sums[0:3:2], sums[1:4:2])
    cond_grad = cond_mine * sigmoid * (1.0 + cond_slice * (1.0 - sigmoid))
    pair = o.bias_out[:, 2]
    ga, gb = o.ga_out, o.gb_out
    qkv_grad = ga[:, :, :384].reshape(2, 32, 3, 128).transpose(1, 2, 0, 3).reshape(1, 32, 3, 256)
    out_grad = ga[:, :, 384:].transpose(0, 2, 1).reshape(1, 256, 32)
    first_grad = gb[:, :, :512].transpose(1, 0, 2).reshape(1, 32, 1024)
    second_grad = gb[:, :, 512:].transpose(0, 2, 1).reshape(1, 1024, 32)
    return (
        o.block_out.reshape(2, 64, 1024),
        o.grad_out.reshape(2, 64, 1024),
        cond_grad,
        o.ada_out[None, :, :192],
        o.ada_bias_out,
        qkv_grad,
        pair[:, 512:768].reshape(2, 2, 128).transpose(1, 0, 2).reshape(1, 2, 256),
        out_grad,
        o.wide_out[0:1],
        first_grad,
        pair[:, :512].reshape(1, 1024),
        second_grad,
        o.wide_out[1:2],
    )


def solution(mesh):
    return jax.shard_map(
        on_device,
        mesh=mesh,
        in_specs=(
            P("dp", "context", None),
            P("dp", None),
            P(None, "tensor", ("dp", "context")),
            P(),
            P(None, ("dp", "context"), None, "tensor"),
            P(None, None, "tensor"),
            P(None, "tensor", ("dp", "context")),
            P(),
            P(None, ("dp", "context"), "tensor"),
            P(None, "tensor"),
            P(None, "tensor", ("dp", "context")),
            P(),
            P("dp", "context", None),
        ),
        out_specs=(
            P("dp", "context", None),
            P("dp", "context", None),
            P("dp", "tensor"),
            P(None, "tensor", ("dp", "context")),
            P(),
            P(None, ("dp", "context"), None, "tensor"),
            P(None, None, "tensor"),
            P(None, "tensor", ("dp", "context")),
            P(),
            P(None, ("dp", "context"), "tensor"),
            P(None, "tensor"),
            P(None, "tensor", ("dp", "context")),
            P(),
        ),
        check_vma=False,
    )
```

```python
import math

import jax
import jax.numpy as jnp
from jax import lax
from jax.experimental import pallas as pl
from jax.experimental.pallas import tpu as pltpu
from jax.sharding import PartitionSpec as P

EPSILON = 1e-06
F32 = jnp.float32
BF16 = jnp.bfloat16
MESH = pl.DeviceIdType.MESH
VMEM = pl.BlockSpec(memory_space=pltpu.VMEM)
DMA = pltpu.SemaphoreType.DMA


def place():
    dp = lax.axis_index("dp")
    ctx = lax.axis_index("context")
    t = lax.axis_index("tensor")
    return dp, ctx, t, (t // 2) * 2 + dp, ctx % 4, ctx // 4, t % 2


def device(x, y, z, core):
    return (x % 2, z * 4 + y, (x // 2) * 2 + core)


def remote(src, dst, send, recv, target):
    return pltpu.make_async_remote_copy(
        src_ref=src, dst_ref=dst, send_sem=send, recv_sem=recv,
        device_id=target, device_id_type=MESH,
    )


def greet(targets):
    barrier = pltpu.get_barrier_semaphore()
    count = 0
    for first, last, target in targets:
        def one(k, carry, target=target):
            pl.semaphore_signal(barrier, inc=1, device_id=target(k), device_id_type=MESH)
            return carry
        lax.fori_loop(first, last, one, 0)
        count += last - first
    pl.semaphore_wait(barrier, count)


def z_peer(k):
    dp, ctx, t, x, y, z, core = place()
    return (dp, ((z + k) % 4) * 4 + y, t)


def y_peer(k):
    dp, ctx, t, x, y, z, core = place()
    return (dp, z * 4 + (y + k) % 4, t)


def x_peer(k):
    dp, ctx, t, x, y, z, core = place()
    return device((x + k) % 4, y, z, core)


def sibling():
    dp, ctx, t, x, y, z, core = place()
    return device(x, y, z, 1 - core)


def ring_peer(k):
    dp, ctx, t, x, y, z, core = place()
    r = (x * 2 + core + k) % 8
    return device(r // 2, y, z, r % 2)


def gather_start(own, slots, mine, n, peer, send, recv):
    def one(k, carry):
        remote(own, slots.at[mine], send.at[k], recv.at[mine], peer(k)).start()
        return carry
    lax.fori_loop(1, n, one, 0)


def gather_wait(own, slots, mine, n, peer, send, recv):
    def one(k, carry):
        other = (mine + k) % n
        copy = remote(own, slots.at[other], send.at[k], recv.at[other], peer(k))
        copy.wait_recv()
        copy.wait_send()
        return carry
    lax.fori_loop(1, n, one, 0)


def scatter_start(parts, slots, mine, n, peer, send, recv):
    def one(k, carry):
        other = (mine + k) % n
        remote(parts.at[other], slots.at[mine], send.at[k], recv.at[mine], peer(k)).start()
        return carry
    lax.fori_loop(1, n, one, 0)


def scatter_wait(parts, slots, mine, n, peer, send, recv):
    def one(k, carry):
        other = (mine + k) % n
        copy = remote(parts.at[other], slots.at[other], send.at[k], recv.at[other], peer(k))
        copy.wait_recv()
        copy.wait_send()
        return carry
    lax.fori_loop(1, n, one, 0)


def shape(dims, dtype):
    return jax.ShapeDtypeStruct(dims, dtype)


def normalize(values):
    center = values - jnp.mean(values, axis=-1, keepdims=True)
    inverse = lax.rsqrt(jnp.mean(center * center, axis=-1, keepdims=True) + EPSILON)
    return center * inverse, inverse


def norm_back(grad_hat, normed, inverse):
    first = jnp.mean(grad_hat, axis=-1, keepdims=True)
    second = jnp.mean(grad_hat * normed, axis=-1, keepdims=True)
    return inverse * (grad_hat - first - normed * second)


def dot(left, right, contract, precision=None):
    return lax.dot_general(
        left, right, (contract, ((), ())), precision=precision, preferred_element_type=F32
    )


NN = ((1,), (0,))
NT = ((1,), (1,))
TN = ((0,), (0,))
SCALE = 1.0 / math.sqrt(64)
ROOT = math.sqrt(2.0 / math.pi)
STEPS = (1, 3, 2)


def from_back(k):
    y, z = lax.axis_index("context") % 4, lax.axis_index("context") // 4
    return (y + 4 - k) % 4, (z + 4 - k) % 4


def plane_one(full, h, send, recv, start):
    dp, ctx, t, x, y, z, core = place()
    mine = full.at[h, z, y]
    for k in STEPS:
        target = (dp, ((z + h * k) % 4) * 4 + (y + (1 - h) * k) % 4, t)
        if start:
            remote(mine, mine, send.at[h, k], recv.at[h, k], target).start()
        else:
            slot = full.at[h, (z + h * (4 - k)) % 4, (y + (1 - h) * (4 - k)) % 4]
            remote(mine, slot, send.at[h, k], recv.at[h, k], target).wait()


def plane_two(full, send, recv, start):
    dp, ctx, t, x, y, z, core = place()
    for k in STEPS:
        by, bz = from_back(k)
        row, column = full.at[0, z], full.at[1, :, y]
        if start:
            remote(row, row, send.at[0, k], recv.at[0, k], z_peer(k)).start()
            remote(column, column, send.at[1, k], recv.at[1, k], y_peer(k)).start()
        else:
            remote(row, full.at[0, bz], send.at[0, k], recv.at[0, k], z_peer(k)).wait()
            remote(column, full.at[1, :, by], send.at[1, k], recv.at[1, k], y_peer(k)).wait()


def reduce_one(parts, slots, send, recv, start):
    dp, ctx, t, x, y, z, core = place()
    for k in STEPS:
        by, bz = from_back(k)
        row, column = parts.at[0, (z + k) % 4], parts.at[1, :, (y + k) % 4]
        to_row = slots.at[0, z if start else bz]
        to_column = slots.at[1, y if start else by]
        for copy in (remote(row, to_row, send.at[0, k], recv.at[0, k], z_peer(k)),
                     remote(column, to_column, send.at[1, k], recv.at[1, k], y_peer(k))):
            copy.start() if start else copy.wait()
    if start:
        slots[0, z] = parts[0, z]
        slots[1, y] = parts[1, :, y]


def reduce_two(parts, slots, send, recv, start):
    dp, ctx, t, x, y, z, core = place()
    for k in STEPS:
        by, bz = from_back(k)
        to_y = slots.at[0, y if start else by]
        to_z = slots.at[1, z if start else bz]
        for copy in (remote(parts.at[0, (y + k) % 4], to_y, send.at[0, k], recv.at[0, k], y_peer(k)),
                     remote(parts.at[1, (z + k) % 4], to_z, send.at[1, k], recv.at[1, k], z_peer(k))):
            copy.start() if start else copy.wait()
    if start:
        slots[0, y] = parts[0, y]
        slots[1, z] = parts[1, z]


def add_slots(slots, out):
    for h in range(2):
        total = slots[h, 0].astype(F32)
        for k in range(1, 4):
            total = total + slots[h, k].astype(F32)
        out[h] = total.astype(out.dtype)


def tokens(src, dst, send, recv, start):
    dp, ctx, t, x, y, z, core = place()
    own = src.at[t // 2, pl.ds(pl.multiple_of(core * 32, 32), 32)]
    for other in range(4):
        same = jnp.logical_and(x == y, x == other)
        copy = remote(own, dst.at[y, core], send.at[other], recv.at[y], device(other, x, z, core))
        if start:
            @pl.when(jnp.logical_not(same))
            def _():
                copy.start()

            @pl.when(same)
            def _():
                pltpu.make_async_copy(own, dst.at[y, core], recv.at[y]).start()
        else:
            @pl.when(jnp.logical_not(same))
            def _():
                copy.wait_send()

            remote(own, dst.at[other, core], send.at[other], recv.at[other],
                   (1 - dp, ctx, t)).wait_recv()


def tokens_relay(dst, send, recv, start):
    dp, ctx, t, x, y, z, core = place()
    mine = dst.at[:, core]
    if start:
        remote(mine, mine, send, recv, sibling()).start()
    else:
        remote(mine, dst.at[:, 1 - core], send, recv, sibling()).wait()


def ring_gather(own, slots, send, recv, start):
    dp, ctx, t, x, y, z, core = place()
    if start:
        for k in (2, 1, 3):
            remote(own, slots.at[x, core], send.at[0, k], recv.at[0, k], x_peer(k)).start()
        remote(own, slots.at[x, core], send.at[1, 0], recv.at[1, 0], sibling()).start()
        slots[x, core] = own[...]
        return
    for k in STEPS:
        slot = slots.at[(x + 4 - k) % 4, core]
        remote(own, slot, send.at[0, k], recv.at[0, k], x_peer(k)).wait()
        remote(slot, slot, send.at[1, k], recv.at[1, k], sibling()).start()
    for k in (0,) + STEPS:
        slot = slots.at[(x + 4 - k) % 4, 1 - core]
        remote(slot, slot, send.at[1, k], recv.at[1, k], sibling()).wait()


def ring_scatter(parts, halves, mid, slots, send, recv, step):
    dp, ctx, t, x, y, z, core = place()
    order = (2, 1, 3, 0)
    if step == 0:
        for k in order:
            to = (x + k) % 4
            remote(parts.at[to, 1 - core], halves.at[to], send.at[0, k], recv.at[0, k],
                   sibling()).start()
    elif step == 1:
        for k in order:
            to = (x + k) % 4
            remote(parts.at[to, 1 - core], halves.at[to], send.at[0, k], recv.at[0, k],
                   sibling()).wait()
            both = parts[to, core].astype(F32) + halves[to].astype(F32)
            if k == 0:
                slots[x] = both.astype(BF16)
            else:
                mid[to] = both.astype(BF16)
                remote(mid.at[to], slots.at[x], send.at[1, k], recv.at[1, k], x_peer(k)).start()
    else:
        for k in STEPS:
            remote(mid.at[(x + k) % 4], slots.at[(x + 4 - k) % 4], send.at[1, k], recv.at[1, k],
                   x_peer(k)).wait()


def spread(src, dst, send, recv, start):
    dp, ctx, t, x, y, z, core = place()
    for k in range(4):
        x_hi, other = k // 2, k % 2
        x_to = 2 * x_hi + y % 2
        same = jnp.logical_and(jnp.logical_and(x_to == x, x == y), core == other)
        slot = dst.at[y // 2, core]
        recv_sem = recv.at[(y // 2) * 2 + core]
        copy = remote(src, slot, send.at[k], recv_sem, device(x_to, x, z, other))
        if start:
            @pl.when(jnp.logical_not(same))
            def _():
                copy.start()

            @pl.when(same)
            def _():
                pltpu.make_async_copy(src, slot, recv_sem).start()
        else:
            @pl.when(jnp.logical_not(same))
            def _():
                copy.wait_send()

            remote(src, dst.at[k // 2, k % 2], send.at[k], recv.at[k],
                   (1 - dp, ctx, t)).wait_recv()


def tokens_target(k):
    dp, ctx, t, x, y, z, core = place()
    return device(k, x, z, core)


def tokens_source(k):
    dp, ctx, t, x, y, z, core = place()
    return device(y, k, z, core)


def spread_target(k):
    dp, ctx, t, x, y, z, core = place()
    return device(2 * (k // 2) + y % 2, x, z, k % 2)


def spread_source(k):
    dp, ctx, t, x, y, z, core = place()
    return device(y, 2 * (k // 2) + dp, z, k % 2)


def ctx_peer(k):
    dp, ctx, t, x, y, z, core = place()
    return (dp, (ctx + k) % 16, t)


INPUTS = dict(lat=0, cond=1, ada=2, ada_bias=3, qkv=4, qv=5, wo=6, ob=7, w1=8, b1=9, w2=10, b2=11, cot=12)
OUTPUTS = dict(
    block_out=((2, 2, 32, 1024), BF16),
    grad_out=((2, 2, 32, 1024), BF16),
    cond_out=((2, 256), F32),
    ada_out=((192, 256), F32),
    ada_bias_out=((1, 6144), F32),
    ga_out=((2, 32, 512), F32),
    gb_out=((2, 32, 1024), F32),
    bias_out=((2, 1, 1024), F32),
    wide_out=((2, 1024), F32),
)
RING = ((4, 2, 32, 1024), BF16)
FOUR = ((4, 32, 1024), BF16)
BUFFERS = dict(
    xg=RING, cg=RING,
    packa=((2, 32, 512), BF16), packb=((2, 32, 1024), BF16),
    wa=((2, 4, 4, 32, 512), BF16), wb=((2, 4, 4, 32, 1024), BF16),
    cond_a=((8, 256), F32), cond_b=((8, 256), F32), cond8=((8, 256), F32),
    part=((4, 256), F32), parts=((8, 4, 256), F32), pair=((4, 2, 256), F32),
    modg=((16, 2, 256), F32), flat=((1, 6144), F32),
    normed=((256, 1024), F32), hidden=((256, 1024), BF16),
    k_own=((256, 128), BF16), kg=((4, 256, 128), BF16),
    v_own=((256, 128), BF16), vg=((4, 256, 128), BF16), prob=((2, 256, 1024), F32),
    branch_part=RING, branch_half=FOUR, branch_mid=FOUR, branch_slots=FOUR,
    h2_own=((32, 1024), BF16), h2=RING,
    d_feed=((256, 1024), BF16), d_act=((256, 512), F32),
    dh2_part=RING, dh2_half=FOUR, dh2_mid=FOUR, dh2_slots=FOUR,
    feed_part=RING, feed_half=FOUR, feed_mid=FOUR, feed_slots=FOUR,
    db_own=((32, 1024), BF16), db=RING,
    block_own=((32, 1024), BF16), d_middle=((32, 1024), F32),
    dk_part=((4, 256, 128), BF16), dk_slots=((4, 256, 128), BF16),
    dv_part=((4, 256, 128), BF16), dv_slots=((4, 256, 128), BF16),
    dh_part=RING, dh_half=FOUR, dh_mid=FOUR, dh_slots=FOUR,
    grad_own=((32, 1024), BF16),
    m_own=((4, 1024), F32), m_slots=((8, 4, 1024), F32),
    z_own=((8, 1024), F32), z_slots=((4, 8, 1024), F32),
    y_own=((8, 1024), F32), y_slots=((4, 8, 1024), F32),
    n_own=((2, 1024), F32), n_slots=((8, 2, 1024), F32),
    l_own=((4, 1024), F32), l_slots=((16, 4, 1024), F32),
    dm=((8, 6144), F32), bias_own=((1, 1024), F32),
    cond_part=((8, 256), F32), cond_slots=((16, 8, 256), F32), cond_sum=((8, 256), F32),
    cond_other=((8, 256), F32),
    ga=((2, 4, 4, 32, 512), BF16), ga1=((2, 4, 4, 32, 512), BF16),
    ga2=((2, 4, 32, 512), BF16), ga3=((2, 4, 32, 512), BF16), gas=((2, 32, 512), F32),
    gb=((2, 4, 4, 32, 1024), BF16), gb1=((2, 4, 4, 32, 1024), BF16),
    gb2=((2, 4, 32, 1024), BF16), gb3=((2, 4, 32, 1024), BF16), gbs=((2, 32, 1024), F32),
)
SEMS = dict(
    s_cond=(), s_xa=(), s_xb=(), s_xg=(4,), s_xr=(), s_cg=(4,), s_cr=(),
    s_wa1=(2, 4), s_wa2=(2, 4), s_wb1=(2, 4), s_wb2=(2, 4),
    s_mod=(8,), s_mod2=(16,), s_k=(4,), s_v=(4,),
    s_branch=(2, 4), s_h2=(2, 4), s_dh2=(2, 4), s_feed=(2, 4), s_db=(2, 4),
    s_block=(4,), s_dk=(4,), s_dv=(4,), s_dh=(2, 4), s_grad=(4,),
    s_m=(8,), s_z=(4,), s_y=(4,), s_n=(8,), s_l=(16,), s_bias=(), s_c=(16,), s_cx=(),
    s_ga1=(2, 4), s_ga2=(2, 4), s_gb1=(2, 4), s_gb2=(2, 4), s_gax=(), s_gbx=(),
)


class Refs:
    pass


def block_kernel(*refs):
    g = Refs()
    names = list(INPUTS) + list(OUTPUTS) + list(BUFFERS)
    for name, ref in zip(names, refs):
        setattr(g, name, ref)
    sems = refs[len(names):]
    for i, name in enumerate(SEMS):
        setattr(g, name, (sems[2 * i], sems[2 * i + 1]))
    dp, ctx, t, x, y, z, core = place()
    r = x * 2 + core
    partner = (1 - dp, ctx, t)

    greet([(1, 8, ring_peer), (1, 16, ctx_peer)] + [(0, 4, f) for f in (
        tokens_target, tokens_source, spread_target, spread_source)])

    cond_slice = g.cond[:, pl.ds(pl.multiple_of(t * 256, 256), 256)].astype(F32)
    sigmoid = 1.0 / (1.0 + jnp.exp(-cond_slice))
    cond_act = (cond_slice * sigmoid).astype(BF16).astype(F32)
    rows = lax.broadcasted_iota(jnp.int32, (8, 256), 0)
    g.cond_a[...] = jnp.where(rows == dp, cond_act[0:1], jnp.where(rows == dp + 2, cond_act[1:2], 0.0))
    cond_copy = remote(g.cond_a, g.cond_b, *g.s_cond, partner)
    cond_copy.start()
    tokens(g.lat, g.xg, *g.s_xg, True)
    for h in range(2):
        for k in range(3):
            g.packa[h, :, 128 * k:128 * k + 128] = g.qkv[k, :, 128 * h:128 * h + 128]
        g.packa[h, :, 384:] = g.wo[:, 128 * h:128 * h + 128]
    across_a = remote(g.packa.at[1 - dp], g.wa.at[dp, z, y], *g.s_xa, partner)
    across_a.start()
    g.wa[dp, z, y] = g.packa[dp]
    plane_one(g.wa, dp, *g.s_wa1, True)
    cond_copy.wait()
    g.cond8[...] = g.cond_a[...] + g.cond_b[...]
    g.part[:, :192] = dot(g.cond8[...].astype(BF16), g.ada[...], NT)[:4]
    gather_start(g.part, g.parts, r, 8, ring_peer, *g.s_mod)
    g.parts[r] = g.part[...]
    for h in range(2):
        g.packb[h, :, :512] = g.w1[0, :, 512 * h:512 * h + 512]
        g.packb[h, :, 512:] = g.w2[:, 512 * h:512 * h + 512]
    across_b = remote(g.packb.at[1 - dp], g.wb.at[dp, z, y], *g.s_xb, partner)
    across_b.start()
    g.wb[dp, z, y] = g.packb[dp]
    remote(g.packa.at[1 - dp], g.wa.at[1 - dp, z, y], *g.s_xa, partner).wait()
    plane_one(g.wa, 1 - dp, *g.s_wa1, True)
    gather_wait(g.part, g.parts, r, 8, ring_peer, *g.s_mod)
    for c in range(2):
        both = (g.parts[2 * c] + g.parts[2 * c + 1]) + (g.parts[2 * c + 4] + g.parts[2 * c + 5])
        for i in range(4):
            g.pair[i, c:c + 1, :192] = both[i:i + 1, :192]

    def mod_start(k, carry):
        remote(g.pair.at[(ctx + k) % 4], g.modg.at[ctx], g.s_mod2[0].at[k], g.s_mod2[1].at[ctx],
               ctx_peer(k)).start()
        return carry
    lax.fori_loop(1, 16, mod_start, 0)
    g.modg[ctx] = g.pair[y]
    tokens(g.lat, g.xg, *g.s_xg, False)
    tokens_relay(g.xg, *g.s_xr, True)
    plane_one(g.wa, dp, *g.s_wa1, False)
    plane_one(g.wa, 1 - dp, *g.s_wa1, False)
    plane_two(g.wa, *g.s_wa2, True)
    tokens_relay(g.xg, *g.s_xr, False)
    normed, _ = normalize(g.xg[...].astype(F32).reshape(256, 1024))
    g.normed[...] = normed
    plane_one(g.wb, dp, *g.s_wb1, True)
    remote(g.packb.at[1 - dp], g.wb.at[1 - dp, z, y], *g.s_xb, partner).wait()
    plane_one(g.wb, 1 - dp, *g.s_wb1, True)
    tokens(g.cot, g.cg, *g.s_cg, True)

    def mod_wait(k, carry):
        other = (ctx + k) % 16
        remote(g.pair.at[0], g.modg.at[other], g.s_mod2[0].at[k], g.s_mod2[1].at[other],
               ctx_peer(k)).wait()
        return carry
    lax.fori_loop(1, 16, mod_wait, 0)
    for p in range(16):
        c, first = p // 8, (2 * p) % 16
        both = jnp.concatenate(
            [g.modg[first, c:c + 1, :192], g.modg[first + 1, c:c + 1, :192]], axis=1)
        g.flat[:, 384 * p:384 * p + 384] = both + g.ada_bias[:, 384 * p:384 * p + 384].astype(F32)
    shift1, scale1, gate1, shift2, scale2, gate2 = [
        g.flat[:, k * 1024:(k + 1) * 1024] for k in range(6)]
    hidden = (g.normed[...] * (1.0 + scale1) + shift1).astype(BF16)
    g.hidden[...] = hidden
    plane_two(g.wa, *g.s_wa2, False)
    mixed = dot(hidden, g.wa[:, :, :, :, :384].reshape(1024, 384), NN)
    qv = g.qv[0, :, pl.ds(pl.multiple_of(dp * 128, 128), 128)].astype(F32)
    g.k_own[...] = mixed[:, 128:256].astype(BF16)
    gather_start(g.k_own, g.kg, z, 4, z_peer, *g.s_k)
    g.v_own[...] = (mixed[:, 256:] + qv[1:2]).astype(BF16)
    gather_start(g.v_own, g.vg, z, 4, z_peer, *g.s_v)
    query = (mixed[:, :128] + qv[0:1]).astype(BF16)
    g.kg[z] = g.k_own[...]
    g.vg[z] = g.v_own[...]
    plane_one(g.wb, dp, *g.s_wb1, False)
    plane_one(g.wb, 1 - dp, *g.s_wb1, False)
    plane_two(g.wb, *g.s_wb2, True)
    gather_wait(g.k_own, g.kg, z, 4, z_peer, *g.s_k)
    for h in range(2):
        key = g.kg[:, :, 64 * h:64 * h + 64].reshape(1024, 64)
        scores = dot(query[:, 64 * h:64 * h + 64], key, NT) * SCALE
        expo = jnp.exp(scores - jnp.max(scores, axis=-1, keepdims=True))
        g.prob[h] = expo / jnp.sum(expo, axis=-1, keepdims=True)
    gather_wait(g.v_own, g.vg, z, 4, z_peer, *g.s_v)
    heads = []
    for h in range(2):
        value = g.vg[:, :, 64 * h:64 * h + 64].reshape(1024, 64)
        heads.append(dot(g.prob[h].astype(BF16), value, NN))
    attended = jnp.concatenate(heads, axis=1).astype(BF16)
    w_out = g.wa[:, :, :, :, 384:].reshape(1024, 128)
    g.branch_part[...] = dot(attended, w_out, NT).astype(BF16).reshape(4, 2, 32, 1024)
    branch_ring = (g.branch_part, g.branch_half, g.branch_mid, g.branch_slots, *g.s_branch)
    ring_scatter(*branch_ring, 0)
    ring_scatter(*branch_ring, 1)
    tokens(g.cot, g.cg, *g.s_cg, False)
    tokens_relay(g.cg, *g.s_cr, True)
    tokens_relay(g.cg, *g.s_cr, False)
    d_feed = (g.cg[...].astype(F32).reshape(256, 1024) * gate2).astype(BF16)
    g.d_feed[...] = d_feed
    plane_two(g.wb, *g.s_wb2, False)
    w_second = g.wb[:, :, :, :, 512:].reshape(1024, 512)
    g.d_act[...] = dot(d_feed, w_second, NN)
    g.z_own[...] = jnp.zeros_like(g.z_own)
    g.z_own[5:6] = jnp.sum(d_feed.astype(F32), axis=0, keepdims=True)
    ring_scatter(*branch_ring, 2)

    x_own = g.xg[x, core].astype(F32)
    branch = jnp.sum(g.branch_slots[...].astype(F32), axis=0) + g.ob[...].astype(F32)
    middle = x_own + gate1 * branch
    normed_two, inverse_two = normalize(middle)
    g.h2_own[...] = (normed_two * (1.0 + scale2) + shift2).astype(BF16)
    ring_gather(g.h2_own, g.h2, *g.s_h2, True)
    ring_gather(g.h2_own, g.h2, *g.s_h2, False)

    hidden_two = g.h2[...].reshape(256, 1024)
    w_first = g.wb[:, :, :, :, :512].reshape(1024, 512)
    bias_first = g.b1[:, pl.ds(pl.multiple_of(dp * 512, 512), 512)].astype(F32)
    before = dot(hidden_two, w_first, NN) + bias_first
    square = before * before
    tanh = jnp.tanh(ROOT * before * (1.0 + 0.044715 * square))
    slope = 0.5 * (1.0 + tanh) + (0.5 * ROOT) * before * (1.0 - tanh * tanh) * (
        1.0 + (3.0 * 0.044715) * square)
    d_before = (g.d_act[...] * slope).astype(BF16)
    g.dh2_part[...] = dot(d_before, w_first, NT).astype(BF16).reshape(4, 2, 32, 1024)
    dh2_ring = (g.dh2_part, g.dh2_half, g.dh2_mid, g.dh2_slots, *g.s_dh2)
    ring_scatter(*dh2_ring, 0)
    activated = (0.5 * before * (1.0 + tanh)).astype(BF16)
    ring_scatter(*dh2_ring, 1)
    g.feed_part[...] = dot(activated, w_second, NT).astype(BF16).reshape(4, 2, 32, 1024)
    g.gb[:, :, :, :, :512] = dot(hidden_two, d_before, TN).astype(BF16).reshape(2, 4, 4, 32, 512)
    g.gb[:, :, :, :, 512:] = dot(d_feed, activated, TN).astype(BF16).reshape(2, 4, 4, 32, 512)
    reduce_one(g.gb, g.gb1, *g.s_gb1, True)
    g.z_own[6:7, :512] = jnp.sum(d_before.astype(F32), axis=0, keepdims=True)
    ring_scatter(*dh2_ring, 2)

    cot_own = g.cg[x, core].astype(F32)
    d_hidden = jnp.sum(g.dh2_slots[...].astype(F32), axis=0)
    d_middle = cot_own + norm_back(d_hidden * (1.0 + scale2), normed_two, inverse_two)
    g.d_middle[...] = d_middle
    g.db_own[...] = (d_middle * gate1).astype(BF16)
    ring_gather(g.db_own, g.db, *g.s_db, True)
    feed_ring = (g.feed_part, g.feed_half, g.feed_mid, g.feed_slots, *g.s_feed)
    ring_scatter(*feed_ring, 0)
    g.m_own[0:1] = jnp.sum(d_middle * branch, axis=0, keepdims=True)
    g.m_own[1:2] = jnp.sum(d_hidden, axis=0, keepdims=True)
    g.m_own[2:3] = jnp.sum(d_hidden * normed_two, axis=0, keepdims=True)
    ring_gather(g.db_own, g.db, *g.s_db, False)
    ring_scatter(*feed_ring, 1)

    d_branch = g.db[...].reshape(256, 1024)
    d_attended = dot(d_branch, w_out, NN).astype(BF16)
    d_one = [d_attended[:, 64 * h:64 * h + 64] for h in range(2)]
    d_value = [dot(g.prob[h].astype(BF16), d_one[h], TN) for h in range(2)]
    g.dv_part[...] = jnp.concatenate(d_value, axis=1).astype(BF16).reshape(4, 256, 128)
    scatter_start(g.dv_part, g.dv_slots, z, 4, z_peer, *g.s_dv)
    g.dv_slots[z] = g.dv_part[z]
    d_query, d_key = [], []
    for h in range(2):
        key = g.kg[:, :, 64 * h:64 * h + 64].reshape(1024, 64)
        value = g.vg[:, :, 64 * h:64 * h + 64].reshape(1024, 64)
        prob = g.prob[h]
        d_prob = dot(d_one[h], value, NT)
        d_scores = (prob * (d_prob - jnp.sum(prob * d_prob, axis=-1, keepdims=True))).astype(BF16)
        d_key.append(dot(d_scores, query[:, 64 * h:64 * h + 64], TN) * SCALE)
        d_query.append(dot(d_scores, key, NN) * SCALE)
    g.dk_part[...] = jnp.concatenate(d_key, axis=1).astype(BF16).reshape(4, 256, 128)
    scatter_start(g.dk_part, g.dk_slots, z, 4, z_peer, *g.s_dk)
    g.dk_slots[z] = g.dk_part[z]
    d_query = jnp.concatenate(d_query, axis=1).astype(BF16)
    ring_scatter(*feed_ring, 2)
    feed = jnp.sum(g.feed_slots[...].astype(F32), axis=0) + g.b2[...].astype(F32)
    g.block_own[...] = (middle + gate2 * feed).astype(BF16)
    spread(g.block_own, g.block_out, *g.s_block, True)
    g.m_own[3:4] = jnp.sum(cot_own * feed, axis=0, keepdims=True)
    gather_start(g.m_own, g.m_slots, r, 8, ring_peer, *g.s_m)
    g.m_slots[r] = g.m_own[...]
    g.ga[:, :, :, :, 384:] = dot(d_branch, attended, TN).astype(BF16).reshape(2, 4, 4, 32, 128)
    g.z_own[4:5] = jnp.sum(d_branch.astype(F32), axis=0, keepdims=True)
    g.z_own[6:7, 512:640] = jnp.sum(d_query.astype(F32), axis=0, keepdims=True)
    reduce_one(g.gb, g.gb1, *g.s_gb1, False)
    add_slots(g.gb1, g.gb2)
    scatter_wait(g.dv_part, g.dv_slots, z, 4, z_peer, *g.s_dv)
    scatter_wait(g.dk_part, g.dk_slots, z, 4, z_peer, *g.s_dk)
    reduce_two(g.gb2, g.gb3, *g.s_gb2, True)

    d_keys = jnp.sum(g.dk_slots[...].astype(F32), axis=0).astype(BF16)
    d_values = jnp.sum(g.dv_slots[...].astype(F32), axis=0).astype(BF16)
    d_qkv = jnp.concatenate([d_query, d_keys, d_values], axis=1)
    d_part = dot(d_qkv, g.wa[:, :, :, :, :384].reshape(1024, 384), NT)
    g.dh_part[...] = d_part.astype(BF16).reshape(4, 2, 32, 1024)
    dh_ring = (g.dh_part, g.dh_half, g.dh_mid, g.dh_slots, *g.s_dh)
    ring_scatter(*dh_ring, 0)
    g.n_own[0:1] = jnp.sum(d_part, axis=0, keepdims=True)
    g.n_own[1:2] = jnp.sum(d_part * g.normed[...], axis=0, keepdims=True)
    ring_scatter(*dh_ring, 1)
    gather_start(g.n_own, g.n_slots, r, 8, ring_peer, *g.s_n)
    g.n_slots[r] = g.n_own[...]
    g.ga[:, :, :, :, :384] = dot(g.hidden[...], d_qkv, TN).astype(BF16).reshape(2, 4, 4, 32, 384)
    reduce_one(g.ga, g.ga1, *g.s_ga1, True)
    gather_wait(g.m_own, g.m_slots, r, 8, ring_peer, *g.s_m)
    g.z_own[0:4] = jnp.sum(g.m_slots[...], axis=0)
    gather_start(g.z_own, g.z_slots, z, 4, z_peer, *g.s_z)
    g.z_slots[z] = g.z_own[...]
    gather_wait(g.n_own, g.n_slots, r, 8, ring_peer, *g.s_n)
    g.l_own[0:2] = jnp.sum(g.n_slots[...], axis=0)
    g.l_own[2:4] = jnp.zeros((2, 1024), F32)
    g.l_own[2:3, :128] = jnp.sum(d_values.astype(F32), axis=0, keepdims=True)
    gather_start(g.l_own, g.l_slots, ctx, 16, ctx_peer, *g.s_l)
    g.l_slots[ctx] = g.l_own[...]
    ring_scatter(*dh_ring, 2)

    x_normed, x_inverse = normalize(x_own)
    d_hidden = jnp.sum(g.dh_slots[...].astype(F32), axis=0)
    grad = g.d_middle[...] + norm_back(d_hidden * (1.0 + scale1), x_normed, x_inverse)
    g.grad_own[...] = grad.astype(BF16)
    spread(g.grad_own, g.grad_out, *g.s_grad, True)
    gather_wait(g.z_own, g.z_slots, z, 4, z_peer, *g.s_z)
    g.y_own[...] = jnp.sum(g.z_slots[...], axis=0)
    gather_start(g.y_own, g.y_slots, y, 4, y_peer, *g.s_y)
    g.y_slots[y] = g.y_own[...]
    reduce_two(g.gb2, g.gb3, *g.s_gb2, False)
    add_slots(g.gb3, g.gbs)
    remote(g.gbs.at[1 - dp], g.gb_out.at[dp], *g.s_gbx, partner).start()
    g.gb_out[dp] = g.gbs[dp]
    reduce_one(g.ga, g.ga1, *g.s_ga1, False)
    add_slots(g.ga1, g.ga2)
    reduce_two(g.ga2, g.ga3, *g.s_ga2, True)
    gather_wait(g.l_own, g.l_slots, ctx, 16, ctx_peer, *g.s_l)
    gather_wait(g.y_own, g.y_slots, y, 4, y_peer, *g.s_y)

    late = jnp.sum(g.l_slots[...].reshape(4, 4, 4, 1024), axis=0)
    early = jnp.sum(g.y_slots[...], axis=0)
    g.wide_out[...] = early[4:6]
    g.bias_own[:, :640] = early[6:7, :640]
    g.bias_own[:, 640:768] = jnp.sum(late[:, 2], axis=0, keepdims=True)[:, :128]
    g.bias_own[:, 768:] = jnp.zeros((1, 256), F32)
    remote(g.bias_own, g.bias_out.at[dp], *g.s_bias, partner).start()
    g.bias_out[dp] = g.bias_own[...]
    g.dm[...] = jnp.zeros_like(g.dm)
    for k in range(6):
        for i in range(4):
            row = late[i, k:k + 1] if k < 2 else g.y_slots[i, k - 2:k - 1]
            g.dm[i:i + 1, k * 1024:(k + 1) * 1024] = row
    g.ada_bias_out[...] = jnp.sum(g.dm[...], axis=0, keepdims=True)
    chunk = dp * 16 + ctx
    columns = g.dm[:, pl.ds(pl.multiple_of(((3 * chunk) // 2) * 128, 128), 256)]
    columns = jnp.where(chunk % 2 == 1, pltpu.roll(columns, 192, 1), columns)[:, :192]
    g.cond_part[...] = dot(columns, g.ada[...].astype(F32), NN, lax.Precision.HIGHEST)
    gather_start(g.cond_part, g.cond_slots, ctx, 16, ctx_peer, *g.s_c)
    g.cond_slots[ctx] = g.cond_part[...]
    g.ada_out[...] = dot(columns, g.cond8[...], TN, lax.Precision.HIGHEST)
    gather_wait(g.cond_part, g.cond_slots, ctx, 16, ctx_peer, *g.s_c)
    g.cond_sum[...] = jnp.sum(g.cond_slots[...], axis=0)
    cond_copy = remote(g.cond_sum, g.cond_other, *g.s_cx, partner)
    cond_copy.start()
    reduce_two(g.ga2, g.ga3, *g.s_ga2, False)
    add_slots(g.ga3, g.gas)
    remote(g.gas.at[1 - dp], g.ga_out.at[dp], *g.s_gax, partner).start()
    g.ga_out[dp] = g.gas[dp]
    cond_copy.wait()
    g.cond_part[...] = g.cond_sum[...] + g.cond_other[...]
    slope = sigmoid * (1.0 + cond_slice * (1.0 - sigmoid))
    for i in range(2):
        g.cond_out[i:i + 1] = g.cond_part[pl.ds(2 * i + dp, 1)] * slope[i:i + 1]
    remote(g.bias_own, g.bias_out.at[1 - dp], *g.s_bias, partner).wait()
    remote(g.gbs.at[1 - dp], g.gb_out.at[1 - dp], *g.s_gbx, partner).wait()
    remote(g.gas.at[1 - dp], g.ga_out.at[1 - dp], *g.s_gax, partner).wait()
    spread(g.block_own, g.block_out, *g.s_block, False)
    spread(g.grad_own, g.grad_out, *g.s_grad, False)


def unpack_kernel(block, grad, cond, ada, ada_bias, ga, gb, bias, wide,
                  block_out, grad_out, cond_out, ada_out, ada_bias_out, qkv_out, qv_out,
                  wo_out, ob_out, w1_out, b1_out, w2_out, b2_out):
    block_out[...] = block[...].reshape(2, 64, 1024)
    grad_out[...] = grad[...].astype(F32).reshape(2, 64, 1024)
    cond_out[...] = cond[...]
    ada_out[...] = ada[...]
    ada_bias_out[...] = ada_bias[...]
    for h in range(2):
        for k in range(3):
            qkv_out[k, :, 128 * h:128 * h + 128] = ga[h, :, 128 * k:128 * k + 128]
        for k in range(2):
            qv_out[0, k:k + 1, 128 * h:128 * h + 128] = bias[h, :, 512 + 128 * k:640 + 128 * k]
        wo_out[:, 128 * h:128 * h + 128] = ga[h, :, 384:]
        w1_out[0, :, 512 * h:512 * h + 512] = gb[h, :, :512]
        w2_out[:, 512 * h:512 * h + 512] = gb[h, :, 512:]
        b1_out[:, 512 * h:512 * h + 512] = bias[h, :, :512]
    ob_out[...] = wide[0:1]
    b2_out[...] = wide[1:2]


def on_device(
    latents, cond, ada_weight, ada_bias, qkv_weight, qv_bias, out_weight, out_bias,
    first_weight, first_bias, second_weight, second_bias, cotangent,
):
    args = [
        latents, cond, ada_weight[0].T, ada_bias, qkv_weight[0].transpose(1, 0, 2), qv_bias,
        out_weight[0].T, out_bias, first_weight, first_bias, second_weight[0].T, second_bias,
        cotangent,
    ]
    outs = pl.pallas_call(
        block_kernel,
        out_shape=[shape(*one) for one in OUTPUTS.values()],
        in_specs=[VMEM] * len(args),
        out_specs=[VMEM] * len(OUTPUTS),
        scratch_shapes=[pltpu.VMEM(*one) for one in BUFFERS.values()]
        + [DMA(one) for one in SEMS.values() for _ in range(2)],
        compiler_params=pltpu.CompilerParams(
            collective_id=1, has_side_effects=True, vmem_limit_bytes=56 << 20
        ),
        name="block",
    )(*args)
    final = [
        shape((2, 64, 1024), BF16), shape((2, 64, 1024), F32), shape((2, 256), F32),
        shape((192, 256), F32), shape((1, 6144), F32), shape((3, 32, 256), F32),
        shape((1, 2, 256), F32), shape((32, 256), F32), shape((1, 1024), F32),
        shape((1, 32, 1024), F32), shape((1, 1024), F32), shape((32, 1024), F32),
        shape((1, 1024), F32),
    ]
    results = pl.pallas_call(
        unpack_kernel, out_shape=final, in_specs=[VMEM] * len(outs), out_specs=[VMEM] * len(final),
        name="unpack",
    )(*outs)
    results = list(results)
    for k in (3, 7, 11):
        results[k] = results[k].T[None]
    results[5] = results[5].transpose(1, 0, 2)[None]
    return tuple(results)


def solution(mesh):
    return jax.shard_map(
        on_device,
        mesh=mesh,
        in_specs=(
            P("dp", "context", None),
            P("dp", None),
            P(None, "tensor", ("dp", "context")),
            P(),
            P(None, ("dp", "context"), None, "tensor"),
            P(None, None, "tensor"),
            P(None, "tensor", ("dp", "context")),
            P(),
            P(None, ("dp", "context"), "tensor"),
            P(None, "tensor"),
            P(None, "tensor", ("dp", "context")),
            P(),
            P("dp", "context", None),
        ),
        out_specs=(
            P("dp", "context", None),
            P("dp", "context", None),
            P("dp", "tensor"),
            P(None, "tensor", ("dp", "context")),
            P(),
            P(None, ("dp", "context"), None, "tensor"),
            P(None, None, "tensor"),
            P(None, "tensor", ("dp", "context")),
            P(),
            P(None, ("dp", "context"), "tensor"),
            P(None, "tensor"),
            P(None, "tensor", ("dp", "context")),
            P(),
        ),
        check_vma=False,
    )
```

```python
import math

import jax
import jax.numpy as jnp
from jax import lax
from jax.experimental import pallas as pl
from jax.experimental.pallas import tpu as pltpu
from jax.sharding import PartitionSpec as P

EPSILON = 1e-06
F32 = jnp.float32
BF16 = jnp.bfloat16
MESH = pl.DeviceIdType.MESH
VMEM = pl.BlockSpec(memory_space=pltpu.VMEM)
DMA = pltpu.SemaphoreType.DMA


def mod(a, b):
    return a % b if isinstance(a, int) else lax.rem(a, jnp.int32(b))


def div(a, b):
    return a // b if isinstance(a, int) else lax.div(a, jnp.int32(b))


def place():
    dp = lax.axis_index("dp")
    ctx = lax.axis_index("context")
    t = lax.axis_index("tensor")
    return dp, ctx, t, div(t, 2) * 2 + dp, mod(ctx, 4), div(ctx, 4), mod(t, 2)


def loop(first, last, one):
    for k in range(first, last):
        one(k, 0)


def device(x, y, z, core):
    return (mod(x, 2), z * 4 + y, div(x, 2) * 2 + core)


def remote(src, dst, send, recv, target):
    return pltpu.make_async_remote_copy(
        src_ref=src, dst_ref=dst, send_sem=send, recv_sem=recv,
        device_id=target, device_id_type=MESH,
    )


def greet(targets):
    barrier = pltpu.get_barrier_semaphore()
    count = 0
    for first, last, target in targets:
        def one(k, carry, target=target):
            pl.semaphore_signal(barrier, inc=1, device_id=target(k), device_id_type=MESH)
            return carry
        loop(first, last, one)
        count += last - first
    pl.semaphore_wait(barrier, count)


def z_peer(k):
    dp, ctx, t, x, y, z, core = place()
    return (dp, mod(z + k, 4) * 4 + y, t)


def y_peer(k):
    dp, ctx, t, x, y, z, core = place()
    return (dp, z * 4 + mod(y + k, 4), t)


def x_peer(k):
    dp, ctx, t, x, y, z, core = place()
    return device(mod(x + k, 4), y, z, core)


def sibling():
    dp, ctx, t, x, y, z, core = place()
    return device(x, y, z, 1 - core)


def ring_peer(k):
    dp, ctx, t, x, y, z, core = place()
    r = mod(x * 2 + core + k, 8)
    return device(div(r, 2), y, z, mod(r, 2))


def gather_start(own, slots, mine, n, peer, send, recv):
    def one(k, carry):
        remote(own, slots.at[mine], send.at[k], recv.at[mine], peer(k)).start()
        return carry
    loop(1, n, one)


def gather_wait(own, slots, mine, n, peer, send, recv):
    def one(k, carry):
        other = mod(mine + k, n)
        copy = remote(own, slots.at[other], send.at[k], recv.at[other], peer(k))
        copy.wait_recv()
        copy.wait_send()
        return carry
    loop(1, n, one)


def scatter_start(parts, slots, mine, n, peer, send, recv):
    def one(k, carry):
        other = mod(mine + k, n)
        remote(parts.at[other], slots.at[mine], send.at[k], recv.at[mine], peer(k)).start()
        return carry
    loop(1, n, one)


def scatter_wait(parts, slots, mine, n, peer, send, recv):
    def one(k, carry):
        other = mod(mine + k, n)
        copy = remote(parts.at[other], slots.at[other], send.at[k], recv.at[other], peer(k))
        copy.wait_recv()
        copy.wait_send()
        return carry
    loop(1, n, one)


def shape(dims, dtype):
    return jax.ShapeDtypeStruct(dims, dtype)


def normalize(values):
    center = values - jnp.mean(values, axis=-1, keepdims=True)
    inverse = lax.rsqrt(jnp.mean(center * center, axis=-1, keepdims=True) + EPSILON)
    return center * inverse, inverse


def norm_back(grad_hat, normed, inverse):
    first = jnp.mean(grad_hat, axis=-1, keepdims=True)
    second = jnp.mean(grad_hat * normed, axis=-1, keepdims=True)
    return inverse * (grad_hat - first - normed * second)


def dot(left, right, contract, precision=None):
    return lax.dot_general(
        left, right, (contract, ((), ())), precision=precision, preferred_element_type=F32
    )


def dot_split(left, right):
    high = left.astype(BF16)
    rest = left - high.astype(F32)
    middle = rest.astype(BF16)
    low = (rest - middle.astype(F32)).astype(BF16)
    out = dot(jnp.concatenate([high, middle, low], axis=0), right, NN)
    n = left.shape[0]
    return out[:n] + (out[n:2 * n] + out[2 * n:])


NN = ((1,), (0,))
NT = ((1,), (1,))
TN = ((0,), (0,))
SCALE = 1.0 / math.sqrt(64)
ROOT = math.sqrt(2.0 / math.pi)
STEPS = (1, 3, 2)


def from_back(k):
    y, z = mod(lax.axis_index("context"), 4), div(lax.axis_index("context"), 4)
    return mod(y + 4 - k, 4), mod(z + 4 - k, 4)


def line_target(to, h, k):
    dp, ctx, t, x, y, z, core = place()
    return (to, mod(z + h * k, 4) * 4 + mod(y + (1 - h) * k, 4), t)


def cross_y(k):
    return line_target(1 - lax.axis_index("dp"), 0, k)


def cross_z(k):
    return line_target(1 - lax.axis_index("dp"), 1, k)


def plane_one(full, pack, send, recv, start):
    dp, ctx, t, x, y, z, core = place()
    for side, order in ((0, STEPS), (1, (2, 1, 3, 0))):
        to = dp if side == 0 else 1 - dp
        for k in order:
            target = line_target(to, dp, k)
            if start:
                remote(pack.at[to], full.at[dp, z, y], send.at[side, k], recv.at[side, k],
                       target).start()
            else:
                slot = full.at[to, mod(z + to * (4 - k), 4), mod(y + (1 - to) * (4 - k), 4)]
                remote(pack.at[to], slot, send.at[side, k], recv.at[side, k], target).wait()
    if start:
        full[dp, z, y] = pack[dp]


def plane_two(full, send, recv, start):
    dp, ctx, t, x, y, z, core = place()
    for k in STEPS:
        by, bz = from_back(k)
        row, column = full.at[0, z], full.at[1, :, y]
        if start:
            remote(row, row, send.at[0, k], recv.at[0, k], z_peer(k)).start()
            remote(column, column, send.at[1, k], recv.at[1, k], y_peer(k)).start()
        else:
            remote(row, full.at[0, bz], send.at[0, k], recv.at[0, k], z_peer(k)).wait()
            remote(column, full.at[1, :, by], send.at[1, k], recv.at[1, k], y_peer(k)).wait()


def reduce_one(parts, slots, send, recv, start):
    dp, ctx, t, x, y, z, core = place()
    for k in STEPS:
        by, bz = from_back(k)
        row, column = parts.at[0, mod(z + k, 4)], parts.at[1, :, mod(y + k, 4)]
        to_row = slots.at[0, z if start else bz]
        to_column = slots.at[1, y if start else by]
        for copy in (remote(row, to_row, send.at[0, k], recv.at[0, k], z_peer(k)),
                     remote(column, to_column, send.at[1, k], recv.at[1, k], y_peer(k))):
            copy.start() if start else copy.wait()
    if start:
        slots[0, z] = parts[0, z]
        slots[1, y] = parts[1, :, y]


def reduce_two(parts, slots, send, recv, start):
    dp, ctx, t, x, y, z, core = place()
    for side, order in ((0, STEPS), (1, (2, 1, 3, 0))):
        to = dp if side == 0 else 1 - dp
        at = y * (1 - to) + z * to
        mine = y * (1 - dp) + z * dp
        for k in order:
            slot = slots.at[dp, at] if start else slots.at[to, mod(mine + 4 - k, 4)]
            copy = remote(parts.at[to, mod(at + k, 4)], slot, send.at[side, k], recv.at[side, k],
                          line_target(to, to, k))
            copy.start() if start else copy.wait()
        if start and side == 0:
            slots[dp, at] = parts[dp, at]


def add_slots(slots, out):
    for h in range(2):
        total = slots[h, 0].astype(F32)
        for k in range(1, 4):
            total = total + slots[h, k].astype(F32)
        out[h] = total.astype(out.dtype)


def tokens(src, dst, send, recv, start):
    dp, ctx, t, x, y, z, core = place()
    own = src.at[div(t, 2), pl.ds(pl.multiple_of(core * 32, 32), 32)]
    for other in range(4):
        same = jnp.logical_and(x == y, x == other)
        copy = remote(own, dst.at[y, core], send.at[other], recv.at[y], device(other, x, z, core))
        if start:
            @pl.when(jnp.logical_not(same))
            def _():
                copy.start()

            @pl.when(same)
            def _():
                pltpu.make_async_copy(own, dst.at[y, core], recv.at[y]).start()
        else:
            @pl.when(jnp.logical_not(same))
            def _():
                copy.wait_send()

            remote(own, dst.at[other, core], send.at[other], recv.at[other],
                   (1 - dp, ctx, t)).wait_recv()


def relay(dst, send, recv, start):
    dp, ctx, t, x, y, z, core = place()
    mine = dst.at[:, core]
    if start:
        remote(mine, mine, send, recv, sibling()).start()
    else:
        remote(mine, dst.at[:, 1 - core], send, recv, sibling()).wait()


def ring_gather(own, slots, send, recv, start):
    dp, ctx, t, x, y, z, core = place()
    if start:
        for k in (2, 1, 3):
            remote(own, slots.at[x, core], send.at[0, k], recv.at[0, k], x_peer(k)).start()
        remote(own, slots.at[x, core], send.at[1, 0], recv.at[1, 0], sibling()).start()
        slots[x, core] = own[...]
        return
    for k in STEPS:
        slot = slots.at[mod(x + 4 - k, 4), core]
        remote(own, slot, send.at[0, k], recv.at[0, k], x_peer(k)).wait()
        remote(slot, slot, send.at[1, k], recv.at[1, k], sibling()).start()
    for k in (0,) + STEPS:
        slot = slots.at[mod(x + 4 - k, 4), 1 - core]
        remote(slot, slot, send.at[1, k], recv.at[1, k], sibling()).wait()


def ring_scatter(parts, halves, mid, slots, send, recv, step):
    dp, ctx, t, x, y, z, core = place()
    order = (2, 1, 3, 0)
    if step == 0:
        for k in order:
            to = mod(x + k, 4)
            remote(parts.at[to, 1 - core], halves.at[to], send.at[0, k], recv.at[0, k],
                   sibling()).start()
    elif step == 1:
        for k in order:
            to = mod(x + k, 4)
            remote(parts.at[to, 1 - core], halves.at[to], send.at[0, k], recv.at[0, k],
                   sibling()).wait()
            both = parts[to, core].astype(F32) + halves[to].astype(F32)
            if k == 0:
                slots[x] = both.astype(BF16)
            else:
                mid[to] = both.astype(BF16)
                remote(mid.at[to], slots.at[x], send.at[1, k], recv.at[1, k], x_peer(k)).start()
    else:
        for k in STEPS:
            remote(mid.at[mod(x + k, 4)], slots.at[mod(x + 4 - k, 4)], send.at[1, k], recv.at[1, k],
                   x_peer(k)).wait()


def spread(src, dst, send, recv, start):
    dp, ctx, t, x, y, z, core = place()
    for k in range(2):
        x_to = 2 * k + mod(y, 2)
        same = jnp.logical_and(x_to == x, x == y)
        slot = dst.at[div(y, 2), core]
        copy = remote(src, slot, send.at[k], recv.at[div(y, 2)], device(x_to, x, z, core))
        if start:
            @pl.when(jnp.logical_not(same))
            def _():
                copy.start()

            @pl.when(same)
            def _():
                pltpu.make_async_copy(src, slot, recv.at[div(y, 2)]).start()
        else:
            @pl.when(jnp.logical_not(same))
            def _():
                copy.wait_send()

            remote(src, dst.at[k, core], send.at[k], recv.at[k], (1 - dp, ctx, t)).wait_recv()


def tokens_target(k):
    dp, ctx, t, x, y, z, core = place()
    return device(k, x, z, core)


def tokens_source(k):
    dp, ctx, t, x, y, z, core = place()
    return device(y, k, z, core)


def ctx_peer(k):
    dp, ctx, t, x, y, z, core = place()
    return (dp, mod(ctx + k, 16), t)


INPUTS = dict(lat=0, cond=1, ada=2, ada_bias=3, qkv=4, qv=5, wo=6, ob=7, w1=8, b1=9, w2=10, b2=11, cot=12)
OUTPUTS = dict(
    block_out=((2, 2, 32, 1024), BF16),
    grad_out=((2, 2, 32, 1024), BF16),
    cond_out=((2, 256), F32),
    ada_out=((192, 256), F32),
    ada_bias_out=((1, 6144), F32),
    ga_out=((2, 32, 256), F32),
    gb_out=((2, 32, 1024), F32),
    gc_out=((2, 32, 256), F32),
    bias_out=((2, 1, 1024), F32),
    wide_out=((2, 1024), F32),
)
RING = ((4, 2, 32, 1024), BF16)
FOUR = ((4, 32, 1024), BF16)
BUFFERS = dict(
    xg=RING, cg=RING,
    packa=((2, 32, 512), BF16), packb=((2, 32, 1024), BF16),
    wa=((2, 4, 4, 32, 512), BF16), wb=((2, 4, 4, 32, 1024), BF16),
    cond_a=((8, 256), F32), cond_b=((8, 256), F32), cond8=((8, 256), F32),
    part=((4, 256), F32), parts=((8, 4, 256), F32), pair=((4, 2, 256), F32),
    modg=((16, 2, 256), F32), flat=((1, 6144), F32),
    normed=((256, 1024), F32), hidden=((256, 1024), BF16),
    k_own=((256, 128), BF16), kg=((4, 256, 128), BF16),
    v_own=((256, 128), BF16), vg=((4, 256, 128), BF16), prob=((2, 256, 1024), F32),
    branch_part=RING, branch_half=FOUR, branch_mid=FOUR, branch_slots=FOUR,
    h2_own=((32, 1024), BF16), h2=RING,
    d_feed=((256, 1024), BF16), d_act=((256, 512), F32),
    dh2_part=RING, dh2_half=FOUR, dh2_mid=FOUR, dh2_slots=FOUR,
    feed_part=RING, feed_half=FOUR, feed_mid=FOUR, feed_slots=FOUR,
    db_own=((32, 1024), BF16), db=RING,
    block_own=((32, 1024), BF16), d_middle=((32, 1024), F32),
    dk_part=((4, 256, 128), BF16), dk_slots=((4, 256, 128), BF16),
    dv_part=((4, 256, 128), BF16), dv_slots=((4, 256, 128), BF16),
    dh_part=RING, dh_half=FOUR, dh_mid=FOUR, dh_slots=FOUR,
    grad_own=((32, 1024), BF16),
    m_own=((4, 1024), F32), m_slots=((8, 4, 1024), F32),
    z_own=((8, 1024), F32), z_slots=((4, 8, 1024), F32),
    y_own=((8, 1024), F32), y_slots=((4, 8, 1024), F32),
    n_own=((2, 1024), F32), n_slots=((8, 2, 1024), F32),
    l_own=((4, 1024), F32), l_slots=((16, 4, 1024), F32),
    dm=((8, 6144), F32), bias_own=((1, 1024), F32),
    cond_part=((4, 256), F32), cond_slots=((16, 4, 256), F32), cond_sum=((4, 256), F32), ada_b=((192, 256), BF16),
    ga=((2, 4, 4, 32, 256), BF16), ga1=((2, 4, 4, 32, 256), BF16),
    ga2=((2, 4, 32, 256), BF16), ga3=((2, 4, 32, 256), BF16),
    gb=((2, 4, 4, 32, 1024), BF16), gb1=((2, 4, 4, 32, 1024), BF16),
    gb2=((2, 4, 32, 1024), BF16), gb3=((2, 4, 32, 1024), BF16),
    gc=((2, 4, 4, 32, 256), BF16), gc1=((2, 4, 4, 32, 256), BF16),
    gc2=((2, 4, 32, 256), BF16), gc3=((2, 4, 32, 256), BF16),
)
SEMS = dict(
    s_cond=(), s_xg=(4,), s_xr=(), s_cg=(4,), s_cr=(),
    s_wa1=(2, 4), s_wa2=(2, 4), s_wb1=(2, 4), s_wb2=(2, 4),
    s_mod=(8,), s_mod2=(16,), s_k=(4,), s_v=(4,),
    s_branch=(2, 4), s_h2=(2, 4), s_dh2=(2, 4), s_feed=(2, 4), s_db=(2, 4),
    s_block=(2,), s_dk=(4,), s_dv=(4,), s_dh=(2, 4), s_grad=(2,), s_blockr=(), s_gradr=(), s_ada=(),
    s_m=(8,), s_z=(4,), s_y=(4,), s_n=(8,), s_l=(16,), s_bias=(), s_c=(16,),
    s_ga1=(2, 4), s_ga2=(2, 4), s_gb1=(2, 4), s_gb2=(2, 4), s_gc1=(2, 4), s_gc2=(2, 4),
)


class Refs:
    pass


def block_kernel(*refs):
    g = Refs()
    names = list(INPUTS) + list(OUTPUTS) + list(BUFFERS)
    for name, ref in zip(names, refs):
        setattr(g, name, ref)
    sems = refs[len(names):]
    for i, name in enumerate(SEMS):
        setattr(g, name, (sems[2 * i], sems[2 * i + 1]))
    dp, ctx, t, x, y, z, core = place()
    r = x * 2 + core
    partner = (1 - dp, ctx, t)

    greet([(1, 8, ring_peer), (1, 16, ctx_peer), (0, 4, tokens_target), (0, 4, tokens_source),
           (1, 4, cross_y), (1, 4, cross_z)])

    cond_slice = g.cond[:, pl.ds(pl.multiple_of(t * 256, 256), 256)].astype(F32)
    sigmoid = 1.0 / (1.0 + jnp.exp(-cond_slice))
    cond_act = (cond_slice * sigmoid).astype(BF16).astype(F32)
    rows = lax.broadcasted_iota(jnp.int32, (8, 256), 0)
    g.cond_a[...] = jnp.where(rows == dp, cond_act[0:1], jnp.where(rows == dp + 2, cond_act[1:2], 0.0))
    cond_copy = remote(g.cond_a, g.cond_b, *g.s_cond, partner)
    cond_copy.start()
    for h in range(2):
        for k in range(3):
            g.packa[h, :, 128 * k:128 * k + 128] = g.qkv[k, :, 128 * h:128 * h + 128]
        g.packa[h, :, 384:] = g.wo[:, 128 * h:128 * h + 128]
    plane_one(g.wa, g.packa, *g.s_wa1, True)
    tokens(g.lat, g.xg, *g.s_xg, True)
    cond_copy.wait()
    g.cond8[...] = g.cond_a[...] + g.cond_b[...]
    g.part[:, :192] = dot(g.cond8[...].astype(BF16), g.ada[...], NT)[:4]
    gather_start(g.part, g.parts, r, 8, ring_peer, *g.s_mod)
    g.parts[r] = g.part[...]
    for h in range(2):
        g.packb[h, :, :512] = g.w1[0, :, 512 * h:512 * h + 512]
        g.packb[h, :, 512:] = g.w2[:, 512 * h:512 * h + 512]
    gather_wait(g.part, g.parts, r, 8, ring_peer, *g.s_mod)
    for c in range(2):
        both = (g.parts[2 * c] + g.parts[2 * c + 1]) + (g.parts[2 * c + 4] + g.parts[2 * c + 5])
        for i in range(4):
            g.pair[i, c:c + 1, :192] = both[i:i + 1, :192]

    def mod_start(k, carry):
        remote(g.pair.at[mod(ctx + k, 4)], g.modg.at[ctx], g.s_mod2[0].at[k], g.s_mod2[1].at[ctx],
               ctx_peer(k)).start()
        return carry
    loop(1, 16, mod_start)
    g.modg[ctx] = g.pair[y]
    tokens(g.lat, g.xg, *g.s_xg, False)
    relay(g.xg, *g.s_xr, True)
    plane_one(g.wa, g.packa, *g.s_wa1, False)
    plane_two(g.wa, *g.s_wa2, True)
    relay(g.xg, *g.s_xr, False)
    normed, _ = normalize(g.xg[...].astype(F32).reshape(256, 1024))
    g.normed[...] = normed
    plane_one(g.wb, g.packb, *g.s_wb1, True)
    ada_copy = remote(g.ada, g.ada_b, *g.s_ada, partner)
    ada_copy.start()

    def mod_wait(k, carry):
        other = mod(ctx + k, 16)
        remote(g.pair.at[0], g.modg.at[other], g.s_mod2[0].at[k], g.s_mod2[1].at[other],
               ctx_peer(k)).wait()
        return carry
    loop(1, 16, mod_wait)
    for p in range(16):
        c, first = div(p, 8), mod(2 * p, 16)
        both = jnp.concatenate(
            [g.modg[first, c:c + 1, :192], g.modg[first + 1, c:c + 1, :192]], axis=1)
        g.flat[:, 384 * p:384 * p + 384] = both + g.ada_bias[:, 384 * p:384 * p + 384].astype(F32)
    shift1, scale1, gate1, shift2, scale2, gate2 = [
        g.flat[:, k * 1024:(k + 1) * 1024] for k in range(6)]
    hidden = (g.normed[...] * (1.0 + scale1) + shift1).astype(BF16)
    g.hidden[...] = hidden
    plane_two(g.wa, *g.s_wa2, False)
    mixed = dot(hidden, g.wa[:, :, :, :, :384].reshape(1024, 384), NN)
    qv = g.qv[0, :, pl.ds(pl.multiple_of(dp * 128, 128), 128)].astype(F32)
    g.k_own[...] = mixed[:, 128:256].astype(BF16)
    gather_start(g.k_own, g.kg, z, 4, z_peer, *g.s_k)
    g.v_own[...] = (mixed[:, 256:] + qv[1:2]).astype(BF16)
    gather_start(g.v_own, g.vg, z, 4, z_peer, *g.s_v)
    query = (mixed[:, :128] + qv[0:1]).astype(BF16)
    g.kg[z] = g.k_own[...]
    g.vg[z] = g.v_own[...]
    tokens(g.cot, g.cg, *g.s_cg, True)
    gather_wait(g.k_own, g.kg, z, 4, z_peer, *g.s_k)
    plane_one(g.wb, g.packb, *g.s_wb1, False)
    plane_two(g.wb, *g.s_wb2, True)
    for h in range(2):
        key = g.kg[:, :, 64 * h:64 * h + 64].reshape(1024, 64)
        scores = dot(query[:, 64 * h:64 * h + 64], key, NT) * SCALE
        expo = jnp.exp(scores - jnp.max(scores, axis=-1, keepdims=True))
        g.prob[h] = expo / jnp.sum(expo, axis=-1, keepdims=True)
    gather_wait(g.v_own, g.vg, z, 4, z_peer, *g.s_v)
    heads = []
    for h in range(2):
        value = g.vg[:, :, 64 * h:64 * h + 64].reshape(1024, 64)
        heads.append(dot(g.prob[h].astype(BF16), value, NN))
    attended = jnp.concatenate(heads, axis=1).astype(BF16)
    w_out = g.wa[:, :, :, :, 384:].reshape(1024, 128)
    g.branch_part[...] = dot(attended, w_out, NT).astype(BF16).reshape(4, 2, 32, 1024)
    branch_ring = (g.branch_part, g.branch_half, g.branch_mid, g.branch_slots, *g.s_branch)
    ring_scatter(*branch_ring, 0)
    ring_scatter(*branch_ring, 1)
    tokens(g.cot, g.cg, *g.s_cg, False)
    relay(g.cg, *g.s_cr, True)
    relay(g.cg, *g.s_cr, False)
    d_feed = (g.cg[...].astype(F32).reshape(256, 1024) * gate2).astype(BF16)
    g.d_feed[...] = d_feed
    g.z_own[...] = jnp.zeros_like(g.z_own)
    g.z_own[5:6] = jnp.sum(d_feed.astype(F32), axis=0, keepdims=True)
    ring_scatter(*branch_ring, 2)

    x_own = g.xg[x, core].astype(F32)
    branch = jnp.sum(g.branch_slots[...].astype(F32), axis=0) + g.ob[...].astype(F32)
    middle = x_own + gate1 * branch
    normed_two, inverse_two = normalize(middle)
    g.h2_own[...] = (normed_two * (1.0 + scale2) + shift2).astype(BF16)
    ring_gather(g.h2_own, g.h2, *g.s_h2, True)
    plane_two(g.wb, *g.s_wb2, False)
    w_second = g.wb[:, :, :, :, 512:].reshape(1024, 512)
    g.d_act[...] = dot(d_feed, w_second, NN)
    ring_gather(g.h2_own, g.h2, *g.s_h2, False)

    hidden_two = g.h2[...].reshape(256, 1024)
    w_first = g.wb[:, :, :, :, :512].reshape(1024, 512)
    bias_first = g.b1[:, pl.ds(pl.multiple_of(dp * 512, 512), 512)].astype(F32)
    before = dot(hidden_two, w_first, NN) + bias_first
    square = before * before
    tanh = jnp.tanh(ROOT * before * (1.0 + 0.044715 * square))
    slope = 0.5 * (1.0 + tanh) + (0.5 * ROOT) * before * (1.0 - tanh * tanh) * (
        1.0 + (3.0 * 0.044715) * square)
    d_before = (g.d_act[...] * slope).astype(BF16)
    g.dh2_part[...] = dot(d_before, w_first, NT).astype(BF16).reshape(4, 2, 32, 1024)
    dh2_ring = (g.dh2_part, g.dh2_half, g.dh2_mid, g.dh2_slots, *g.s_dh2)
    ring_scatter(*dh2_ring, 0)
    activated = (0.5 * before * (1.0 + tanh)).astype(BF16)
    ring_scatter(*dh2_ring, 1)
    feed_part = dot(activated, w_second, NT)
    g.feed_part[...] = feed_part.astype(BF16).reshape(4, 2, 32, 1024)
    g.gb[:, :, :, :, :512] = dot(hidden_two, d_before, TN).astype(BF16).reshape(2, 4, 4, 32, 512)
    g.gb[:, :, :, :, 512:] = dot(d_feed, activated, TN).astype(BF16).reshape(2, 4, 4, 32, 512)
    reduce_one(g.gb, g.gb1, *g.s_gb1, True)
    g.m_own[3:4] = jnp.sum(
        g.cg[...].astype(F32).reshape(256, 1024) * feed_part, axis=0, keepdims=True)
    g.z_own[6:7, :512] = jnp.sum(d_before.astype(F32), axis=0, keepdims=True)
    ring_scatter(*dh2_ring, 2)

    cot_own = g.cg[x, core].astype(F32)
    d_hidden = jnp.sum(g.dh2_slots[...].astype(F32), axis=0)
    d_middle = cot_own + norm_back(d_hidden * (1.0 + scale2), normed_two, inverse_two)
    g.d_middle[...] = d_middle
    g.db_own[...] = (d_middle * gate1).astype(BF16)
    ring_gather(g.db_own, g.db, *g.s_db, True)
    feed_ring = (g.feed_part, g.feed_half, g.feed_mid, g.feed_slots, *g.s_feed)
    ring_scatter(*feed_ring, 0)
    g.m_own[0:1] = jnp.sum(d_middle * branch, axis=0, keepdims=True)
    g.m_own[1:2] = jnp.sum(d_hidden, axis=0, keepdims=True)
    g.m_own[2:3] = jnp.sum(d_hidden * normed_two, axis=0, keepdims=True)
    g.m_own[3:4] += jnp.sum(cot_own, axis=0, keepdims=True) * g.b2[...].astype(F32)
    gather_start(g.m_own, g.m_slots, r, 8, ring_peer, *g.s_m)
    g.m_slots[r] = g.m_own[...]
    ring_gather(g.db_own, g.db, *g.s_db, False)
    ring_scatter(*feed_ring, 1)

    d_branch = g.db[...].reshape(256, 1024)
    d_attended = dot(d_branch, w_out, NN).astype(BF16)
    d_one = [d_attended[:, 64 * h:64 * h + 64] for h in range(2)]
    d_value = [dot(g.prob[h].astype(BF16), d_one[h], TN) for h in range(2)]
    g.dv_part[...] = jnp.concatenate(d_value, axis=1).astype(BF16).reshape(4, 256, 128)
    scatter_start(g.dv_part, g.dv_slots, z, 4, z_peer, *g.s_dv)
    g.dv_slots[z] = g.dv_part[z]
    d_query, d_key = [], []
    for h in range(2):
        key = g.kg[:, :, 64 * h:64 * h + 64].reshape(1024, 64)
        value = g.vg[:, :, 64 * h:64 * h + 64].reshape(1024, 64)
        prob = g.prob[h]
        d_prob = dot(d_one[h], value, NT)
        d_scores = (prob * (d_prob - jnp.sum(prob * d_prob, axis=-1, keepdims=True))).astype(BF16)
        d_key.append(dot(d_scores, query[:, 64 * h:64 * h + 64], TN) * SCALE)
        d_query.append(dot(d_scores, key, NN) * SCALE)
    g.dk_part[...] = jnp.concatenate(d_key, axis=1).astype(BF16).reshape(4, 256, 128)
    scatter_start(g.dk_part, g.dk_slots, z, 4, z_peer, *g.s_dk)
    g.dk_slots[z] = g.dk_part[z]
    d_query = jnp.concatenate(d_query, axis=1).astype(BF16)
    g.z_own[4:5] = jnp.sum(d_branch.astype(F32), axis=0, keepdims=True)
    g.z_own[6:7, 512:640] = jnp.sum(d_query.astype(F32), axis=0, keepdims=True)
    gather_wait(g.m_own, g.m_slots, r, 8, ring_peer, *g.s_m)
    g.z_own[0:4] = jnp.sum(g.m_slots[...], axis=0)
    gather_start(g.z_own, g.z_slots, z, 4, z_peer, *g.s_z)
    g.z_slots[z] = g.z_own[...]
    ring_scatter(*feed_ring, 2)
    feed = jnp.sum(g.feed_slots[...].astype(F32), axis=0) + g.b2[...].astype(F32)
    g.block_own[...] = (middle + gate2 * feed).astype(BF16)
    spread(g.block_own, g.block_out, *g.s_block, True)
    g.gc[:, :, :, :, :128] = dot(g.hidden[...], d_query, TN).astype(BF16).reshape(2, 4, 4, 32, 128)
    g.gc[:, :, :, :, 128:] = dot(d_branch, attended, TN).astype(BF16).reshape(2, 4, 4, 32, 128)
    reduce_one(g.gc, g.gc1, *g.s_gc1, True)
    reduce_one(g.gb, g.gb1, *g.s_gb1, False)
    add_slots(g.gb1, g.gb2)
    reduce_two(g.gb2, g.gb3, *g.s_gb2, True)
    scatter_wait(g.dv_part, g.dv_slots, z, 4, z_peer, *g.s_dv)
    scatter_wait(g.dk_part, g.dk_slots, z, 4, z_peer, *g.s_dk)

    d_keys = jnp.sum(g.dk_slots[...].astype(F32), axis=0).astype(BF16)
    d_values = jnp.sum(g.dv_slots[...].astype(F32), axis=0).astype(BF16)
    d_qkv = jnp.concatenate([d_query, d_keys, d_values], axis=1)
    d_part = dot(d_qkv, g.wa[:, :, :, :, :384].reshape(1024, 384), NT)
    g.dh_part[...] = d_part.astype(BF16).reshape(4, 2, 32, 1024)
    dh_ring = (g.dh_part, g.dh_half, g.dh_mid, g.dh_slots, *g.s_dh)
    ring_scatter(*dh_ring, 0)
    d_kv = jnp.concatenate([d_keys, d_values], axis=1)
    g.ga[...] = dot(g.hidden[...], d_kv, TN).astype(BF16).reshape(2, 4, 4, 32, 256)
    reduce_one(g.ga, g.ga1, *g.s_ga1, True)
    g.n_own[0:1] = jnp.sum(d_part, axis=0, keepdims=True)
    g.n_own[1:2] = jnp.sum(d_part * g.normed[...], axis=0, keepdims=True)
    gather_start(g.n_own, g.n_slots, r, 8, ring_peer, *g.s_n)
    g.n_slots[r] = g.n_own[...]
    ring_scatter(*dh_ring, 1)
    gather_wait(g.z_own, g.z_slots, z, 4, z_peer, *g.s_z)
    g.y_own[...] = jnp.sum(g.z_slots[...], axis=0)
    gather_start(g.y_own, g.y_slots, y, 4, y_peer, *g.s_y)
    g.y_slots[y] = g.y_own[...]
    reduce_one(g.gc, g.gc1, *g.s_gc1, False)
    add_slots(g.gc1, g.gc2)
    reduce_two(g.gc2, g.gc3, *g.s_gc2, True)
    gather_wait(g.n_own, g.n_slots, r, 8, ring_peer, *g.s_n)
    g.l_own[0:2] = jnp.sum(g.n_slots[...], axis=0)
    g.l_own[2:4] = jnp.zeros((2, 1024), F32)
    g.l_own[2:3, :128] = jnp.sum(d_values.astype(F32), axis=0, keepdims=True)
    gather_start(g.l_own, g.l_slots, ctx, 16, ctx_peer, *g.s_l)
    g.l_slots[ctx] = g.l_own[...]
    ring_scatter(*dh_ring, 2)

    x_normed, x_inverse = normalize(x_own)
    d_hidden = jnp.sum(g.dh_slots[...].astype(F32), axis=0)
    grad = g.d_middle[...] + norm_back(d_hidden * (1.0 + scale1), x_normed, x_inverse)
    g.grad_own[...] = grad.astype(BF16)
    spread(g.grad_own, g.grad_out, *g.s_grad, True)
    reduce_one(g.ga, g.ga1, *g.s_ga1, False)
    add_slots(g.ga1, g.ga2)
    reduce_two(g.ga2, g.ga3, *g.s_ga2, True)
    g.dm[...] = jnp.zeros_like(g.dm)
    gather_wait(g.y_own, g.y_slots, y, 4, y_peer, *g.s_y)
    for k in range(2, 6):
        for i in range(4):
            g.dm[i:i + 1, k * 1024:(k + 1) * 1024] = g.y_slots[i, k - 2:k - 1]
    gather_wait(g.l_own, g.l_slots, ctx, 16, ctx_peer, *g.s_l)

    late = jnp.sum(g.l_slots[...].reshape(4, 4, 4, 1024), axis=0)
    for k in range(2):
        for i in range(4):
            g.dm[i:i + 1, k * 1024:(k + 1) * 1024] = late[i, k:k + 1]

    def columns(chunk):
        wide = g.dm[:, pl.ds(pl.multiple_of(div(3 * chunk, 2) * 128, 128), 256)]
        return jnp.where(mod(chunk, 2) == 1, pltpu.roll(wide, 192, 1), wide)[:, :192]

    own_columns = columns(dp * 16 + ctx)
    ada_copy.wait()
    highest = lax.Precision.HIGHEST
    g.cond_part[...] = (
        dot_split(own_columns, g.ada[...]) + dot_split(columns((1 - dp) * 16 + ctx), g.ada_b[...]))[:4]
    gather_start(g.cond_part, g.cond_slots, ctx, 16, ctx_peer, *g.s_c)
    g.cond_slots[ctx] = g.cond_part[...]
    early = jnp.sum(g.y_slots[...], axis=0)
    g.wide_out[...] = early[4:6]
    g.bias_own[:, :640] = early[6:7, :640]
    g.bias_own[:, 640:768] = jnp.sum(late[:, 2], axis=0, keepdims=True)[:, :128]
    g.bias_own[:, 768:] = jnp.zeros((1, 256), F32)
    remote(g.bias_own, g.bias_out.at[dp], *g.s_bias, partner).start()
    g.bias_out[dp] = g.bias_own[...]
    g.ada_bias_out[...] = jnp.sum(g.dm[...], axis=0, keepdims=True)
    spread(g.block_own, g.block_out, *g.s_block, False)
    relay(g.block_out, *g.s_blockr, True)
    reduce_two(g.gb2, g.gb3, *g.s_gb2, False)
    add_slots(g.gb3, g.gb_out)
    reduce_two(g.gc2, g.gc3, *g.s_gc2, False)
    add_slots(g.gc3, g.gc_out)
    spread(g.grad_own, g.grad_out, *g.s_grad, False)
    relay(g.grad_out, *g.s_gradr, True)
    g.ada_out[...] = dot(own_columns, g.cond8[...], TN, highest)
    reduce_two(g.ga2, g.ga3, *g.s_ga2, False)
    add_slots(g.ga3, g.ga_out)
    gather_wait(g.cond_part, g.cond_slots, ctx, 16, ctx_peer, *g.s_c)
    g.cond_sum[...] = jnp.sum(g.cond_slots[...], axis=0)
    slope = sigmoid * (1.0 + cond_slice * (1.0 - sigmoid))
    for i in range(2):
        g.cond_out[i:i + 1] = g.cond_sum[pl.ds(2 * i + dp, 1)] * slope[i:i + 1]
    remote(g.bias_own, g.bias_out.at[1 - dp], *g.s_bias, partner).wait()
    relay(g.block_out, *g.s_blockr, False)
    relay(g.grad_out, *g.s_gradr, False)


def unpack_kernel(block, grad, cond, ada, ada_bias, ga, gb, gc, bias, wide,
                  block_out, grad_out, cond_out, ada_out, ada_bias_out, qkv_out, qv_out,
                  wo_out, ob_out, w1_out, b1_out, w2_out, b2_out):
    block_out[...] = block[...].reshape(2, 64, 1024)
    grad_out[...] = grad[...].astype(F32).reshape(2, 64, 1024)
    cond_out[...] = cond[...]
    ada_out[...] = ada[...]
    ada_bias_out[...] = ada_bias[...]
    for h in range(2):
        for k in range(3):
            part = gc[h, :, :128] if k == 0 else ga[h, :, 128 * k - 128:128 * k]
            qkv_out[k, :, 128 * h:128 * h + 128] = part
        for k in range(2):
            qv_out[0, k:k + 1, 128 * h:128 * h + 128] = bias[h, :, 512 + 128 * k:640 + 128 * k]
        wo_out[:, 128 * h:128 * h + 128] = gc[h, :, 128:]
        w1_out[0, :, 512 * h:512 * h + 512] = gb[h, :, :512]
        w2_out[:, 512 * h:512 * h + 512] = gb[h, :, 512:]
        b1_out[:, 512 * h:512 * h + 512] = bias[h, :, :512]
    ob_out[...] = wide[0:1]
    b2_out[...] = wide[1:2]


def on_device(
    latents, cond, ada_weight, ada_bias, qkv_weight, qv_bias, out_weight, out_bias,
    first_weight, first_bias, second_weight, second_bias, cotangent,
):
    args = [
        latents, cond, ada_weight[0].T, ada_bias, qkv_weight[0].transpose(1, 0, 2), qv_bias,
        out_weight[0].T, out_bias, first_weight, first_bias, second_weight[0].T, second_bias,
        cotangent,
    ]
    outs = pl.pallas_call(
        block_kernel,
        out_shape=[shape(*one) for one in OUTPUTS.values()],
        in_specs=[VMEM] * len(args),
        out_specs=[VMEM] * len(OUTPUTS),
        scratch_shapes=[pltpu.VMEM(*one) for one in BUFFERS.values()]
        + [DMA(one) for one in SEMS.values() for _ in range(2)],
        compiler_params=pltpu.CompilerParams(
            collective_id=1, has_side_effects=True, vmem_limit_bytes=56 << 20
        ),
        name="block",
    )(*args)
    final = [
        shape((2, 64, 1024), BF16), shape((2, 64, 1024), F32), shape((2, 256), F32),
        shape((192, 256), F32), shape((1, 6144), F32), shape((3, 32, 256), F32),
        shape((1, 2, 256), F32), shape((32, 256), F32), shape((1, 1024), F32),
        shape((1, 32, 1024), F32), shape((1, 1024), F32), shape((32, 1024), F32),
        shape((1, 1024), F32),
    ]
    results = pl.pallas_call(
        unpack_kernel, out_shape=final, in_specs=[VMEM] * len(outs), out_specs=[VMEM] * len(final),
        name="unpack",
    )(*outs)
    results = list(results)
    for k in (3, 7, 11):
        results[k] = results[k].T[None]
    results[5] = results[5].transpose(1, 0, 2)[None]
    return tuple(results)


def solution(mesh):
    return jax.shard_map(
        on_device,
        mesh=mesh,
        in_specs=(
            P("dp", "context", None),
            P("dp", None),
            P(None, "tensor", ("dp", "context")),
            P(),
            P(None, ("dp", "context"), None, "tensor"),
            P(None, None, "tensor"),
            P(None, "tensor", ("dp", "context")),
            P(),
            P(None, ("dp", "context"), "tensor"),
            P(None, "tensor"),
            P(None, "tensor", ("dp", "context")),
            P(),
            P("dp", "context", None),
        ),
        out_specs=(
            P("dp", "context", None),
            P("dp", "context", None),
            P("dp", "tensor"),
            P(None, "tensor", ("dp", "context")),
            P(),
            P(None, ("dp", "context"), None, "tensor"),
            P(None, None, "tensor"),
            P(None, "tensor", ("dp", "context")),
            P(),
            P(None, ("dp", "context"), "tensor"),
            P(None, "tensor"),
            P(None, "tensor", ("dp", "context")),
            P(),
        ),
        check_vma=False,
    )
```

```python
import math

import jax
import jax.numpy as jnp
from jax import lax
from jax.experimental import pallas as pl
from jax.experimental.pallas import tpu as pltpu
from jax.sharding import PartitionSpec as P

EPSILON = 1e-06
F32 = jnp.float32
BF16 = jnp.bfloat16
MESH = pl.DeviceIdType.MESH
VMEM = pl.BlockSpec(memory_space=pltpu.VMEM)
DMA = pltpu.SemaphoreType.DMA


def mod(a, b):
    return a % b if isinstance(a, int) else lax.rem(a, jnp.int32(b))


def div(a, b):
    return a // b if isinstance(a, int) else lax.div(a, jnp.int32(b))


def place():
    dp = lax.axis_index("dp")
    ctx = lax.axis_index("context")
    t = lax.axis_index("tensor")
    return dp, ctx, t, div(t, 2) * 2 + dp, mod(ctx, 4), div(ctx, 4), mod(t, 2)


def loop(first, last, one):
    for k in range(first, last):
        one(k, 0)


def device(x, y, z, core):
    return (mod(x, 2), z * 4 + y, div(x, 2) * 2 + core)


def remote(src, dst, send, recv, target):
    return pltpu.make_async_remote_copy(
        src_ref=src, dst_ref=dst, send_sem=send, recv_sem=recv,
        device_id=target, device_id_type=MESH,
    )


def greet(targets):
    barrier = pltpu.get_barrier_semaphore()
    count = 0
    for first, last, target in targets:
        def one(k, carry, target=target):
            pl.semaphore_signal(barrier, inc=1, device_id=target(k), device_id_type=MESH)
            return carry
        loop(first, last, one)
        count += last - first
    pl.semaphore_wait(barrier, count)


def z_peer(k):
    dp, ctx, t, x, y, z, core = place()
    return (dp, mod(z + k, 4) * 4 + y, t)


def y_peer(k):
    dp, ctx, t, x, y, z, core = place()
    return (dp, z * 4 + mod(y + k, 4), t)


def x_peer(k):
    dp, ctx, t, x, y, z, core = place()
    return device(mod(x + k, 4), y, z, core)


def sibling():
    dp, ctx, t, x, y, z, core = place()
    return device(x, y, z, 1 - core)


def ring_peer(k):
    dp, ctx, t, x, y, z, core = place()
    r = mod(x * 2 + core + k, 8)
    return device(div(r, 2), y, z, mod(r, 2))


def gather_start(own, slots, mine, n, peer, send, recv):
    def one(k, carry):
        remote(own, slots.at[mine], send.at[k], recv.at[mine], peer(k)).start()
        return carry
    loop(1, n, one)


def gather_wait(own, slots, mine, n, peer, send, recv):
    def one(k, carry):
        other = mod(mine + k, n)
        copy = remote(own, slots.at[other], send.at[k], recv.at[other], peer(k))
        copy.wait_recv()
        copy.wait_send()
        return carry
    loop(1, n, one)


def scatter_start(parts, slots, mine, n, peer, send, recv):
    def one(k, carry):
        other = mod(mine + k, n)
        remote(parts.at[other], slots.at[mine], send.at[k], recv.at[mine], peer(k)).start()
        return carry
    loop(1, n, one)


def scatter_wait(parts, slots, mine, n, peer, send, recv):
    def one(k, carry):
        other = mod(mine + k, n)
        copy = remote(parts.at[other], slots.at[other], send.at[k], recv.at[other], peer(k))
        copy.wait_recv()
        copy.wait_send()
        return carry
    loop(1, n, one)


def shape(dims, dtype):
    return jax.ShapeDtypeStruct(dims, dtype)


def normalize(values):
    center = values - jnp.mean(values, axis=-1, keepdims=True)
    inverse = lax.rsqrt(jnp.mean(center * center, axis=-1, keepdims=True) + EPSILON)
    return center * inverse, inverse


def norm_back(grad_hat, normed, inverse):
    first = jnp.mean(grad_hat, axis=-1, keepdims=True)
    second = jnp.mean(grad_hat * normed, axis=-1, keepdims=True)
    return inverse * (grad_hat - first - normed * second)


def dot(left, right, contract, precision=None):
    return lax.dot_general(
        left, right, (contract, ((), ())), precision=precision, preferred_element_type=F32
    )


def dot_split(left, right):
    high = left.astype(BF16)
    rest = left - high.astype(F32)
    middle = rest.astype(BF16)
    low = (rest - middle.astype(F32)).astype(BF16)
    out = dot(jnp.concatenate([high, middle, low], axis=0), right, NN)
    n = left.shape[0]
    return out[:n] + (out[n:2 * n] + out[2 * n:])


NN = ((1,), (0,))
NT = ((1,), (1,))
TN = ((0,), (0,))
SCALE = 1.0 / math.sqrt(64)
ROOT = math.sqrt(2.0 / math.pi)
STEPS = (1, 3, 2)


def from_back(k):
    y, z = mod(lax.axis_index("context"), 4), div(lax.axis_index("context"), 4)
    return mod(y + 4 - k, 4), mod(z + 4 - k, 4)


def line_target(to, h, k):
    dp, ctx, t, x, y, z, core = place()
    return (to, mod(z + h * k, 4) * 4 + mod(y + (1 - h) * k, 4), t)


def cross_y(k):
    return line_target(1 - lax.axis_index("dp"), 0, k)


def cross_z(k):
    return line_target(1 - lax.axis_index("dp"), 1, k)


def plane_one(full, pack, send, recv, start):
    dp, ctx, t, x, y, z, core = place()
    for side, order in ((0, STEPS), (1, (2, 1, 3, 0))):
        to = dp if side == 0 else 1 - dp
        for k in order:
            target = line_target(to, dp, k)
            if start:
                remote(pack.at[to], full.at[dp, z, y], send.at[side, k], recv.at[side, k],
                       target).start()
            else:
                slot = full.at[to, mod(z + to * (4 - k), 4), mod(y + (1 - to) * (4 - k), 4)]
                remote(pack.at[to], slot, send.at[side, k], recv.at[side, k], target).wait()
    if start:
        full[dp, z, y] = pack[dp]


def plane_two(full, send, recv, start):
    dp, ctx, t, x, y, z, core = place()
    for k in STEPS:
        by, bz = from_back(k)
        row, column = full.at[0, z], full.at[1, :, y]
        if start:
            remote(row, row, send.at[0, k], recv.at[0, k], z_peer(k)).start()
            remote(column, column, send.at[1, k], recv.at[1, k], y_peer(k)).start()
        else:
            remote(row, full.at[0, bz], send.at[0, k], recv.at[0, k], z_peer(k)).wait()
            remote(column, full.at[1, :, by], send.at[1, k], recv.at[1, k], y_peer(k)).wait()


def reduce_one(parts, slots, send, recv, start):
    dp, ctx, t, x, y, z, core = place()
    for k in STEPS:
        by, bz = from_back(k)
        row, column = parts.at[0, mod(z + k, 4)], parts.at[1, :, mod(y + k, 4)]
        to_row = slots.at[0, z if start else bz]
        to_column = slots.at[1, y if start else by]
        for copy in (remote(row, to_row, send.at[0, k], recv.at[0, k], z_peer(k)),
                     remote(column, to_column, send.at[1, k], recv.at[1, k], y_peer(k))):
            copy.start() if start else copy.wait()
    if start:
        slots[0, z] = parts[0, z]
        slots[1, y] = parts[1, :, y]


def reduce_two(parts, slots, send, recv, start):
    dp, ctx, t, x, y, z, core = place()
    for side, order in ((0, STEPS), (1, (2, 1, 3, 0))):
        to = dp if side == 0 else 1 - dp
        at = y * (1 - to) + z * to
        mine = y * (1 - dp) + z * dp
        for k in order:
            slot = slots.at[dp, at] if start else slots.at[to, mod(mine + 4 - k, 4)]
            copy = remote(parts.at[to, mod(at + k, 4)], slot, send.at[side, k], recv.at[side, k],
                          line_target(to, to, k))
            copy.start() if start else copy.wait()
        if start and side == 0:
            slots[dp, at] = parts[dp, at]


def add_slots(slots, out):
    for h in range(2):
        total = slots[h, 0].astype(F32)
        for k in range(1, 4):
            total = total + slots[h, k].astype(F32)
        out[h] = total.astype(out.dtype)


def tokens(src, dst, send, recv, start):
    dp, ctx, t, x, y, z, core = place()
    own = src.at[div(t, 2), pl.ds(pl.multiple_of(core * 32, 32), 32)]
    for other in range(4):
        same = jnp.logical_and(x == y, x == other)
        copy = remote(own, dst.at[y, core], send.at[other], recv.at[y], device(other, x, z, core))
        if start:
            @pl.when(jnp.logical_not(same))
            def _():
                copy.start()

            @pl.when(same)
            def _():
                pltpu.make_async_copy(own, dst.at[y, core], recv.at[y]).start()
        else:
            @pl.when(jnp.logical_not(same))
            def _():
                copy.wait_send()

            remote(own, dst.at[other, core], send.at[other], recv.at[other],
                   (1 - dp, ctx, t)).wait_recv()


def relay(dst, send, recv, start):
    dp, ctx, t, x, y, z, core = place()
    mine = dst.at[:, core]
    if start:
        remote(mine, mine, send, recv, sibling()).start()
    else:
        remote(mine, dst.at[:, 1 - core], send, recv, sibling()).wait()


def ring_gather(own, slots, send, recv, start):
    dp, ctx, t, x, y, z, core = place()
    if start:
        for k in (2, 1, 3):
            remote(own, slots.at[x, core], send.at[0, k], recv.at[0, k], x_peer(k)).start()
        remote(own, slots.at[x, core], send.at[1, 0], recv.at[1, 0], sibling()).start()
        slots[x, core] = own[...]
        return
    for k in STEPS:
        slot = slots.at[mod(x + 4 - k, 4), core]
        remote(own, slot, send.at[0, k], recv.at[0, k], x_peer(k)).wait()
        remote(slot, slot, send.at[1, k], recv.at[1, k], sibling()).start()
    for k in (0,) + STEPS:
        slot = slots.at[mod(x + 4 - k, 4), 1 - core]
        remote(slot, slot, send.at[1, k], recv.at[1, k], sibling()).wait()


def ring_scatter(parts, halves, mid, slots, send, recv, step):
    dp, ctx, t, x, y, z, core = place()
    order = (2, 1, 3, 0)
    if step == 0:
        for k in order:
            to = mod(x + k, 4)
            remote(parts.at[to, 1 - core], halves.at[to], send.at[0, k], recv.at[0, k],
                   sibling()).start()
    elif step == 1:
        for k in order:
            to = mod(x + k, 4)
            remote(parts.at[to, 1 - core], halves.at[to], send.at[0, k], recv.at[0, k],
                   sibling()).wait()
            both = parts[to, core].astype(F32) + halves[to].astype(F32)
            if k == 0:
                slots[x] = both.astype(BF16)
            else:
                mid[to] = both.astype(BF16)
                remote(mid.at[to], slots.at[x], send.at[1, k], recv.at[1, k], x_peer(k)).start()
    else:
        for k in STEPS:
            remote(mid.at[mod(x + k, 4)], slots.at[mod(x + 4 - k, 4)], send.at[1, k], recv.at[1, k],
                   x_peer(k)).wait()


def spread(src, dst, send, recv, start):
    dp, ctx, t, x, y, z, core = place()
    for k in range(2):
        x_to = 2 * k + mod(y, 2)
        same = jnp.logical_and(x_to == x, x == y)
        slot = dst.at[div(y, 2), core]
        copy = remote(src, slot, send.at[k], recv.at[div(y, 2)], device(x_to, x, z, core))
        if start:
            @pl.when(jnp.logical_not(same))
            def _():
                copy.start()

            @pl.when(same)
            def _():
                pltpu.make_async_copy(src, slot, recv.at[div(y, 2)]).start()
        else:
            @pl.when(jnp.logical_not(same))
            def _():
                copy.wait_send()

            remote(src, dst.at[k, core], send.at[k], recv.at[k], (1 - dp, ctx, t)).wait_recv()


def tokens_target(k):
    dp, ctx, t, x, y, z, core = place()
    return device(k, x, z, core)


def tokens_source(k):
    dp, ctx, t, x, y, z, core = place()
    return device(y, k, z, core)


def ctx_peer(k):
    dp, ctx, t, x, y, z, core = place()
    return (dp, mod(ctx + k, 16), t)


INPUTS = dict(lat=0, cond=1, ada=2, ada_bias=3, qkv=4, qv=5, wo=6, ob=7, w1=8, b1=9, w2=10, b2=11, cot=12)
OUTPUTS = dict(
    block_out=((2, 2, 32, 1024), BF16),
    grad_out=((2, 2, 32, 1024), BF16),
    cond_out=((2, 256), F32),
    ada_out=((192, 256), F32),
    ada_bias_out=((1, 6144), F32),
    ga_out=((2, 32, 384), F32),
    gb_out=((2, 32, 1024), F32),
    gc_out=((2, 32, 128), F32),
    bias_out=((2, 1, 1024), F32),
    wide_out=((2, 1024), F32),
)
RING = ((4, 2, 32, 1024), BF16)
FOUR = ((4, 32, 1024), BF16)
BUFFERS = dict(
    xg=RING, cg=RING,
    packa=((2, 32, 512), BF16), packb=((2, 32, 1024), BF16),
    wa=((2, 4, 4, 32, 512), BF16), wb=((2, 4, 4, 32, 1024), BF16),
    cond_a=((8, 256), F32), cond_b=((8, 256), F32), cond8=((8, 256), F32),
    part=((4, 256), F32), parts=((8, 4, 256), F32), pair=((4, 2, 256), F32),
    modg=((16, 2, 256), F32), flat=((1, 6144), F32),
    normed=((256, 1024), F32), hidden=((256, 1024), BF16),
    k_own=((256, 128), BF16), kg=((4, 256, 128), BF16),
    v_own=((256, 128), BF16), vg=((4, 256, 128), BF16), prob=((2, 256, 1024), F32),
    branch_part=RING, branch_half=FOUR, branch_mid=FOUR, branch_slots=FOUR,
    h2_own=((32, 1024), BF16), h2=RING,
    d_feed=((256, 1024), BF16), d_act=((256, 512), F32),
    dh2_part=RING, dh2_half=FOUR, dh2_mid=FOUR, dh2_slots=FOUR,
    feed_part=RING, feed_half=FOUR, feed_mid=FOUR, feed_slots=FOUR,
    db_own=((32, 1024), BF16), db=RING,
    block_own=((32, 1024), BF16), d_middle=((32, 1024), F32),
    dk_part=((4, 256, 128), BF16), dk_slots=((4, 256, 128), BF16),
    dv_part=((4, 256, 128), BF16), dv_slots=((4, 256, 128), BF16),
    dh_part=RING, dh_half=FOUR, dh_mid=FOUR, dh_slots=FOUR,
    grad_own=((32, 1024), BF16),
    m_own=((4, 1024), F32), m_slots=((8, 4, 1024), F32),
    z_own=((8, 1024), F32), z_slots=((4, 8, 1024), F32),
    y_own=((8, 1024), F32), y_slots=((4, 8, 1024), F32),
    n_own=((2, 1024), F32), n_slots=((8, 2, 1024), F32),
    l_own=((4, 1024), F32), l_slots=((16, 4, 1024), F32),
    dm=((8, 6144), F32), bias_own=((1, 1024), F32),
    cond_part=((4, 256), F32), cond_slots=((16, 4, 256), F32), cond_sum=((4, 256), F32), ada_b=((192, 256), BF16),
    ga=((2, 4, 4, 32, 384), BF16), ga1=((2, 4, 4, 32, 384), BF16),
    ga2=((2, 4, 32, 384), BF16), ga3=((2, 4, 32, 384), BF16),
    gb=((2, 4, 4, 32, 1024), BF16), gb1=((2, 4, 4, 32, 1024), BF16),
    gb2=((2, 4, 32, 1024), BF16), gb3=((2, 4, 32, 1024), BF16),
    gc=((2, 4, 4, 32, 128), BF16), gc1=((2, 4, 4, 32, 128), BF16),
    gc2=((2, 4, 32, 128), BF16), gc3=((2, 4, 32, 128), BF16),
)
SEMS = dict(
    s_cond=(), s_xg=(4,), s_xr=(), s_cg=(4,), s_cr=(),
    s_wa1=(2, 4), s_wa2=(2, 4), s_wb1=(2, 4), s_wb2=(2, 4),
    s_mod=(8,), s_mod2=(16,), s_k=(4,), s_v=(4,),
    s_branch=(2, 4), s_h2=(2, 4), s_dh2=(2, 4), s_feed=(2, 4), s_db=(2, 4),
    s_block=(2,), s_dk=(4,), s_dv=(4,), s_dh=(2, 4), s_grad=(2,), s_blockr=(), s_gradr=(), s_ada=(),
    s_m=(8,), s_z=(4,), s_y=(4,), s_n=(8,), s_l=(16,), s_bias=(), s_c=(16,),
    s_ga1=(2, 4), s_ga2=(2, 4), s_gb1=(2, 4), s_gb2=(2, 4), s_gc1=(2, 4), s_gc2=(2, 4),
)


class Refs:
    pass


def block_kernel(*refs):
    g = Refs()
    names = list(INPUTS) + list(OUTPUTS) + list(BUFFERS)
    for name, ref in zip(names, refs):
        setattr(g, name, ref)
    sems = refs[len(names):]
    for i, name in enumerate(SEMS):
        setattr(g, name, (sems[2 * i], sems[2 * i + 1]))
    dp, ctx, t, x, y, z, core = place()
    r = x * 2 + core
    partner = (1 - dp, ctx, t)

    greet([(1, 8, ring_peer), (1, 16, ctx_peer), (0, 4, tokens_target), (0, 4, tokens_source),
           (1, 4, cross_y), (1, 4, cross_z)])

    cond_slice = g.cond[:, pl.ds(pl.multiple_of(t * 256, 256), 256)].astype(F32)
    sigmoid = 1.0 / (1.0 + jnp.exp(-cond_slice))
    cond_act = (cond_slice * sigmoid).astype(BF16).astype(F32)
    rows = lax.broadcasted_iota(jnp.int32, (8, 256), 0)
    g.cond_a[...] = jnp.where(rows == dp, cond_act[0:1], jnp.where(rows == dp + 2, cond_act[1:2], 0.0))
    cond_copy = remote(g.cond_a, g.cond_b, *g.s_cond, partner)
    cond_copy.start()
    for h in range(2):
        for k in range(3):
            g.packa[h, :, 128 * k:128 * k + 128] = g.qkv[k, :, 128 * h:128 * h + 128]
        g.packa[h, :, 384:] = g.wo[:, 128 * h:128 * h + 128]
    plane_one(g.wa, g.packa, *g.s_wa1, True)
    tokens(g.lat, g.xg, *g.s_xg, True)
    cond_copy.wait()
    g.cond8[...] = g.cond_a[...] + g.cond_b[...]
    g.part[:, :192] = dot(g.cond8[...].astype(BF16), g.ada[...], NT)[:4]
    gather_start(g.part, g.parts, r, 8, ring_peer, *g.s_mod)
    g.parts[r] = g.part[...]
    for h in range(2):
        g.packb[h, :, :512] = g.w1[0, :, 512 * h:512 * h + 512]
        g.packb[h, :, 512:] = g.w2[:, 512 * h:512 * h + 512]
    gather_wait(g.part, g.parts, r, 8, ring_peer, *g.s_mod)
    for c in range(2):
        both = (g.parts[2 * c] + g.parts[2 * c + 1]) + (g.parts[2 * c + 4] + g.parts[2 * c + 5])
        for i in range(4):
            g.pair[i, c:c + 1, :192] = both[i:i + 1, :192]

    def mod_start(k, carry):
        remote(g.pair.at[mod(ctx + k, 4)], g.modg.at[ctx], g.s_mod2[0].at[k], g.s_mod2[1].at[ctx],
               ctx_peer(k)).start()
        return carry
    loop(1, 16, mod_start)
    g.modg[ctx] = g.pair[y]
    tokens(g.lat, g.xg, *g.s_xg, False)
    relay(g.xg, *g.s_xr, True)
    plane_one(g.wa, g.packa, *g.s_wa1, False)
    plane_two(g.wa, *g.s_wa2, True)
    relay(g.xg, *g.s_xr, False)
    normed, _ = normalize(g.xg[...].astype(F32).reshape(256, 1024))
    g.normed[...] = normed
    plane_one(g.wb, g.packb, *g.s_wb1, True)
    ada_copy = remote(g.ada, g.ada_b, *g.s_ada, partner)
    ada_copy.start()

    def mod_wait(k, carry):
        other = mod(ctx + k, 16)
        remote(g.pair.at[0], g.modg.at[other], g.s_mod2[0].at[k], g.s_mod2[1].at[other],
               ctx_peer(k)).wait()
        return carry
    loop(1, 16, mod_wait)
    for p in range(16):
        c, first = div(p, 8), mod(2 * p, 16)
        both = jnp.concatenate(
            [g.modg[first, c:c + 1, :192], g.modg[first + 1, c:c + 1, :192]], axis=1)
        g.flat[:, 384 * p:384 * p + 384] = both + g.ada_bias[:, 384 * p:384 * p + 384].astype(F32)
    shift1, scale1, gate1, shift2, scale2, gate2 = [
        g.flat[:, k * 1024:(k + 1) * 1024] for k in range(6)]
    hidden = (g.normed[...] * (1.0 + scale1) + shift1).astype(BF16)
    g.hidden[...] = hidden
    plane_two(g.wa, *g.s_wa2, False)
    mixed = dot(hidden, g.wa[:, :, :, :, :384].reshape(1024, 384), NN)
    qv = g.qv[0, :, pl.ds(pl.multiple_of(dp * 128, 128), 128)].astype(F32)
    g.k_own[...] = mixed[:, 128:256].astype(BF16)
    gather_start(g.k_own, g.kg, z, 4, z_peer, *g.s_k)
    g.v_own[...] = (mixed[:, 256:] + qv[1:2]).astype(BF16)
    gather_start(g.v_own, g.vg, z, 4, z_peer, *g.s_v)
    query = (mixed[:, :128] + qv[0:1]).astype(BF16)
    g.kg[z] = g.k_own[...]
    g.vg[z] = g.v_own[...]
    tokens(g.cot, g.cg, *g.s_cg, True)
    gather_wait(g.k_own, g.kg, z, 4, z_peer, *g.s_k)
    plane_one(g.wb, g.packb, *g.s_wb1, False)
    plane_two(g.wb, *g.s_wb2, True)
    for h in range(2):
        key = g.kg[:, :, 64 * h:64 * h + 64].reshape(1024, 64)
        scores = dot(query[:, 64 * h:64 * h + 64], key, NT) * SCALE
        expo = jnp.exp(scores - jnp.max(scores, axis=-1, keepdims=True))
        g.prob[h] = expo / jnp.sum(expo, axis=-1, keepdims=True)
    gather_wait(g.v_own, g.vg, z, 4, z_peer, *g.s_v)
    heads = []
    for h in range(2):
        value = g.vg[:, :, 64 * h:64 * h + 64].reshape(1024, 64)
        heads.append(dot(g.prob[h].astype(BF16), value, NN))
    attended = jnp.concatenate(heads, axis=1).astype(BF16)
    w_out = g.wa[:, :, :, :, 384:].reshape(1024, 128)
    g.branch_part[...] = dot(attended, w_out, NT).astype(BF16).reshape(4, 2, 32, 1024)
    branch_ring = (g.branch_part, g.branch_half, g.branch_mid, g.branch_slots, *g.s_branch)
    ring_scatter(*branch_ring, 0)
    ring_scatter(*branch_ring, 1)
    tokens(g.cot, g.cg, *g.s_cg, False)
    relay(g.cg, *g.s_cr, True)
    relay(g.cg, *g.s_cr, False)
    d_feed = (g.cg[...].astype(F32).reshape(256, 1024) * gate2).astype(BF16)
    g.d_feed[...] = d_feed
    g.z_own[...] = jnp.zeros_like(g.z_own)
    g.z_own[5:6] = jnp.sum(d_feed.astype(F32), axis=0, keepdims=True)
    ring_scatter(*branch_ring, 2)

    x_own = g.xg[x, core].astype(F32)
    branch = jnp.sum(g.branch_slots[...].astype(F32), axis=0) + g.ob[...].astype(F32)
    middle = x_own + gate1 * branch
    normed_two, inverse_two = normalize(middle)
    g.h2_own[...] = (normed_two * (1.0 + scale2) + shift2).astype(BF16)
    ring_gather(g.h2_own, g.h2, *g.s_h2, True)
    plane_two(g.wb, *g.s_wb2, False)
    w_second = g.wb[:, :, :, :, 512:].reshape(1024, 512)
    g.d_act[...] = dot(d_feed, w_second, NN)
    ring_gather(g.h2_own, g.h2, *g.s_h2, False)

    hidden_two = g.h2[...].reshape(256, 1024)
    w_first = g.wb[:, :, :, :, :512].reshape(1024, 512)
    bias_first = g.b1[:, pl.ds(pl.multiple_of(dp * 512, 512), 512)].astype(F32)
    before = dot(hidden_two, w_first, NN) + bias_first
    square = before * before
    tanh = jnp.tanh(ROOT * before * (1.0 + 0.044715 * square))
    slope = 0.5 * (1.0 + tanh) + (0.5 * ROOT) * before * (1.0 - tanh * tanh) * (
        1.0 + (3.0 * 0.044715) * square)
    d_before = (g.d_act[...] * slope).astype(BF16)
    g.dh2_part[...] = dot(d_before, w_first, NT).astype(BF16).reshape(4, 2, 32, 1024)
    dh2_ring = (g.dh2_part, g.dh2_half, g.dh2_mid, g.dh2_slots, *g.s_dh2)
    ring_scatter(*dh2_ring, 0)
    activated = (0.5 * before * (1.0 + tanh)).astype(BF16)
    ring_scatter(*dh2_ring, 1)
    feed_part = dot(activated, w_second, NT)
    g.feed_part[...] = feed_part.astype(BF16).reshape(4, 2, 32, 1024)
    g.gb[:, :, :, :, :512] = dot(hidden_two, d_before, TN).astype(BF16).reshape(2, 4, 4, 32, 512)
    g.gb[:, :, :, :, 512:] = dot(d_feed, activated, TN).astype(BF16).reshape(2, 4, 4, 32, 512)
    reduce_one(g.gb, g.gb1, *g.s_gb1, True)
    g.m_own[3:4] = jnp.sum(
        g.cg[...].astype(F32).reshape(256, 1024) * feed_part, axis=0, keepdims=True)
    g.z_own[6:7, :512] = jnp.sum(d_before.astype(F32), axis=0, keepdims=True)
    ring_scatter(*dh2_ring, 2)

    cot_own = g.cg[x, core].astype(F32)
    d_hidden = jnp.sum(g.dh2_slots[...].astype(F32), axis=0)
    d_middle = cot_own + norm_back(d_hidden * (1.0 + scale2), normed_two, inverse_two)
    g.d_middle[...] = d_middle
    g.db_own[...] = (d_middle * gate1).astype(BF16)
    ring_gather(g.db_own, g.db, *g.s_db, True)
    feed_ring = (g.feed_part, g.feed_half, g.feed_mid, g.feed_slots, *g.s_feed)
    ring_scatter(*feed_ring, 0)
    g.m_own[0:1] = jnp.sum(d_middle * branch, axis=0, keepdims=True)
    g.m_own[1:2] = jnp.sum(d_hidden, axis=0, keepdims=True)
    g.m_own[2:3] = jnp.sum(d_hidden * normed_two, axis=0, keepdims=True)
    g.m_own[3:4] += jnp.sum(cot_own, axis=0, keepdims=True) * g.b2[...].astype(F32)
    gather_start(g.m_own, g.m_slots, r, 8, ring_peer, *g.s_m)
    g.m_slots[r] = g.m_own[...]
    ring_gather(g.db_own, g.db, *g.s_db, False)
    ring_scatter(*feed_ring, 1)

    d_branch = g.db[...].reshape(256, 1024)
    g.gc[...] = dot(d_branch, attended, TN).astype(BF16).reshape(2, 4, 4, 32, 128)
    reduce_one(g.gc, g.gc1, *g.s_gc1, True)
    d_attended = dot(d_branch, w_out, NN).astype(BF16)
    d_one = [d_attended[:, 64 * h:64 * h + 64] for h in range(2)]
    d_value = [dot(g.prob[h].astype(BF16), d_one[h], TN) for h in range(2)]
    g.dv_part[...] = jnp.concatenate(d_value, axis=1).astype(BF16).reshape(4, 256, 128)
    scatter_start(g.dv_part, g.dv_slots, z, 4, z_peer, *g.s_dv)
    g.dv_slots[z] = g.dv_part[z]
    d_query, d_key = [], []
    for h in range(2):
        key = g.kg[:, :, 64 * h:64 * h + 64].reshape(1024, 64)
        value = g.vg[:, :, 64 * h:64 * h + 64].reshape(1024, 64)
        prob = g.prob[h]
        d_prob = dot(d_one[h], value, NT)
        d_scores = (prob * (d_prob - jnp.sum(prob * d_prob, axis=-1, keepdims=True))).astype(BF16)
        d_key.append(dot(d_scores, query[:, 64 * h:64 * h + 64], TN) * SCALE)
        d_query.append(dot(d_scores, key, NN) * SCALE)
    g.dk_part[...] = jnp.concatenate(d_key, axis=1).astype(BF16).reshape(4, 256, 128)
    scatter_start(g.dk_part, g.dk_slots, z, 4, z_peer, *g.s_dk)
    g.dk_slots[z] = g.dk_part[z]
    d_query = jnp.concatenate(d_query, axis=1).astype(BF16)
    g.z_own[4:5] = jnp.sum(d_branch.astype(F32), axis=0, keepdims=True)
    g.z_own[6:7, 512:640] = jnp.sum(d_query.astype(F32), axis=0, keepdims=True)
    gather_wait(g.m_own, g.m_slots, r, 8, ring_peer, *g.s_m)
    g.z_own[0:4] = jnp.sum(g.m_slots[...], axis=0)
    gather_start(g.z_own, g.z_slots, z, 4, z_peer, *g.s_z)
    g.z_slots[z] = g.z_own[...]
    ring_scatter(*feed_ring, 2)
    feed = jnp.sum(g.feed_slots[...].astype(F32), axis=0) + g.b2[...].astype(F32)
    g.block_own[...] = (middle + gate2 * feed).astype(BF16)
    spread(g.block_own, g.block_out, *g.s_block, True)
    reduce_one(g.gb, g.gb1, *g.s_gb1, False)
    add_slots(g.gb1, g.gb2)
    reduce_two(g.gb2, g.gb3, *g.s_gb2, True)
    scatter_wait(g.dv_part, g.dv_slots, z, 4, z_peer, *g.s_dv)
    scatter_wait(g.dk_part, g.dk_slots, z, 4, z_peer, *g.s_dk)

    d_keys = jnp.sum(g.dk_slots[...].astype(F32), axis=0).astype(BF16)
    d_values = jnp.sum(g.dv_slots[...].astype(F32), axis=0).astype(BF16)
    d_qkv = jnp.concatenate([d_query, d_keys, d_values], axis=1)
    d_part = dot(d_qkv, g.wa[:, :, :, :, :384].reshape(1024, 384), NT)
    g.dh_part[...] = d_part.astype(BF16).reshape(4, 2, 32, 1024)
    dh_ring = (g.dh_part, g.dh_half, g.dh_mid, g.dh_slots, *g.s_dh)
    ring_scatter(*dh_ring, 0)
    g.ga[...] = dot(g.hidden[...], d_qkv, TN).astype(BF16).reshape(2, 4, 4, 32, 384)
    reduce_one(g.ga, g.ga1, *g.s_ga1, True)
    g.n_own[0:1] = jnp.sum(d_part, axis=0, keepdims=True)
    g.n_own[1:2] = jnp.sum(d_part * g.normed[...], axis=0, keepdims=True)
    gather_start(g.n_own, g.n_slots, r, 8, ring_peer, *g.s_n)
    g.n_slots[r] = g.n_own[...]
    ring_scatter(*dh_ring, 1)
    gather_wait(g.z_own, g.z_slots, z, 4, z_peer, *g.s_z)
    g.y_own[...] = jnp.sum(g.z_slots[...], axis=0)
    gather_start(g.y_own, g.y_slots, y, 4, y_peer, *g.s_y)
    g.y_slots[y] = g.y_own[...]
    reduce_one(g.gc, g.gc1, *g.s_gc1, False)
    add_slots(g.gc1, g.gc2)
    reduce_two(g.gc2, g.gc3, *g.s_gc2, True)
    gather_wait(g.n_own, g.n_slots, r, 8, ring_peer, *g.s_n)
    g.l_own[0:2] = jnp.sum(g.n_slots[...], axis=0)
    g.l_own[2:4] = jnp.zeros((2, 1024), F32)
    g.l_own[2:3, :128] = jnp.sum(d_values.astype(F32), axis=0, keepdims=True)
    gather_start(g.l_own, g.l_slots, ctx, 16, ctx_peer, *g.s_l)
    g.l_slots[ctx] = g.l_own[...]
    ring_scatter(*dh_ring, 2)

    x_normed, x_inverse = normalize(x_own)
    d_hidden = jnp.sum(g.dh_slots[...].astype(F32), axis=0)
    grad = g.d_middle[...] + norm_back(d_hidden * (1.0 + scale1), x_normed, x_inverse)
    g.grad_own[...] = grad.astype(BF16)
    spread(g.grad_own, g.grad_out, *g.s_grad, True)
    reduce_one(g.ga, g.ga1, *g.s_ga1, False)
    add_slots(g.ga1, g.ga2)
    reduce_two(g.ga2, g.ga3, *g.s_ga2, True)
    g.dm[...] = jnp.zeros_like(g.dm)
    gather_wait(g.y_own, g.y_slots, y, 4, y_peer, *g.s_y)
    for k in range(2, 6):
        for i in range(4):
            g.dm[i:i + 1, k * 1024:(k + 1) * 1024] = g.y_slots[i, k - 2:k - 1]
    gather_wait(g.l_own, g.l_slots, ctx, 16, ctx_peer, *g.s_l)

    late = jnp.sum(g.l_slots[...].reshape(4, 4, 4, 1024), axis=0)
    for k in range(2):
        for i in range(4):
            g.dm[i:i + 1, k * 1024:(k + 1) * 1024] = late[i, k:k + 1]

    def columns(chunk):
        wide = g.dm[:, pl.ds(pl.multiple_of(div(3 * chunk, 2) * 128, 128), 256)]
        return jnp.where(mod(chunk, 2) == 1, pltpu.roll(wide, 192, 1), wide)[:, :192]

    own_columns = columns(dp * 16 + ctx)
    ada_copy.wait()
    highest = lax.Precision.HIGHEST
    g.cond_part[...] = (
        dot_split(own_columns, g.ada[...]) + dot_split(columns((1 - dp) * 16 + ctx), g.ada_b[...]))[:4]
    gather_start(g.cond_part, g.cond_slots, ctx, 16, ctx_peer, *g.s_c)
    g.cond_slots[ctx] = g.cond_part[...]
    early = jnp.sum(g.y_slots[...], axis=0)
    g.wide_out[...] = early[4:6]
    g.bias_own[:, :640] = early[6:7, :640]
    g.bias_own[:, 640:768] = jnp.sum(late[:, 2], axis=0, keepdims=True)[:, :128]
    g.bias_own[:, 768:] = jnp.zeros((1, 256), F32)
    remote(g.bias_own, g.bias_out.at[dp], *g.s_bias, partner).start()
    g.bias_out[dp] = g.bias_own[...]
    g.ada_bias_out[...] = jnp.sum(g.dm[...], axis=0, keepdims=True)
    spread(g.block_own, g.block_out, *g.s_block, False)
    relay(g.block_out, *g.s_blockr, True)
    reduce_two(g.gb2, g.gb3, *g.s_gb2, False)
    add_slots(g.gb3, g.gb_out)
    reduce_two(g.gc2, g.gc3, *g.s_gc2, False)
    add_slots(g.gc3, g.gc_out)
    spread(g.grad_own, g.grad_out, *g.s_grad, False)
    relay(g.grad_out, *g.s_gradr, True)
    g.ada_out[...] = dot(own_columns, g.cond8[...], TN, highest)
    reduce_two(g.ga2, g.ga3, *g.s_ga2, False)
    add_slots(g.ga3, g.ga_out)
    gather_wait(g.cond_part, g.cond_slots, ctx, 16, ctx_peer, *g.s_c)
    g.cond_sum[...] = jnp.sum(g.cond_slots[...], axis=0)
    slope = sigmoid * (1.0 + cond_slice * (1.0 - sigmoid))
    for i in range(2):
        g.cond_out[i:i + 1] = g.cond_sum[pl.ds(2 * i + dp, 1)] * slope[i:i + 1]
    remote(g.bias_own, g.bias_out.at[1 - dp], *g.s_bias, partner).wait()
    relay(g.block_out, *g.s_blockr, False)
    relay(g.grad_out, *g.s_gradr, False)


def unpack_kernel(block, grad, cond, ada, ada_bias, ga, gb, gc, bias, wide,
                  block_out, grad_out, cond_out, ada_out, ada_bias_out, qkv_out, qv_out,
                  wo_out, ob_out, w1_out, b1_out, w2_out, b2_out):
    block_out[...] = block[...].reshape(2, 64, 1024)
    grad_out[...] = grad[...].astype(F32).reshape(2, 64, 1024)
    cond_out[...] = cond[...]
    ada_out[...] = ada[...]
    ada_bias_out[...] = ada_bias[...]
    for h in range(2):
        for k in range(3):
            qkv_out[k, :, 128 * h:128 * h + 128] = ga[h, :, 128 * k:128 * k + 128]
        for k in range(2):
            qv_out[0, k:k + 1, 128 * h:128 * h + 128] = bias[h, :, 512 + 128 * k:640 + 128 * k]
        wo_out[:, 128 * h:128 * h + 128] = gc[h]
        w1_out[0, :, 512 * h:512 * h + 512] = gb[h, :, :512]
        w2_out[:, 512 * h:512 * h + 512] = gb[h, :, 512:]
        b1_out[:, 512 * h:512 * h + 512] = bias[h, :, :512]
    ob_out[...] = wide[0:1]
    b2_out[...] = wide[1:2]


def on_device(
    latents, cond, ada_weight, ada_bias, qkv_weight, qv_bias, out_weight, out_bias,
    first_weight, first_bias, second_weight, second_bias, cotangent,
):
    args = [
        latents, cond, ada_weight[0].T, ada_bias, qkv_weight[0].transpose(1, 0, 2), qv_bias,
        out_weight[0].T, out_bias, first_weight, first_bias, second_weight[0].T, second_bias,
        cotangent,
    ]
    outs = pl.pallas_call(
        block_kernel,
        out_shape=[shape(*one) for one in OUTPUTS.values()],
        in_specs=[VMEM] * len(args),
        out_specs=[VMEM] * len(OUTPUTS),
        scratch_shapes=[pltpu.VMEM(*one) for one in BUFFERS.values()]
        + [DMA(one) for one in SEMS.values() for _ in range(2)],
        compiler_params=pltpu.CompilerParams(
            collective_id=1, has_side_effects=True, vmem_limit_bytes=56 << 20
        ),
        name="block",
    )(*args)
    final = [
        shape((2, 64, 1024), BF16), shape((2, 64, 1024), F32), shape((2, 256), F32),
        shape((192, 256), F32), shape((1, 6144), F32), shape((3, 32, 256), F32),
        shape((1, 2, 256), F32), shape((32, 256), F32), shape((1, 1024), F32),
        shape((1, 32, 1024), F32), shape((1, 1024), F32), shape((32, 1024), F32),
        shape((1, 1024), F32),
    ]
    results = pl.pallas_call(
        unpack_kernel, out_shape=final, in_specs=[VMEM] * len(outs), out_specs=[VMEM] * len(final),
        name="unpack",
    )(*outs)
    results = list(results)
    for k in (3, 7, 11):
        results[k] = results[k].T[None]
    results[5] = results[5].transpose(1, 0, 2)[None]
    return tuple(results)


def solution(mesh):
    return jax.shard_map(
        on_device,
        mesh=mesh,
        in_specs=(
            P("dp", "context", None),
            P("dp", None),
            P(None, "tensor", ("dp", "context")),
            P(),
            P(None, ("dp", "context"), None, "tensor"),
            P(None, None, "tensor"),
            P(None, "tensor", ("dp", "context")),
            P(),
            P(None, ("dp", "context"), "tensor"),
            P(None, "tensor"),
            P(None, "tensor", ("dp", "context")),
            P(),
            P("dp", "context", None),
        ),
        out_specs=(
            P("dp", "context", None),
            P("dp", "context", None),
            P("dp", "tensor"),
            P(None, "tensor", ("dp", "context")),
            P(),
            P(None, ("dp", "context"), None, "tensor"),
            P(None, None, "tensor"),
            P(None, "tensor", ("dp", "context")),
            P(),
            P(None, ("dp", "context"), "tensor"),
            P(None, "tensor"),
            P(None, "tensor", ("dp", "context")),
            P(),
        ),
        check_vma=False,
    )
```

```python
import math

import jax
import jax.numpy as jnp
from jax import lax
from jax.experimental import pallas as pl
from jax.experimental.pallas import tpu as pltpu
from jax.sharding import PartitionSpec as P

EPSILON = 1e-06
F32 = jnp.float32
BF16 = jnp.bfloat16
MESH = pl.DeviceIdType.MESH
VMEM = pl.BlockSpec(memory_space=pltpu.VMEM)
DMA = pltpu.SemaphoreType.DMA


def mod(a, b):
    return a % b if isinstance(a, int) else lax.rem(a, jnp.int32(b))


def div(a, b):
    return a // b if isinstance(a, int) else lax.div(a, jnp.int32(b))


def place():
    dp = lax.axis_index("dp")
    ctx = lax.axis_index("context")
    t = lax.axis_index("tensor")
    return dp, ctx, t, div(t, 2) * 2 + dp, mod(ctx, 4), div(ctx, 4), mod(t, 2)


def loop(first, last, one):
    for k in range(first, last):
        one(k, 0)


def device(x, y, z, core):
    return (mod(x, 2), z * 4 + y, div(x, 2) * 2 + core)


def remote(src, dst, send, recv, target):
    return pltpu.make_async_remote_copy(
        src_ref=src, dst_ref=dst, send_sem=send, recv_sem=recv,
        device_id=target, device_id_type=MESH,
    )


def greet(targets):
    barrier = pltpu.get_barrier_semaphore()
    count = 0
    for first, last, target in targets:
        def one(k, carry, target=target):
            pl.semaphore_signal(barrier, inc=1, device_id=target(k), device_id_type=MESH)
            return carry
        loop(first, last, one)
        count += last - first
    pl.semaphore_wait(barrier, count)


def z_peer(k):
    dp, ctx, t, x, y, z, core = place()
    return (dp, mod(z + k, 4) * 4 + y, t)


def y_peer(k):
    dp, ctx, t, x, y, z, core = place()
    return (dp, z * 4 + mod(y + k, 4), t)


def x_peer(k):
    dp, ctx, t, x, y, z, core = place()
    return device(mod(x + k, 4), y, z, core)


def sibling():
    dp, ctx, t, x, y, z, core = place()
    return device(x, y, z, 1 - core)


def ring_peer(k):
    dp, ctx, t, x, y, z, core = place()
    r = mod(x * 2 + core + k, 8)
    return device(div(r, 2), y, z, mod(r, 2))


def gather_start(own, slots, mine, n, peer, send, recv):
    def one(k, carry):
        remote(own, slots.at[mine], send.at[k], recv.at[mine], peer(k)).start()
        return carry
    loop(1, n, one)


def gather_wait(own, slots, mine, n, peer, send, recv):
    def one(k, carry):
        other = mod(mine + k, n)
        copy = remote(own, slots.at[other], send.at[k], recv.at[other], peer(k))
        copy.wait_recv()
        copy.wait_send()
        return carry
    loop(1, n, one)


def scatter_start(parts, slots, mine, n, peer, send, recv):
    def one(k, carry):
        other = mod(mine + k, n)
        remote(parts.at[other], slots.at[mine], send.at[k], recv.at[mine], peer(k)).start()
        return carry
    loop(1, n, one)


def scatter_wait(parts, slots, mine, n, peer, send, recv):
    def one(k, carry):
        other = mod(mine + k, n)
        copy = remote(parts.at[other], slots.at[other], send.at[k], recv.at[other], peer(k))
        copy.wait_recv()
        copy.wait_send()
        return carry
    loop(1, n, one)


def shape(dims, dtype):
    return jax.ShapeDtypeStruct(dims, dtype)


def normalize(values):
    center = values - jnp.mean(values, axis=-1, keepdims=True)
    inverse = lax.rsqrt(jnp.mean(center * center, axis=-1, keepdims=True) + EPSILON)
    return center * inverse, inverse


def norm_back(grad_hat, normed, inverse):
    first = jnp.mean(grad_hat, axis=-1, keepdims=True)
    second = jnp.mean(grad_hat * normed, axis=-1, keepdims=True)
    return inverse * (grad_hat - first - normed * second)


def dot(left, right, contract, precision=None):
    return lax.dot_general(
        left, right, (contract, ((), ())), precision=precision, preferred_element_type=F32
    )


def dot_split(left, right):
    high = left.astype(BF16)
    rest = left - high.astype(F32)
    middle = rest.astype(BF16)
    low = (rest - middle.astype(F32)).astype(BF16)
    out = dot(jnp.concatenate([high, middle, low], axis=0), right, NN)
    n = left.shape[0]
    return out[:n] + (out[n:2 * n] + out[2 * n:])


NN = ((1,), (0,))
NT = ((1,), (1,))
TN = ((0,), (0,))
SCALE = 1.0 / math.sqrt(64)
ROOT = math.sqrt(2.0 / math.pi)
STEPS = (1, 3, 2)


def from_back(k):
    y, z = mod(lax.axis_index("context"), 4), div(lax.axis_index("context"), 4)
    return mod(y + 4 - k, 4), mod(z + 4 - k, 4)


def line_target(to, h, k):
    dp, ctx, t, x, y, z, core = place()
    return (to, mod(z + h * k, 4) * 4 + mod(y + (1 - h) * k, 4), t)


def cross_y(k):
    return line_target(1 - lax.axis_index("dp"), 0, k)


def cross_z(k):
    return line_target(1 - lax.axis_index("dp"), 1, k)


def plane_one(full, pack, send, recv, start):
    dp, ctx, t, x, y, z, core = place()
    for side, order in ((0, STEPS), (1, (2, 1, 3, 0))):
        to = dp if side == 0 else 1 - dp
        for k in order:
            target = line_target(to, dp, k)
            if start:
                remote(pack.at[to], full.at[dp, z, y], send.at[side, k], recv.at[side, k],
                       target).start()
            else:
                slot = full.at[to, mod(z + to * (4 - k), 4), mod(y + (1 - to) * (4 - k), 4)]
                remote(pack.at[to], slot, send.at[side, k], recv.at[side, k], target).wait()
    if start:
        full[dp, z, y] = pack[dp]


def plane_two(full, send, recv, start):
    dp, ctx, t, x, y, z, core = place()
    for k in STEPS:
        by, bz = from_back(k)
        row, column = full.at[0, z], full.at[1, :, y]
        if start:
            remote(row, row, send.at[0, k], recv.at[0, k], z_peer(k)).start()
            remote(column, column, send.at[1, k], recv.at[1, k], y_peer(k)).start()
        else:
            remote(row, full.at[0, bz], send.at[0, k], recv.at[0, k], z_peer(k)).wait()
            remote(column, full.at[1, :, by], send.at[1, k], recv.at[1, k], y_peer(k)).wait()


def reduce_one(parts, slots, send, recv, start):
    dp, ctx, t, x, y, z, core = place()
    for k in STEPS:
        by, bz = from_back(k)
        row, column = parts.at[0, mod(z + k, 4)], parts.at[1, :, mod(y + k, 4)]
        to_row = slots.at[0, z if start else bz]
        to_column = slots.at[1, y if start else by]
        for copy in (remote(row, to_row, send.at[0, k], recv.at[0, k], z_peer(k)),
                     remote(column, to_column, send.at[1, k], recv.at[1, k], y_peer(k))):
            copy.start() if start else copy.wait()
    if start:
        slots[0, z] = parts[0, z]
        slots[1, y] = parts[1, :, y]


def reduce_two(parts, slots, send, recv, start):
    dp, ctx, t, x, y, z, core = place()
    for side, order in ((0, STEPS), (1, (2, 1, 3, 0))):
        to = dp if side == 0 else 1 - dp
        at = y * (1 - to) + z * to
        mine = y * (1 - dp) + z * dp
        for k in order:
            slot = slots.at[dp, at] if start else slots.at[to, mod(mine + 4 - k, 4)]
            copy = remote(parts.at[to, mod(at + k, 4)], slot, send.at[side, k], recv.at[side, k],
                          line_target(to, to, k))
            copy.start() if start else copy.wait()
        if start and side == 0:
            slots[dp, at] = parts[dp, at]


def add_slots(slots, out):
    for h in range(2):
        total = slots[h, 0].astype(F32)
        for k in range(1, 4):
            total = total + slots[h, k].astype(F32)
        out[h] = total.astype(out.dtype)


def tokens(src, dst, send, recv, start):
    dp, ctx, t, x, y, z, core = place()
    own = src.at[div(t, 2), pl.ds(pl.multiple_of(core * 32, 32), 32)]
    for other in range(4):
        same = jnp.logical_and(x == y, x == other)
        copy = remote(own, dst.at[y, core], send.at[other], recv.at[y], device(other, x, z, core))
        if start:
            @pl.when(jnp.logical_not(same))
            def _():
                copy.start()

            @pl.when(same)
            def _():
                pltpu.make_async_copy(own, dst.at[y, core], recv.at[y]).start()
        else:
            @pl.when(jnp.logical_not(same))
            def _():
                copy.wait_send()

            remote(own, dst.at[other, core], send.at[other], recv.at[other],
                   (1 - dp, ctx, t)).wait_recv()


def relay(dst, send, recv, start):
    dp, ctx, t, x, y, z, core = place()
    mine = dst.at[:, core]
    if start:
        remote(mine, mine, send, recv, sibling()).start()
    else:
        remote(mine, dst.at[:, 1 - core], send, recv, sibling()).wait()


def ring_gather(own, slots, send, recv, start):
    dp, ctx, t, x, y, z, core = place()
    if start:
        for k in (2, 1, 3):
            remote(own, slots.at[x, core], send.at[0, k], recv.at[0, k], x_peer(k)).start()
        remote(own, slots.at[x, core], send.at[1, 0], recv.at[1, 0], sibling()).start()
        slots[x, core] = own[...]
        return
    for k in STEPS:
        slot = slots.at[mod(x + 4 - k, 4), core]
        remote(own, slot, send.at[0, k], recv.at[0, k], x_peer(k)).wait()
        remote(slot, slot, send.at[1, k], recv.at[1, k], sibling()).start()
    for k in (0,) + STEPS:
        slot = slots.at[mod(x + 4 - k, 4), 1 - core]
        remote(slot, slot, send.at[1, k], recv.at[1, k], sibling()).wait()


def ring_scatter(parts, halves, mid, slots, send, recv, step):
    dp, ctx, t, x, y, z, core = place()
    order = (2, 1, 3, 0)
    if step == 0:
        for k in order:
            to = mod(x + k, 4)
            remote(parts.at[to, 1 - core], halves.at[to], send.at[0, k], recv.at[0, k],
                   sibling()).start()
    elif step == 1:
        for k in order:
            to = mod(x + k, 4)
            remote(parts.at[to, 1 - core], halves.at[to], send.at[0, k], recv.at[0, k],
                   sibling()).wait()
            both = parts[to, core].astype(F32) + halves[to].astype(F32)
            if k == 0:
                slots[x] = both.astype(BF16)
            else:
                mid[to] = both.astype(BF16)
                remote(mid.at[to], slots.at[x], send.at[1, k], recv.at[1, k], x_peer(k)).start()
    else:
        for k in STEPS:
            remote(mid.at[mod(x + k, 4)], slots.at[mod(x + 4 - k, 4)], send.at[1, k], recv.at[1, k],
                   x_peer(k)).wait()


def spread(src, dst, send, recv, start):
    dp, ctx, t, x, y, z, core = place()
    for k in range(2):
        x_to = 2 * k + mod(y, 2)
        same = jnp.logical_and(x_to == x, x == y)
        slot = dst.at[div(y, 2), core]
        copy = remote(src, slot, send.at[k], recv.at[div(y, 2)], device(x_to, x, z, core))
        if start:
            @pl.when(jnp.logical_not(same))
            def _():
                copy.start()

            @pl.when(same)
            def _():
                pltpu.make_async_copy(src, slot, recv.at[div(y, 2)]).start()
        else:
            @pl.when(jnp.logical_not(same))
            def _():
                copy.wait_send()

            remote(src, dst.at[k, core], send.at[k], recv.at[k], (1 - dp, ctx, t)).wait_recv()


def tokens_target(k):
    dp, ctx, t, x, y, z, core = place()
    return device(k, x, z, core)


def tokens_source(k):
    dp, ctx, t, x, y, z, core = place()
    return device(y, k, z, core)


def ctx_peer(k):
    dp, ctx, t, x, y, z, core = place()
    return (dp, mod(ctx + k, 16), t)


INPUTS = dict(lat=0, cond=1, ada=2, ada_bias=3, qkv=4, qv=5, wo=6, ob=7, w1=8, b1=9, w2=10, b2=11, cot=12)
OUTPUTS = dict(
    block_out=((2, 2, 32, 1024), BF16),
    grad_out=((2, 2, 32, 1024), BF16),
    cond_out=((2, 256), F32),
    ada_out=((192, 256), F32),
    ada_bias_out=((1, 6144), F32),
    ga_out=((2, 32, 384), F32),
    gb_out=((2, 32, 1024), F32),
    gc_out=((2, 32, 128), F32),
    bias_out=((2, 1, 1024), F32),
    wide_out=((2, 1024), F32),
)
RING = ((4, 2, 32, 1024), BF16)
FOUR = ((4, 32, 1024), BF16)
BUFFERS = dict(
    xg=RING, cg=RING,
    packa=((2, 32, 512), BF16), packb=((2, 32, 1024), BF16),
    wa=((2, 4, 4, 32, 512), BF16), wb=((2, 4, 4, 32, 1024), BF16),
    cond_a=((8, 256), F32), cond_b=((8, 256), F32), cond8=((8, 256), F32),
    part=((4, 256), F32), parts=((8, 4, 256), F32), pair=((4, 2, 256), F32),
    modg=((16, 2, 256), F32), flat=((1, 6144), F32),
    normed=((256, 1024), F32), hidden=((256, 1024), BF16),
    k_own=((256, 128), BF16), kg=((4, 256, 128), BF16),
    v_own=((256, 128), BF16), vg=((4, 256, 128), BF16), prob=((2, 256, 1024), F32),
    branch_part=RING, branch_half=FOUR, branch_mid=FOUR, branch_slots=FOUR,
    h2_own=((32, 1024), BF16), h2=RING,
    d_feed=((256, 1024), BF16), d_act=((256, 512), F32),
    dh2_part=RING, dh2_half=FOUR, dh2_mid=FOUR, dh2_slots=FOUR,
    feed_part=RING, feed_half=FOUR, feed_mid=FOUR, feed_slots=FOUR,
    db_own=((32, 1024), BF16), db=RING,
    block_own=((32, 1024), BF16), d_middle=((32, 1024), F32),
    dk_part=((4, 256, 128), BF16), dk_slots=((4, 256, 128), BF16),
    dv_part=((4, 256, 128), BF16), dv_slots=((4, 256, 128), BF16),
    dh_part=RING, dh_half=FOUR, dh_mid=FOUR, dh_slots=FOUR,
    grad_own=((32, 1024), BF16),
    m_own=((4, 1024), F32), m_slots=((8, 4, 1024), F32),
    z_own=((8, 1024), F32), z_slots=((4, 8, 1024), F32),
    y_own=((8, 1024), F32), y_slots=((4, 8, 1024), F32),
    n_own=((2, 1024), F32), n_slots=((8, 2, 1024), F32),
    l_own=((4, 1024), F32), l_slots=((16, 4, 1024), F32),
    dm=((8, 6144), F32), bias_own=((1, 1024), F32),
    cond_part=((4, 256), F32), cond_slots=((16, 4, 256), F32), cond_sum=((4, 256), F32), ada_b=((192, 256), BF16),
    ga=((2, 4, 4, 32, 384), BF16), ga1=((2, 4, 4, 32, 384), BF16),
    ga2=((2, 4, 32, 384), BF16), ga3=((2, 4, 32, 384), BF16),
    gb=((2, 4, 4, 32, 1024), BF16), gb1=((2, 4, 4, 32, 1024), BF16),
    gb2=((2, 4, 32, 1024), BF16), gb3=((2, 4, 32, 1024), BF16),
    gc=((2, 4, 4, 32, 128), BF16), gc1=((2, 4, 4, 32, 128), BF16),
    gc2=((2, 4, 32, 128), BF16), gc3=((2, 4, 32, 128), BF16),
)
SEMS = dict(
    s_cond=(), s_xg=(4,), s_xr=(), s_cg=(4,), s_cr=(),
    s_wa1=(2, 4), s_wa2=(2, 4), s_wb1=(2, 4), s_wb2=(2, 4),
    s_mod=(8,), s_mod2=(16,), s_k=(4,), s_v=(4,),
    s_branch=(2, 4), s_h2=(2, 4), s_dh2=(2, 4), s_feed=(2, 4), s_db=(2, 4),
    s_block=(2,), s_dk=(4,), s_dv=(4,), s_dh=(2, 4), s_grad=(2,), s_blockr=(), s_gradr=(), s_ada=(),
    s_m=(8,), s_z=(4,), s_y=(4,), s_n=(8,), s_l=(16,), s_bias=(), s_c=(16,),
    s_ga1=(2, 4), s_ga2=(2, 4), s_gb1=(2, 4), s_gb2=(2, 4), s_gc1=(2, 4), s_gc2=(2, 4),
)


class Refs:
    pass


def block_kernel(*refs):
    g = Refs()
    names = list(INPUTS) + list(OUTPUTS) + list(BUFFERS)
    for name, ref in zip(names, refs):
        setattr(g, name, ref)
    sems = refs[len(names):]
    for i, name in enumerate(SEMS):
        setattr(g, name, (sems[2 * i], sems[2 * i + 1]))
    dp, ctx, t, x, y, z, core = place()
    r = x * 2 + core
    partner = (1 - dp, ctx, t)

    greet([(1, 8, ring_peer), (1, 16, ctx_peer), (0, 4, tokens_target), (0, 4, tokens_source),
           (1, 4, cross_y), (1, 4, cross_z)])

    cond_slice = g.cond[:, pl.ds(pl.multiple_of(t * 256, 256), 256)].astype(F32)
    sigmoid = 1.0 / (1.0 + jnp.exp(-cond_slice))
    cond_act = (cond_slice * sigmoid).astype(BF16).astype(F32)
    rows = lax.broadcasted_iota(jnp.int32, (8, 256), 0)
    g.cond_a[...] = jnp.where(rows == dp, cond_act[0:1], jnp.where(rows == dp + 2, cond_act[1:2], 0.0))
    cond_copy = remote(g.cond_a, g.cond_b, *g.s_cond, partner)
    cond_copy.start()
    for h in range(2):
        for k in range(3):
            g.packa[h, :, 128 * k:128 * k + 128] = g.qkv[k, :, 128 * h:128 * h + 128]
        g.packa[h, :, 384:] = g.wo[:, 128 * h:128 * h + 128]
    plane_one(g.wa, g.packa, *g.s_wa1, True)
    tokens(g.lat, g.xg, *g.s_xg, True)
    cond_copy.wait()
    g.cond8[...] = g.cond_a[...] + g.cond_b[...]
    g.part[:, :192] = dot(g.cond8[...].astype(BF16), g.ada[...], NT)[:4]
    gather_start(g.part, g.parts, r, 8, ring_peer, *g.s_mod)
    g.parts[r] = g.part[...]
    for h in range(2):
        g.packb[h, :, :512] = g.w1[0, :, 512 * h:512 * h + 512]
        g.packb[h, :, 512:] = g.w2[:, 512 * h:512 * h + 512]
    gather_wait(g.part, g.parts, r, 8, ring_peer, *g.s_mod)
    for c in range(2):
        both = (g.parts[2 * c] + g.parts[2 * c + 1]) + (g.parts[2 * c + 4] + g.parts[2 * c + 5])
        for i in range(4):
            g.pair[i, c:c + 1, :192] = both[i:i + 1, :192]

    def mod_start(k, carry):
        remote(g.pair.at[mod(ctx + k, 4)], g.modg.at[ctx], g.s_mod2[0].at[k], g.s_mod2[1].at[ctx],
               ctx_peer(k)).start()
        return carry
    loop(1, 16, mod_start)
    g.modg[ctx] = g.pair[y]
    tokens(g.lat, g.xg, *g.s_xg, False)
    relay(g.xg, *g.s_xr, True)
    plane_one(g.wa, g.packa, *g.s_wa1, False)
    plane_two(g.wa, *g.s_wa2, True)
    relay(g.xg, *g.s_xr, False)
    normed, _ = normalize(g.xg[...].astype(F32).reshape(256, 1024))
    g.normed[...] = normed
    plane_one(g.wb, g.packb, *g.s_wb1, True)
    ada_copy = remote(g.ada, g.ada_b, *g.s_ada, partner)
    ada_copy.start()

    def mod_wait(k, carry):
        other = mod(ctx + k, 16)
        remote(g.pair.at[0], g.modg.at[other], g.s_mod2[0].at[k], g.s_mod2[1].at[other],
               ctx_peer(k)).wait()
        return carry
    loop(1, 16, mod_wait)
    for p in range(16):
        c, first = div(p, 8), mod(2 * p, 16)
        both = jnp.concatenate(
            [g.modg[first, c:c + 1, :192], g.modg[first + 1, c:c + 1, :192]], axis=1)
        g.flat[:, 384 * p:384 * p + 384] = both + g.ada_bias[:, 384 * p:384 * p + 384].astype(F32)
    shift1, scale1, gate1, shift2, scale2, gate2 = [
        g.flat[:, k * 1024:(k + 1) * 1024] for k in range(6)]
    hidden = (g.normed[...] * (1.0 + scale1) + shift1).astype(BF16)
    g.hidden[...] = hidden
    plane_two(g.wa, *g.s_wa2, False)
    mixed = dot(hidden, g.wa[:, :, :, :, :384].reshape(1024, 384), NN)
    qv = g.qv[0, :, pl.ds(pl.multiple_of(dp * 128, 128), 128)].astype(F32)
    g.k_own[...] = mixed[:, 128:256].astype(BF16)
    gather_start(g.k_own, g.kg, z, 4, z_peer, *g.s_k)
    g.v_own[...] = (mixed[:, 256:] + qv[1:2]).astype(BF16)
    gather_start(g.v_own, g.vg, z, 4, z_peer, *g.s_v)
    query = (mixed[:, :128] + qv[0:1]).astype(BF16)
    g.kg[z] = g.k_own[...]
    g.vg[z] = g.v_own[...]
    tokens(g.cot, g.cg, *g.s_cg, True)
    gather_wait(g.k_own, g.kg, z, 4, z_peer, *g.s_k)
    plane_one(g.wb, g.packb, *g.s_wb1, False)
    plane_two(g.wb, *g.s_wb2, True)
    for h in range(2):
        key = g.kg[:, :, 64 * h:64 * h + 64].reshape(1024, 64)
        scores = dot(query[:, 64 * h:64 * h + 64], key, NT) * SCALE
        expo = jnp.exp(scores - jnp.max(scores, axis=-1, keepdims=True))
        g.prob[h] = expo / jnp.sum(expo, axis=-1, keepdims=True)
    gather_wait(g.v_own, g.vg, z, 4, z_peer, *g.s_v)
    heads = []
    for h in range(2):
        value = g.vg[:, :, 64 * h:64 * h + 64].reshape(1024, 64)
        heads.append(dot(g.prob[h].astype(BF16), value, NN))
    attended = jnp.concatenate(heads, axis=1).astype(BF16)
    w_out = g.wa[:, :, :, :, 384:].reshape(1024, 128)
    g.branch_part[...] = dot(attended, w_out, NT).astype(BF16).reshape(4, 2, 32, 1024)
    branch_ring = (g.branch_part, g.branch_half, g.branch_mid, g.branch_slots, *g.s_branch)
    ring_scatter(*branch_ring, 0)
    ring_scatter(*branch_ring, 1)
    tokens(g.cot, g.cg, *g.s_cg, False)
    relay(g.cg, *g.s_cr, True)
    relay(g.cg, *g.s_cr, False)
    d_feed = (g.cg[...].astype(F32).reshape(256, 1024) * gate2).astype(BF16)
    g.d_feed[...] = d_feed
    g.z_own[...] = jnp.zeros_like(g.z_own)
    g.z_own[5:6] = jnp.sum(d_feed.astype(F32), axis=0, keepdims=True)
    ring_scatter(*branch_ring, 2)

    x_own = g.xg[x, core].astype(F32)
    branch = jnp.sum(g.branch_slots[...].astype(F32), axis=0) + g.ob[...].astype(F32)
    middle = x_own + gate1 * branch
    normed_two, inverse_two = normalize(middle)
    g.h2_own[...] = (normed_two * (1.0 + scale2) + shift2).astype(BF16)
    ring_gather(g.h2_own, g.h2, *g.s_h2, True)
    plane_two(g.wb, *g.s_wb2, False)
    w_second = g.wb[:, :, :, :, 512:].reshape(1024, 512)
    g.d_act[...] = dot(d_feed, w_second, NN)
    ring_gather(g.h2_own, g.h2, *g.s_h2, False)

    hidden_two = g.h2[...].reshape(256, 1024)
    w_first = g.wb[:, :, :, :, :512].reshape(1024, 512)
    bias_first = g.b1[:, pl.ds(pl.multiple_of(dp * 512, 512), 512)].astype(F32)
    before = dot(hidden_two, w_first, NN) + bias_first
    square = before * before
    tanh = jnp.tanh(ROOT * before * (1.0 + 0.044715 * square))
    slope = 0.5 * (1.0 + tanh) + (0.5 * ROOT) * before * (1.0 - tanh * tanh) * (
        1.0 + (3.0 * 0.044715) * square)
    d_before = (g.d_act[...] * slope).astype(BF16)
    g.dh2_part[...] = dot(d_before, w_first, NT).astype(BF16).reshape(4, 2, 32, 1024)
    dh2_ring = (g.dh2_part, g.dh2_half, g.dh2_mid, g.dh2_slots, *g.s_dh2)
    ring_scatter(*dh2_ring, 0)
    activated = (0.5 * before * (1.0 + tanh)).astype(BF16)
    ring_scatter(*dh2_ring, 1)
    feed_part = dot(activated, w_second, NT)
    g.feed_part[...] = feed_part.astype(BF16).reshape(4, 2, 32, 1024)
    g.gb[:, :, :, :, :512] = dot(hidden_two, d_before, TN).astype(BF16).reshape(2, 4, 4, 32, 512)
    g.gb[:, :, :, :, 512:] = dot(d_feed, activated, TN).astype(BF16).reshape(2, 4, 4, 32, 512)
    reduce_one(g.gb, g.gb1, *g.s_gb1, True)
    g.m_own[3:4] = jnp.sum(
        g.cg[...].astype(F32).reshape(256, 1024) * feed_part, axis=0, keepdims=True)
    g.z_own[6:7, :512] = jnp.sum(d_before.astype(F32), axis=0, keepdims=True)
    ring_scatter(*dh2_ring, 2)

    cot_own = g.cg[x, core].astype(F32)
    d_hidden = jnp.sum(g.dh2_slots[...].astype(F32), axis=0)
    d_middle = cot_own + norm_back(d_hidden * (1.0 + scale2), normed_two, inverse_two)
    g.d_middle[...] = d_middle
    g.db_own[...] = (d_middle * gate1).astype(BF16)
    ring_gather(g.db_own, g.db, *g.s_db, True)
    feed_ring = (g.feed_part, g.feed_half, g.feed_mid, g.feed_slots, *g.s_feed)
    ring_scatter(*feed_ring, 0)
    g.m_own[0:1] = jnp.sum(d_middle * branch, axis=0, keepdims=True)
    g.m_own[1:2] = jnp.sum(d_hidden, axis=0, keepdims=True)
    g.m_own[2:3] = jnp.sum(d_hidden * normed_two, axis=0, keepdims=True)
    g.m_own[3:4] += jnp.sum(cot_own, axis=0, keepdims=True) * g.b2[...].astype(F32)
    gather_start(g.m_own, g.m_slots, r, 8, ring_peer, *g.s_m)
    g.m_slots[r] = g.m_own[...]
    ring_gather(g.db_own, g.db, *g.s_db, False)
    ring_scatter(*feed_ring, 1)

    d_branch = g.db[...].reshape(256, 1024)
    g.gc[...] = dot(d_branch, attended, TN).astype(BF16).reshape(2, 4, 4, 32, 128)
    reduce_one(g.gc, g.gc1, *g.s_gc1, True)
    d_attended = dot(d_branch, w_out, NN).astype(BF16)
    d_one = [d_attended[:, 64 * h:64 * h + 64] for h in range(2)]
    d_value = [dot(g.prob[h].astype(BF16), d_one[h], TN) for h in range(2)]
    g.dv_part[...] = jnp.concatenate(d_value, axis=1).astype(BF16).reshape(4, 256, 128)
    scatter_start(g.dv_part, g.dv_slots, z, 4, z_peer, *g.s_dv)
    g.dv_slots[z] = g.dv_part[z]
    d_query, d_key = [], []
    for h in range(2):
        key = g.kg[:, :, 64 * h:64 * h + 64].reshape(1024, 64)
        value = g.vg[:, :, 64 * h:64 * h + 64].reshape(1024, 64)
        prob = g.prob[h]
        d_prob = dot(d_one[h], value, NT)
        d_scores = (prob * (d_prob - jnp.sum(prob * d_prob, axis=-1, keepdims=True))).astype(BF16)
        d_key.append(dot(d_scores, query[:, 64 * h:64 * h + 64], TN) * SCALE)
        d_query.append(dot(d_scores, key, NN) * SCALE)
    g.dk_part[...] = jnp.concatenate(d_key, axis=1).astype(BF16).reshape(4, 256, 128)
    scatter_start(g.dk_part, g.dk_slots, z, 4, z_peer, *g.s_dk)
    g.dk_slots[z] = g.dk_part[z]
    d_query = jnp.concatenate(d_query, axis=1).astype(BF16)
    g.z_own[4:5] = jnp.sum(d_branch.astype(F32), axis=0, keepdims=True)
    g.z_own[6:7, 512:640] = jnp.sum(d_query.astype(F32), axis=0, keepdims=True)
    gather_wait(g.m_own, g.m_slots, r, 8, ring_peer, *g.s_m)
    g.z_own[0:4] = jnp.sum(g.m_slots[...], axis=0)
    gather_start(g.z_own, g.z_slots, z, 4, z_peer, *g.s_z)
    g.z_slots[z] = g.z_own[...]
    ring_scatter(*feed_ring, 2)
    feed = jnp.sum(g.feed_slots[...].astype(F32), axis=0) + g.b2[...].astype(F32)
    g.block_own[...] = (middle + gate2 * feed).astype(BF16)
    spread(g.block_own, g.block_out, *g.s_block, True)
    scatter_wait(g.dv_part, g.dv_slots, z, 4, z_peer, *g.s_dv)
    scatter_wait(g.dk_part, g.dk_slots, z, 4, z_peer, *g.s_dk)

    d_keys = jnp.sum(g.dk_slots[...].astype(F32), axis=0).astype(BF16)
    d_values = jnp.sum(g.dv_slots[...].astype(F32), axis=0).astype(BF16)
    d_qkv = jnp.concatenate([d_query, d_keys, d_values], axis=1)
    d_part = dot(d_qkv, g.wa[:, :, :, :, :384].reshape(1024, 384), NT)
    g.dh_part[...] = d_part.astype(BF16).reshape(4, 2, 32, 1024)
    dh_ring = (g.dh_part, g.dh_half, g.dh_mid, g.dh_slots, *g.s_dh)
    ring_scatter(*dh_ring, 0)
    g.ga[...] = dot(g.hidden[...], d_qkv, TN).astype(BF16).reshape(2, 4, 4, 32, 384)
    reduce_one(g.ga, g.ga1, *g.s_ga1, True)
    g.n_own[0:1] = jnp.sum(d_part, axis=0, keepdims=True)
    g.n_own[1:2] = jnp.sum(d_part * g.normed[...], axis=0, keepdims=True)
    gather_start(g.n_own, g.n_slots, r, 8, ring_peer, *g.s_n)
    g.n_slots[r] = g.n_own[...]
    ring_scatter(*dh_ring, 1)
    gather_wait(g.z_own, g.z_slots, z, 4, z_peer, *g.s_z)
    g.y_own[...] = jnp.sum(g.z_slots[...], axis=0)
    gather_start(g.y_own, g.y_slots, y, 4, y_peer, *g.s_y)
    g.y_slots[y] = g.y_own[...]
    reduce_one(g.gb, g.gb1, *g.s_gb1, False)
    add_slots(g.gb1, g.gb2)
    reduce_two(g.gb2, g.gb3, *g.s_gb2, True)
    reduce_one(g.gc, g.gc1, *g.s_gc1, False)
    add_slots(g.gc1, g.gc2)
    reduce_two(g.gc2, g.gc3, *g.s_gc2, True)
    gather_wait(g.n_own, g.n_slots, r, 8, ring_peer, *g.s_n)
    g.l_own[0:2] = jnp.sum(g.n_slots[...], axis=0)
    g.l_own[2:4] = jnp.zeros((2, 1024), F32)
    g.l_own[2:3, :128] = jnp.sum(d_values.astype(F32), axis=0, keepdims=True)
    gather_start(g.l_own, g.l_slots, ctx, 16, ctx_peer, *g.s_l)
    g.l_slots[ctx] = g.l_own[...]
    ring_scatter(*dh_ring, 2)

    x_normed, x_inverse = normalize(x_own)
    d_hidden = jnp.sum(g.dh_slots[...].astype(F32), axis=0)
    grad = g.d_middle[...] + norm_back(d_hidden * (1.0 + scale1), x_normed, x_inverse)
    g.grad_own[...] = grad.astype(BF16)
    spread(g.grad_own, g.grad_out, *g.s_grad, True)
    reduce_one(g.ga, g.ga1, *g.s_ga1, False)
    add_slots(g.ga1, g.ga2)
    reduce_two(g.ga2, g.ga3, *g.s_ga2, True)
    g.dm[...] = jnp.zeros_like(g.dm)
    gather_wait(g.y_own, g.y_slots, y, 4, y_peer, *g.s_y)
    for k in range(2, 6):
        for i in range(4):
            g.dm[i:i + 1, k * 1024:(k + 1) * 1024] = g.y_slots[i, k - 2:k - 1]
    gather_wait(g.l_own, g.l_slots, ctx, 16, ctx_peer, *g.s_l)

    late = jnp.sum(g.l_slots[...].reshape(4, 4, 4, 1024), axis=0)
    for k in range(2):
        for i in range(4):
            g.dm[i:i + 1, k * 1024:(k + 1) * 1024] = late[i, k:k + 1]

    def columns(chunk):
        wide = g.dm[:, pl.ds(pl.multiple_of(div(3 * chunk, 2) * 128, 128), 256)]
        return jnp.where(mod(chunk, 2) == 1, pltpu.roll(wide, 192, 1), wide)[:, :192]

    own_columns = columns(dp * 16 + ctx)
    ada_copy.wait()
    highest = lax.Precision.HIGHEST
    g.cond_part[...] = (
        dot_split(own_columns, g.ada[...]) + dot_split(columns((1 - dp) * 16 + ctx), g.ada_b[...]))[:4]
    gather_start(g.cond_part, g.cond_slots, ctx, 16, ctx_peer, *g.s_c)
    g.cond_slots[ctx] = g.cond_part[...]
    early = jnp.sum(g.y_slots[...], axis=0)
    g.wide_out[...] = early[4:6]
    g.bias_own[:, :640] = early[6:7, :640]
    g.bias_own[:, 640:768] = jnp.sum(late[:, 2], axis=0, keepdims=True)[:, :128]
    g.bias_own[:, 768:] = jnp.zeros((1, 256), F32)
    remote(g.bias_own, g.bias_out.at[dp], *g.s_bias, partner).start()
    g.bias_out[dp] = g.bias_own[...]
    g.ada_bias_out[...] = jnp.sum(g.dm[...], axis=0, keepdims=True)
    spread(g.block_own, g.block_out, *g.s_block, False)
    relay(g.block_out, *g.s_blockr, True)
    reduce_two(g.gb2, g.gb3, *g.s_gb2, False)
    add_slots(g.gb3, g.gb_out)
    reduce_two(g.gc2, g.gc3, *g.s_gc2, False)
    add_slots(g.gc3, g.gc_out)
    spread(g.grad_own, g.grad_out, *g.s_grad, False)
    relay(g.grad_out, *g.s_gradr, True)
    g.ada_out[...] = dot(own_columns, g.cond8[...], TN, highest)
    reduce_two(g.ga2, g.ga3, *g.s_ga2, False)
    add_slots(g.ga3, g.ga_out)
    gather_wait(g.cond_part, g.cond_slots, ctx, 16, ctx_peer, *g.s_c)
    g.cond_sum[...] = jnp.sum(g.cond_slots[...], axis=0)
    slope = sigmoid * (1.0 + cond_slice * (1.0 - sigmoid))
    for i in range(2):
        g.cond_out[i:i + 1] = g.cond_sum[pl.ds(2 * i + dp, 1)] * slope[i:i + 1]
    remote(g.bias_own, g.bias_out.at[1 - dp], *g.s_bias, partner).wait()
    relay(g.block_out, *g.s_blockr, False)
    relay(g.grad_out, *g.s_gradr, False)


def unpack_kernel(block, grad, cond, ada, ada_bias, ga, gb, gc, bias, wide,
                  block_out, grad_out, cond_out, ada_out, ada_bias_out, qkv_out, qv_out,
                  wo_out, ob_out, w1_out, b1_out, w2_out, b2_out):
    block_out[...] = block[...].reshape(2, 64, 1024)
    grad_out[...] = grad[...].astype(F32).reshape(2, 64, 1024)
    cond_out[...] = cond[...]
    ada_out[...] = ada[...]
    ada_bias_out[...] = ada_bias[...]
    for h in range(2):
        for k in range(3):
            qkv_out[k, :, 128 * h:128 * h + 128] = ga[h, :, 128 * k:128 * k + 128]
        for k in range(2):
            qv_out[0, k:k + 1, 128 * h:128 * h + 128] = bias[h, :, 512 + 128 * k:640 + 128 * k]
        wo_out[:, 128 * h:128 * h + 128] = gc[h]
        w1_out[0, :, 512 * h:512 * h + 512] = gb[h, :, :512]
        w2_out[:, 512 * h:512 * h + 512] = gb[h, :, 512:]
        b1_out[:, 512 * h:512 * h + 512] = bias[h, :, :512]
    ob_out[...] = wide[0:1]
    b2_out[...] = wide[1:2]


def on_device(
    latents, cond, ada_weight, ada_bias, qkv_weight, qv_bias, out_weight, out_bias,
    first_weight, first_bias, second_weight, second_bias, cotangent,
):
    args = [
        latents, cond, ada_weight[0].T, ada_bias, qkv_weight[0].transpose(1, 0, 2), qv_bias,
        out_weight[0].T, out_bias, first_weight, first_bias, second_weight[0].T, second_bias,
        cotangent,
    ]
    outs = pl.pallas_call(
        block_kernel,
        out_shape=[shape(*one) for one in OUTPUTS.values()],
        in_specs=[VMEM] * len(args),
        out_specs=[VMEM] * len(OUTPUTS),
        scratch_shapes=[pltpu.VMEM(*one) for one in BUFFERS.values()]
        + [DMA(one) for one in SEMS.values() for _ in range(2)],
        compiler_params=pltpu.CompilerParams(
            collective_id=1, has_side_effects=True, vmem_limit_bytes=56 << 20
        ),
        name="block",
    )(*args)
    final = [
        shape((2, 64, 1024), BF16), shape((2, 64, 1024), F32), shape((2, 256), F32),
        shape((192, 256), F32), shape((1, 6144), F32), shape((3, 32, 256), F32),
        shape((1, 2, 256), F32), shape((32, 256), F32), shape((1, 1024), F32),
        shape((1, 32, 1024), F32), shape((1, 1024), F32), shape((32, 1024), F32),
        shape((1, 1024), F32),
    ]
    results = pl.pallas_call(
        unpack_kernel, out_shape=final, in_specs=[VMEM] * len(outs), out_specs=[VMEM] * len(final),
        name="unpack",
    )(*outs)
    results = list(results)
    for k in (3, 7, 11):
        results[k] = results[k].T[None]
    results[5] = results[5].transpose(1, 0, 2)[None]
    return tuple(results)


def solution(mesh):
    return jax.shard_map(
        on_device,
        mesh=mesh,
        in_specs=(
            P("dp", "context", None),
            P("dp", None),
            P(None, "tensor", ("dp", "context")),
            P(),
            P(None, ("dp", "context"), None, "tensor"),
            P(None, None, "tensor"),
            P(None, "tensor", ("dp", "context")),
            P(),
            P(None, ("dp", "context"), "tensor"),
            P(None, "tensor"),
            P(None, "tensor", ("dp", "context")),
            P(),
            P("dp", "context", None),
        ),
        out_specs=(
            P("dp", "context", None),
            P("dp", "context", None),
            P("dp", "tensor"),
            P(None, "tensor", ("dp", "context")),
            P(),
            P(None, ("dp", "context"), None, "tensor"),
            P(None, None, "tensor"),
            P(None, "tensor", ("dp", "context")),
            P(),
            P(None, ("dp", "context"), "tensor"),
            P(None, "tensor"),
            P(None, "tensor", ("dp", "context")),
            P(),
        ),
        check_vma=False,
    )
```
